32 devices in a mesh: ctx: 16 (over z, y, x), head: 2 (over core).
Axes of the slice: x: 2, y: 2, z: 4, core: 2. Of those that a mesh axis runs over, the one named last changes fastest.
Arguments:
- query_proj: bfloat16 [2048, 2048], P('ctx', 'head'), may hold values from -6 to 6
- key_proj: bfloat16 [2048, 2048], P('ctx', 'head'), may hold values from -6 to 6
- value_proj: bfloat16 [2048, 4096], P('ctx', 'head'), may hold values from -6 to 6
- gate_proj: bfloat16 [2048, 4096], P('ctx', 'head'), may hold values from -6 to 6
- write_strength: float32 [2048, 32], P('ctx', 'head'), may hold values from 0 to 1
- log_decay: float32 [2048, 32], P('ctx', 'head'), may hold values from -1 to 0
- norm_gain: float32 [128], replicated, may hold values from 0.1 to 1.9
- out_weight: bfloat16 [4096, 2048], P('head'), may hold values from -0.125 to 0.125
Outputs:
- layer_out: bfloat16 [2048, 2048], P('ctx', 'head')
The draws below stay inside these ranges and needn't reach their ends.
All inputs are finite; a program needn't handle non-finite values.
Results may differ from the reference program's by a relative error of at most 0.017.
Values may be sent and summed in bfloat16 or wider, within the bound.
No kernel may reach another device: no remote copies, remote signals or barrier semaphores. Data moves between devices by JAX's collectives and lax.ppermute only.
A program may use at most 128 MiB of HBM per device.

```python
import math
import jax
import jax.numpy as jnp
from jax import lax

DM = 2048
HV = 32
HK = 16
DK = 128
DV = 128
SPAN = 64
TOK_DEV = 128
SEQUENCE_TOKENS = 2048
N_HEAD = 2


def head_slowness(key, power):
    return jax.random.uniform(key, (HV,), jnp.float32) ** power


def draw_log_decay(key, part):
    power = 1.0
    slowness = head_slowness(key, power)
    key = jax.random.fold_in(key, 11)
    key_rough, key_block, key_place, key_drop = jax.random.split(key, 4)
    learning_rate = jnp.exp(math.log(1.0 / 40.0) * (1.0 - slowness) + jnp.log(0.05 / SEQUENCE_TOKENS) * slowness)
    coarse_estimate = jnp.exp(jax.random.uniform(key_rough, (SEQUENCE_TOKENS, HV), jnp.float32, math.log(0.5), math.log(2.0)))
    blocks = jnp.exp(jax.random.uniform(key_block, (SEQUENCE_TOKENS // TOK_DEV, HV), jnp.float32, math.log(0.5), math.log(2.0)))
    rows_per_block = jnp.repeat(blocks, TOK_DEV, axis=0)
    token_positions = jax.random.randint(key_place, (4,), 0, SEQUENCE_TOKENS)
    token_groups = jnp.any(jnp.arange(SEQUENCE_TOKENS)[:, None] == token_positions[None, :], axis=1)
    decay_factors = jax.random.uniform(key_drop, (SEQUENCE_TOKENS, HV), jnp.float32, math.log(0.5), math.log(0.8))
    return -learning_rate[None, :] * coarse_estimate * rows_per_block + jnp.where(token_groups[:, None], decay_factors, 0.0)


def draw_write_strength(key, part):
    power = 1.0
    slowness = head_slowness(key, power)
    key = jax.random.fold_in(key, 23)
    base = jnp.exp(math.log(0.45) * (1.0 - slowness) + jnp.log(0.5 * DK / SEQUENCE_TOKENS) * slowness)
    coarse_estimate = jnp.exp(jax.random.uniform(key, (SEQUENCE_TOKENS, HV), jnp.float32, math.log(0.5), math.log(2.0)))
    return base[None, :] * coarse_estimate


def with_spikes(entries, stream_key, source, target, parts, factor):
    def block_of(dim):
        return (jnp.arange(entries.shape[dim]) // (entries.shape[dim] // parts)).reshape((-1,) + (1,) * (entries.ndim - 1 - dim))

    near = jax.random.permutation(stream_key, parts)[block_of(target)]
    other_side = (block_of(target) + parts // 2) % parts
    return jnp.where((block_of(source) == near) | (block_of(source) == other_side), factor * entries, entries)


def level_of(own_key, shape, cuts, least, high):
    def one(dim, blocks):
        steps = jax.random.uniform(jax.random.fold_in(jax.random.fold_in(own_key, 6), dim), (blocks,), jnp.float32, least / len(cuts), high / len(cuts))
        return jnp.repeat(jnp.exp(steps), shape[dim] // blocks).reshape((-1,) + (1,) * (len(shape) - dim - 1))

    gain = one(*cuts[0])
    for cut in cuts[1:]:
        gain = gain * one(*cut)
    return gain


def noise(own_key, shape, deviation, limit, cuts=(), kind=jnp.bfloat16):
    factor_of = level_of(own_key, shape, cuts, -0.22, 0.18) if cuts else 1.0
    values = jax.random.normal(own_key, shape, jnp.float32) * deviation * factor_of
    return jnp.minimum(jnp.maximum(values, -limit), limit).astype(kind)


def heavy_noise(own_key, dims, scale, limit, pieces, heavy, held_as=jnp.bfloat16):
    values = scale * jax.random.normal(own_key, dims, jnp.float32)
    if pieces:
        values = values * level_of(own_key, dims, pieces, -0.22, 0.18)
    return jnp.clip(with_spikes(values, jax.random.fold_in(own_key, 3), *heavy), -limit, limit).astype(held_as)


def setup_inputs(seed: int = 0) -> dict:
    arg_keys = jax.random.split(jax.random.key(seed), 9)
    return {
        "query_proj": noise(arg_keys[0], (SEQUENCE_TOKENS, HK * DK), 1.0, 6.0, ((0, 16), (1, 2))),
        "key_proj": noise(arg_keys[1], (SEQUENCE_TOKENS, HK * DK), 1.0, 6.0, ((0, 16), (1, 2))),
        "value_proj": noise(arg_keys[2], (SEQUENCE_TOKENS, HV * DV), 1.0, 6.0, ((0, 16), (1, 2))),
        "gate_proj": noise(arg_keys[3], (SEQUENCE_TOKENS, HV * DV), 1.0, 6.0, ((0, 16), (1, 2))),
        "write_strength": draw_write_strength(jax.random.fold_in(arg_keys[8], 71), 0),
        "log_decay": draw_log_decay(jax.random.fold_in(arg_keys[8], 71), 0),
        "norm_gain": jnp.clip(1.0 + 0.18 * jax.random.normal(arg_keys[6], (DV,), jnp.float32), 0.1, 1.9),
        "out_weight": heavy_noise(arg_keys[7], (HV * DV, DM), (HV * DV) ** -0.5, 0.125, ((0, 2),), (0, 1, 2, 2.0)),
    }


exact_matmul_mode = lax.Precision.HIGHEST
EPSILON = 1e-06

def unit_rows(vectors):
    return vectors * lax.rsqrt(lax.optimization_barrier(jnp.sum(vectors * vectors, axis=-1, keepdims=True)) + EPSILON)

def span_terms(queries, keys, values, strength, decays):
    span_len = decays.shape[-1]
    value_width = values.shape[-1]
    key_width = keys.shape[-1]
    cumulative = jnp.cumsum(decays, axis=-1)
    row_index = jnp.arange(span_len)[:, None]
    col_index = jnp.arange(span_len)[None, :]
    strict = col_index < row_index
    inclusive = col_index <= row_index
    log_gaps = cumulative[..., :, None] - cumulative[..., None, :]
    factors = jnp.where(inclusive, jnp.exp(jnp.where(inclusive, log_gaps, 0.0)), 0.0)
    key_products = jnp.einsum('htk,hsk->hts', keys, keys, precision=exact_matmul_mode)
    lower_part = jnp.where(strict, strength[..., :, None] * factors * key_products, 0.0)
    system = jnp.eye(span_len, dtype=jnp.float32) + lower_part
    growth = jnp.exp(cumulative)
    right_side = jnp.concatenate([strength[..., None] * values, (strength * growth)[..., None] * keys], axis=-1)
    solved = jax.scipy.linalg.solve_triangular(system, right_side, lower=True, unit_diagonal=True)
    value_slice = solved[..., :value_width]
    key_part = solved[..., value_width:]
    tail_decay = jnp.exp(cumulative[..., -1:] - cumulative)
    trailing_keys = keys * tail_decay[..., None]
    identity_k = jnp.eye(key_width, dtype=jnp.float32)
    state_transfer = growth[..., -1, None, None] * identity_k - jnp.einsum('hsk,hsj->hkj', trailing_keys, key_part, precision=exact_matmul_mode)
    start_position = jnp.einsum('nil,nim->nlm', trailing_keys, value_slice, precision=exact_matmul_mode)
    scores = jnp.einsum('htk,hsk->hts', queries, keys, precision=exact_matmul_mode) * factors
    within_block_output = jnp.einsum('hts,hsv->htv', scores, value_slice, precision=exact_matmul_mode)
    window_rows = growth[..., None] * queries - jnp.einsum('hts,hsk->htk', scores, key_part, precision=exact_matmul_mode)
    return (state_transfer, start_position, within_block_output, window_rows)

def gate_norm(output_rows, gate_rows, norm_gain):
    mean_square = lax.optimization_barrier(jnp.mean(output_rows * output_rows, axis=-1, keepdims=True))
    return output_rows * lax.rsqrt(mean_square + EPSILON) * norm_gain * jax.nn.silu(gate_rows)

def reference(query_proj, key_proj, value_proj, gate_proj, write_strength, log_decay, norm_gain, out_weight):
    total = query_proj.shape[0]
    count_spans = total // SPAN
    repeat_by = HV // HK

    def block_step(running_state, block):
        query_block, key_block, value_block, gate_block, strength_block, decay_block = block
        queries = unit_rows(query_block.astype(jnp.float32).reshape(SPAN, HK, DK)) * DK ** (-0.5)
        keys = unit_rows(key_block.astype(jnp.float32).reshape(SPAN, HK, DK))
        queries = jnp.repeat(queries, repeat_by, axis=1).transpose(1, 0, 2)
        keys = jnp.repeat(keys, repeat_by, axis=1).transpose(1, 0, 2)
        values = value_block.astype(jnp.float32).reshape(SPAN, HV, DV).transpose(1, 0, 2)
        state_transfer, start_position, within_block_output, window_rows = span_terms(queries, keys, values, strength_block.T, decay_block.T)
        output_rows = within_block_output + jnp.einsum('lye,lei->lyi', window_rows, running_state, precision=exact_matmul_mode)
        updated_state = jnp.einsum('epn,eni->epi', state_transfer, running_state, precision=exact_matmul_mode) + start_position
        normed = gate_norm(output_rows.transpose(1, 0, 2), gate_block.astype(jnp.float32).reshape(SPAN, HV, DV), norm_gain)
        return (updated_state, normed.reshape(SPAN, HV * DV).astype(jnp.bfloat16))
    blocks = (query_proj.reshape(count_spans, SPAN, HK * DK), key_proj.reshape(count_spans, SPAN, HK * DK), value_proj.reshape(count_spans, SPAN, HV * DV), gate_proj.reshape(count_spans, SPAN, HV * DV), write_strength.reshape(count_spans, SPAN, HV), log_decay.reshape(count_spans, SPAN, HV))
    final_state, mixed = lax.scan(block_step, jnp.zeros((HV, DK, DV), jnp.float32), blocks)
    mixed = mixed.reshape(total, HV * DV)
    group_width = HV * DV // N_HEAD
    result = jnp.zeros((total, DM), jnp.float32)
    for group_index in range(N_HEAD):
        lo_edge = group_index * group_width
        partial_sum = jnp.dot(mixed[:, lo_edge:lo_edge + group_width].astype(jnp.float32), out_weight[lo_edge:lo_edge + group_width].astype(jnp.float32), preferred_element_type=jnp.float32)
        rounded = lax.optimization_barrier(partial_sum.astype(jnp.bfloat16))
        result = result + rounded.astype(jnp.float32)
    return result.astype(jnp.bfloat16)
```

```python
import functools

import jax
import jax.numpy as jnp
from jax import lax
from jax.experimental import pallas as pl
from jax.experimental.pallas import tpu as pltpu
from jax.sharding import PartitionSpec as P

HV = 32
HK = 16
DK = 128
DV = 128
REP = HV // HK
SMALL_BITS = 4
SMALL_ROWS = 1 << SMALL_BITS
CHUNKS = 8
BASE_BITS = 3
BASE = 1 << BASE_BITS
PIECE_ROWS = 8
EPSILON = 1e-06
BF16 = jnp.bfloat16
F32 = jnp.float32


def nn(a, b):
    return lax.dot_general(a, b, (((1,), (0,)), ((), ())), preferred_element_type=F32)


def nt(a, b):
    return lax.dot_general(a, b, (((1,), (1,)), ((), ())), preferred_element_type=F32)


def two_pieces(x):
    high = x.astype(BF16)
    return high, (x - high.astype(F32)).astype(BF16)


def iotas(shape):
    return lax.broadcasted_iota(jnp.int32, shape, 0), lax.broadcasted_iota(jnp.int32, shape, 1)


def triangles(size):
    row, col = iotas((size, size))
    return row, col, (col <= row).astype(BF16), (row <= col).astype(BF16), (row == col).astype(BF16)


def solved(lowers, rights, size):
    count = len(lowers)
    row, col = iotas((size, size))
    place, lane = iotas((BASE, size))
    packed = []
    for low in lowers:
        held = low[0:BASE]
        for b in range(1, size // BASE):
            held = jnp.where(lane >> BASE_BITS == b, low[b * BASE : (b + 1) * BASE], held)
        packed.append(held)
    packed = jnp.concatenate(packed, axis=0).astype(BF16)
    found = [jnp.where(place == (lane & (BASE - 1)), 1.0, 0.0)] * count
    first_col = col & ~(BASE - 1)
    for k in range(BASE - 1):
        spread = jnp.where(row == first_col + k, 1.0, 0.0).astype(BF16)
        column = nn(packed, spread)
        found = [
            x - column[h * BASE : (h + 1) * BASE] * x[k : k + 1] for h, x in enumerate(found)
        ]
    rounded = [low.astype(BF16) for low in lowers]
    step, apart = BASE, row ^ col
    while True:
        pair = 2 * step
        below = jnp.where((apart >= step) & (apart < pair) & (col < row), 1.0, 0.0).astype(BF16)
        diagonal = jnp.where(apart < step, 1.0, 0.0)
        lane = lax.broadcasted_iota(jnp.int32, (step, size), 1)
        even = (lane & step) == 0
        first = [nn(x.astype(BF16), low * below).astype(BF16) for x, low in zip(found, rounded)]
        whole = [
            (jnp.concatenate([x] * (size // step), axis=0) * diagonal).astype(BF16) for x in found
        ]
        if pair == size:
            ends = [nn(w, right) for w, right in zip(whole, rights)]
            fixes = [nn(f, end.astype(BF16)) for f, end in zip(first, ends)]
            return [
                jnp.concatenate([end[:step], end[step:] - fix], axis=0)
                for end, fix in zip(ends, fixes)
            ]
        second = [nn(f, w) for f, w in zip(first, whole)]
        found = [
            jnp.concatenate([jnp.where(even, x, 0.0), jnp.where(even, -y, x)], axis=0)
            for x, y in zip(found, second)
        ]
        step = pair


def decay_gaps(cum_col, cum_row, row, col):
    return jnp.exp(jnp.where(col <= row, cum_col - cum_row, -1e30))


def inverse_norms(gram, row, col):
    diagonal = jnp.where(row == col, gram, 0.0)
    return (
        lax.rsqrt(jnp.sum(diagonal, axis=1, keepdims=True) + EPSILON),
        lax.rsqrt(jnp.sum(diagonal, axis=0, keepdims=True) + EPSILON),
    )


def place_in_group(group):
    return lax.rem(lax.axis_index("ctx"), group)


def pack_kernel(key_hbm, value_hbm, strength_hbm, decay_hbm, *refs):
    group = len(refs) - 6
    out_refs, (rows_ref, held, scalars, small, in_sems, out_sems) = refs[:group], refs[group:]
    tokens = key_hbm.shape[0]
    heads = strength_hbm.shape[0]
    place = place_in_group(group)
    base = (1 + REP) * tokens
    scalar_copies = [
        pltpu.make_async_copy(ref, scalars.at[kind], in_sems.at[group, kind])
        for kind, ref in enumerate((strength_hbm, decay_hbm))
    ]
    arrivals = []
    for s in range(group):
        j = place ^ s
        sources = [key_hbm.at[:, pl.ds(pl.multiple_of(j * DK, DK), DK)]] + [
            value_hbm.at[:, pl.ds(pl.multiple_of((j * REP + r) * DV, DV), DV)] for r in range(REP)
        ]
        arrivals.append(
            [
                pltpu.make_async_copy(
                    source, held.at[s, pl.ds(n * tokens, tokens), :], in_sems.at[s, n]
                )
                for n, source in enumerate(sources)
            ]
        )
    for copy in scalar_copies + sum(arrivals, []):
        copy.start()
    row, col = iotas((SMALL_ROWS * group, 4 * heads))
    slot, target = row & (SMALL_ROWS - 1), row >> SMALL_BITS

    def picked(target):
        pick = jnp.zeros(row.shape, F32)
        for kind in range(2):
            for piece in range(2):
                at = slot - piece * PIECE_ROWS - kind * REP
                wanted = (2 * kind + piece) * heads + target * REP + at
                pick = pick + jnp.where((at >= 0) & (at < REP) & (col == wanted), 1.0, 0.0)
        return pick.astype(BF16)

    picks = picked(target ^ place), picked(target)
    for copy in scalar_copies:
        copy.wait()
    pieces = jnp.concatenate(two_pieces(scalars[0]) + two_pieces(scalars[1]), axis=0)
    sent, natural = [nn(pick, pieces).astype(BF16) for pick in picks]
    if tokens < DK:
        fill = jnp.zeros((sent.shape[0], DK - tokens), BF16)
        sent, natural = [jnp.concatenate([x, fill], axis=1) for x in (sent, natural)]
    small[...] = natural
    departures = [pltpu.make_async_copy(small, rows_ref, out_sems.at[group])]
    departures[0].start()
    for s, out_ref in enumerate(out_refs):
        held[s, base : base + SMALL_ROWS, :] = sent[s * SMALL_ROWS : (s + 1) * SMALL_ROWS, :]
        for copy in arrivals[s]:
            copy.wait()
        departures.append(pltpu.make_async_copy(held.at[s], out_ref, out_sems.at[s]))
        departures[-1].start()
    for copy in departures:
        copy.wait()


def solved_blocks(blocks, small, tokens):
    row, col, lower_ones, upper_ones, eye = triangles(tokens)
    small = small.astype(F32)
    pieces = [
        jnp.concatenate(
            [
                small[b * SMALL_ROWS + start : b * SMALL_ROWS + start + PIECE_ROWS]
                for b in range(len(blocks))
            ],
            axis=0,
        ).astype(BF16)
        for start in (0, PIECE_ROWS)
    ]
    cum_rows = sum(nn(p, upper_ones) for p in pieces)
    plain_cols = sum(nt(eye, p) for p in pieces)
    cum_cols = sum(nt(lower_ones, p) for p in pieces)

    def spread(array, at):
        return jnp.broadcast_to(array[:, at : at + 1], (tokens, DK))

    lowers, rights, works = [], [], []
    for b, (keys, values) in enumerate(blocks):
        gram = nt(keys, keys)
        key_col, key_row = inverse_norms(gram, row, col)
        key_col = jnp.broadcast_to(key_col, (tokens, DK))
        gram = gram * key_row * key_col[:, :tokens]
        unit_keys = keys.astype(F32) * key_col
        for r in range(REP):
            at = b * PIECE_ROWS + r
            strength = spread(plain_cols, at)
            cum_row, cum_col = cum_rows[at + REP : at + REP + 1, :], spread(cum_cols, at + REP)
            factors = decay_gaps(cum_col[:, :tokens], cum_row, row, col)
            lowers.append(jnp.where(col < row, strength[:, :tokens] * factors * gram, 0.0))
            rights.append(
                jnp.concatenate(
                    [
                        (strength * values[r].astype(F32)).astype(BF16),
                        (strength * jnp.exp(cum_col) * unit_keys).astype(BF16),
                    ],
                    axis=1,
                )
            )
            works.append((keys, cum_col, key_col, key_row, factors))
    return solved(lowers, rights, tokens), works


def inside_kernel(query_ref, key_ref, value_ref, rows_ref, *refs, first, shifts=0):
    copies = []
    if shifts:
        weight_hbm, inside_ref, window_ref, early_ref, sems = refs
        target = lax.rem(lax.axis_index("head") + 1, shifts)
        copies = weight_copies(weight_hbm, target, 0, early_ref, sems)
    else:
        inside_ref, window_ref = refs
    tokens = query_ref.shape[0]
    blocks = inside_ref.shape[0] // REP

    def columns(ref, start, size):
        return ref[:, start * size : (start + 1) * size]

    sides, works = solved_blocks(
        [
            (
                columns(key_ref, j, DK),
                [columns(value_ref, j * REP + r, DV) for r in range(REP)],
            )
            for j in range(first, first + blocks)
        ],
        rows_ref[first * SMALL_ROWS : (first + blocks) * SMALL_ROWS, :][:, :tokens],
        tokens,
    )
    for b in range(blocks):
        queries = columns(query_ref, first + b, DK)
        products = nt(queries, works[b * REP][0])
        queries = queries.astype(F32)
        query_col = lax.rsqrt(
            jnp.sum(queries * queries, axis=1, keepdims=True) + EPSILON
        ) * DK**-0.5
        query_col = jnp.broadcast_to(query_col, (tokens, DK))
        queries = queries * query_col
        products = products * works[b * REP][3] * query_col[:, :tokens]
        for r in range(REP):
            at = b * REP + r
            _, cum_col, _, _, factors = works[at]
            scores = (products * factors).astype(BF16)
            both = nn(scores, sides[at].astype(BF16))
            inside_ref[at] = both[:, :DV].astype(BF16)
            window_ref[at] = (jnp.exp(cum_col) * queries - both[:, DV:]).astype(BF16)
    for copy in copies:
        copy.wait()


def in_order(own_half, own, other):
    return jnp.where(own_half == 0, own, other), jnp.where(own_half == 0, other, own)


def half_kernel(*refs, blocks, group, tokens, own, with_map):
    taken, refs = refs[:blocks], refs[blocks:]
    if not own:
        (own_end, own_map), refs = refs[:2], refs[2:]
    before_ref, map_ref, end_ref, end_map_ref, *refs = refs
    if not own:
        group_ref, *refs = refs
        if with_map:
            group_map_ref, *refs = refs
    offsets, removals, decays = refs
    place = place_in_group(group)
    low = lax.rem(place, blocks)
    base = (1 + REP) * tokens
    sides, works = solved_blocks(
        [
            (t[0:tokens, :], [t[(1 + r) * tokens : (2 + r) * tokens, :] for r in range(REP)])
            for t in taken
        ],
        jnp.concatenate([t[base : base + SMALL_ROWS, :][:, :tokens] for t in taken], axis=0),
        tokens,
    )
    for b in range(blocks):
        keys_turned = works[b * REP][0].T
        for r in range(REP):
            at = b * REP + r
            _, cum_col, key_col, _, _ = works[at]
            last = cum_col[tokens - 1 : tokens, :]
            decays[at] = jnp.broadcast_to(jnp.exp(last), (PIECE_ROWS, DK))
            tail = key_col * jnp.exp(last - cum_col)
            tail = jnp.concatenate([tail, tail], axis=1)
            both = nn(keys_turned, (sides[at] * tail).astype(BF16))
            offsets[at] = both[:, :DV]
            removals[at] = both[:, DV:].astype(BF16)

    key_row, key_col = iotas((DK, DK))
    eye = (key_row == key_col).astype(F32)
    states = [None] * REP
    for i in range(blocks):
        following = []
        for r in range(REP):
            at = (low ^ i) * REP + r
            decay = decays[at][0:1, :]
            if i == 0:
                map_ref[at] = eye.astype(BF16)
                before_ref[at] = jnp.zeros((DK, DV), F32)
                following.append(
                    jnp.concatenate(
                        [eye * decay - removals[at].astype(F32), offsets[at]], axis=1
                    )
                )
                continue
            held = states[r].astype(BF16)
            map_ref[at] = held[:, :DK]
            before_ref[at] = states[r][:, DK:]
            moved = nn(removals[at], held)
            following.append(
                jnp.concatenate(
                    [
                        states[r][:, :DK] * decay - moved[:, :DK],
                        states[r][:, DK:] * decay - moved[:, DK:] + offsets[at],
                    ],
                    axis=1,
                )
            )
        states = following
    own_half = place // blocks
    for r in range(REP):
        end_map, end = states[r][:, :DK], states[r][:, DK:]
        end_map_ref[r] = end_map
        end_ref[r] = end
        if not own:
            first_end, second_end = in_order(own_half, own_end[r], end)
            first_map, second_map = in_order(own_half, own_map[r], end_map)
            second_map = second_map.astype(BF16)
            group_ref[r] = (nn(second_map, first_end.astype(BF16)) + second_end).astype(BF16)
            if with_map:
                group_map_ref[r] = nn(second_map, first_map.astype(BF16))


def carry_kernel(
    own_before, own_maps, own_end, own_map, other_before, other_maps, other_end, other_map,
    carried_ref, out_ref, held, sems,
):
    group = held.shape[0]
    half = group // 2
    place = place_in_group(group)
    own_half = place // half
    later_group = lax.axis_index("ctx") >= group
    starts = []
    for r in range(REP):
        carried = jnp.where(later_group, carried_ref[r].astype(F32), 0.0)
        first_end, _ = in_order(own_half, own_end[r], other_end[r])
        first_map, _ = in_order(own_half, own_map[r], other_map[r])
        middle = first_end + nn(first_map.astype(BF16), carried.astype(BF16))
        starts.append([x.astype(BF16) for x in in_order(own_half, carried, middle)])
    copies = []
    for s in range(group):
        before, maps = (own_before, own_maps) if s < half else (other_before, other_maps)
        for r in range(REP):
            at = (s % half) * REP + r
            start = starts[r][0] if s < half else starts[r][1]
            held[s, r * DK : (r + 1) * DK, :] = (before[at] + nn(maps[at], start)).astype(BF16)
        copies.append(pltpu.make_async_copy(held.at[s], out_ref.at[place ^ s], sems.at[s]))
        copies[-1].start()
    for copy in copies:
        copy.wait()


def weight_copies(weight_hbm, target, first, held, sems):
    count, depth, width = held.shape
    columns = pl.ds(pl.multiple_of(target * width, width), width)
    copies = [
        pltpu.make_async_copy(
            weight_hbm.at[pl.ds((first + c) * depth, depth), columns], held.at[c], sems.at[c]
        )
        for c in range(count)
    ]
    for copy in copies:
        copy.start()
    return copies


def project(chunk_of, targets):
    totals = [None] * len(targets)
    for c in range(len(targets[0])):
        rows = chunk_of(c)
        for n, chunks in enumerate(targets):
            chunk, copy = chunks[c]
            if copy is not None:
                copy.wait()
            part = nn(rows, chunk[...])
            totals[n] = part if totals[n] is None else totals[n] + part
    return [total.astype(BF16) for total in totals]


def mixed_kernel(
    state_ref, first_inside, first_window, second_inside, second_window, gate_ref, gain_ref,
    early_ref, weight_hbm, mixed_ref, own_early_ref, *refs, shifts,
):
    out_refs, (held, sems, own_sems) = refs[:-3], refs[-3:]
    me = lax.axis_index("head")
    early, depth, _ = early_ref.shape
    chunks = held.shape[0] // (shifts - 1)
    targets = []
    for n in range(shifts - 1):
        known = early if n == 0 else 0
        slots = pl.ds(n * chunks, chunks - known)
        copies = weight_copies(
            weight_hbm, lax.rem(me + 1 + n, shifts), known, held.at[slots], sems.at[slots]
        )
        targets.append(
            [(early_ref.at[c], None) for c in range(known)]
            + [(held.at[n * chunks + c], copy) for c, copy in enumerate(copies)]
        )
    own_copies = weight_copies(weight_hbm, me, 0, own_early_ref, own_sems)
    gain = gain_ref[...]
    split = first_inside.shape[0]

    def head(h):
        inside, window, at = (
            (first_inside, first_window, h) if h < split
            else (second_inside, second_window, h - split)
        )
        j, r = h // REP, h % REP
        columns = pl.ds(h * DV, DV)
        rows = inside[at].astype(F32) + nn(window[at], state_ref[j, r * DK : (r + 1) * DK, :])
        scale = lax.rsqrt(jnp.mean(rows * rows, axis=1, keepdims=True) + EPSILON)
        gate = gate_ref[:, columns].astype(F32)
        mixed = (rows * scale * gain * (gate / (1.0 + jnp.exp(-gate)))).astype(BF16)
        mixed_ref[:, columns] = mixed
        return mixed

    def chunk_of(c):
        return jnp.concatenate(
            [head(h) for h in range(c * depth // DV, (c + 1) * depth // DV)], axis=1
        )

    for out_ref, total in zip(out_refs, project(chunk_of, targets)):
        out_ref[...] = total
    for copy in own_copies:
        copy.wait()


def own_columns_kernel(mixed_ref, early_ref, weight_hbm, out_ref, held, sems):
    early, depth, _ = early_ref.shape
    copies = weight_copies(weight_hbm, lax.axis_index("head"), early, held, sems)
    chunks = [(early_ref.at[c], None) for c in range(early)]
    chunks += [(held.at[c], copy) for c, copy in enumerate(copies)]
    (out_ref[...],) = project(lambda c: mixed_ref[:, c * depth : (c + 1) * depth], [chunks])


def local(
    query_proj, key_proj, value_proj, gate_proj, write_strength, log_decay, norm_gain, out_weight,
    *, n_ctx, n_head,
):
    tokens = query_proj.shape[0]
    heads = value_proj.shape[1] // DV
    group = query_proj.shape[1] // DK
    half = group // 2
    width = out_weight.shape[1] // n_head
    n_groups = n_ctx // group
    groups = [list(range(g, g + group)) for g in range(0, n_ctx, group)]
    packed_rows = (1 + REP) * tokens + SMALL_ROWS
    mib = 1024 * 1024

    def kernel(body, out, name, limit, micros, scratch=(), specs=None, out_specs=None):
        return pl.pallas_call(
            body,
            out_shape=out,
            scratch_shapes=scratch,
            compiler_params=pltpu.CompilerParams(
                vmem_limit_bytes=None if limit is None else limit * mib
            ),
            cost_estimate=pl.CostEstimate(
                flops=int(micros * 1e9), bytes_accessed=mib, transcendentals=0
            ),
            name=name,
            **({} if specs is None else {"in_specs": specs}),
            **({} if out_specs is None else {"out_specs": out_specs}),
        )

    def shape(dims, kind):
        return jax.ShapeDtypeStruct(dims, kind)

    def shifted(array, distance):
        return lax.ppermute(array, "ctx", [(i, i + distance) for i in range(n_ctx - distance)])

    def swapped(array, distance):
        return lax.ppermute(array, "ctx", [(i, i ^ distance) for i in range(n_ctx)])

    any_space = pl.BlockSpec(memory_space=pl.ANY)
    vmem = pl.BlockSpec(memory_space=pltpu.VMEM)
    *packed, rows = kernel(
        pack_kernel,
        (shape((packed_rows, DK), BF16),) * group + (shape((group * SMALL_ROWS, DK), BF16),),
        "pack",
        None,
        2,
        scratch=[
            pltpu.VMEM((group, packed_rows, DK), BF16),
            pltpu.VMEM((2, heads, tokens), F32),
            pltpu.VMEM((group * SMALL_ROWS, DK), BF16),
            pltpu.SemaphoreType.DMA((group + 1, 1 + REP)),
            pltpu.SemaphoreType.DMA((group + 1,)),
        ],
        specs=[any_space] * 4,
        out_specs=(any_space,) * (group + 1),
    )(key_proj, value_proj, write_strength.T, log_decay.T)
    taken = [packed[0]] + [swapped(packed[s], s) for s in range(1, group)]

    def half_states(blocks, more, name):
        own, with_map = not more, n_groups > 2
        return kernel(
            functools.partial(half_kernel, blocks=half, group=group, tokens=tokens, own=own, with_map=with_map),
            (
                shape((half * REP, DK, DV), F32),
                shape((half * REP, DK, DK), BF16),
                shape((REP, DK, DV), F32),
                shape((REP, DK, DK), F32),
            )
            + (() if own else (shape((REP, DK, DV), BF16),))
            + ((shape((REP, DK, DK), F32),) if with_map and not own else ()),
            name,
            16,
            3.5,
            scratch=[
                pltpu.VMEM((half * REP, DK, DV), F32),
                pltpu.VMEM((half * REP, DK, DK), BF16),
                pltpu.VMEM((half * REP, PIECE_ROWS, DK), F32),
            ],
        )(*blocks, *more)

    own = half_states(taken[:half], (), "own_half")
    later, own = lax.optimization_barrier((taken[half:], own))
    *other, end = half_states(later, own[2:], "other_half")

    if n_groups == 2:
        carried = swapped(end, group)
    elif n_groups > 2:
        carried, mapping = shifted(other[-1], group).astype(F32), shifted(end, group)
        other = other[:-1]
        distance = 1
        while distance < n_groups - 1:
            earlier, earlier_map = shifted(carried, distance * group), shifted(mapping, distance * group)
            carried = carried + jnp.einsum("rkl,rlv->rkv", mapping, earlier, precision="highest")
            mapping = jnp.einsum("rkl,rlv->rkv", mapping, earlier_map, precision="highest")
            distance *= 2
        carried = carried.astype(BF16)
    else:
        carried = jnp.zeros((REP, DK, DV), BF16)

    chunks = min(CHUNKS, out_weight.shape[0] // DV)
    depth = out_weight.shape[0] // chunks

    def inside_part(start, count, rows, micros, limit, fetch):
        return kernel(
            functools.partial(inside_kernel, first=start, shifts=n_head if fetch else 0),
            (
                shape((count * REP, tokens, DV), BF16),
                shape((count * REP, tokens, DK), BF16),
            )
            + ((shape((fetch, depth, width), BF16),) if fetch else ()),
            "inside",
            limit,
            micros,
            scratch=[pltpu.SemaphoreType.DMA((fetch,))] if fetch else (),
            specs=[vmem] * 4 + ([any_space] if fetch else []),
        )(query_proj, key_proj, value_proj, rows, *((out_weight,) if fetch else ()))

    early = half
    rows, end = lax.optimization_barrier((rows, end))
    first = inside_part(0, early, rows, 2.4, 16, 0)
    carried, first = lax.optimization_barrier((carried, first))
    states = kernel(
        carry_kernel,
        shape((group, REP * DK, DV), BF16),
        "carry",
        8,
        0.6,
        scratch=[pltpu.VMEM((group, REP * DK, DV), BF16), pltpu.SemaphoreType.DMA((group,))],
        out_specs=any_space,
    )(*own, *other, carried)
    state_in = lax.all_to_all(states, "ctx", 0, 0, axis_index_groups=groups, tiled=True)
    rows, states = lax.optimization_barrier((rows, states))
    *second, weight_rows = inside_part(early, group - early, rows, 4, 44, chunks // 4)

    early_shape = shape((chunks // 2, depth, width), BF16)
    mixed, own_rows, *others = kernel(
        functools.partial(mixed_kernel, shifts=n_head),
        (shape((tokens, heads * DV), BF16), early_shape)
        + (shape((tokens, width), BF16),) * (n_head - 1),
        "mixed",
        43,
        2.5,
        scratch=[
            pltpu.VMEM(((n_head - 1) * chunks, depth, width), BF16),
            pltpu.SemaphoreType.DMA(((n_head - 1) * chunks,)),
            pltpu.SemaphoreType.DMA((chunks // 2,)),
        ],
        specs=[vmem] * 8 + [any_space],
    )(
        state_in, *first, *second, gate_proj, norm_gain.reshape(1, DV), weight_rows, out_weight
    )
    received = [
        lax.ppermute(other, "head", [(i, (i + 1 + s) % n_head) for i in range(n_head)])
        for s, other in enumerate(others)
    ]
    total = kernel(
        own_columns_kernel,
        shape((tokens, width), BF16),
        "own_columns",
        46,
        2,
        scratch=[
            pltpu.VMEM((chunks - chunks // 2, depth, width), BF16),
            pltpu.SemaphoreType.DMA((chunks - chunks // 2,)),
        ],
        specs=[vmem] * 2 + [any_space],
    )(mixed, own_rows, out_weight).astype(F32)
    for other in received:
        total = total + other.astype(F32)
    return total.astype(BF16)


def solution(mesh):
    return jax.shard_map(
        functools.partial(local, n_ctx=mesh.shape["ctx"], n_head=mesh.shape["head"]),
        mesh=mesh,
        in_specs=(
            P("ctx", "head"),
            P("ctx", "head"),
            P("ctx", "head"),
            P("ctx", "head"),
            P("ctx", "head"),
            P("ctx", "head"),
            P(),
            P("head", None),
        ),
        out_specs=P("ctx", "head"),
        check_vma=False,
    )
```

```python
import functools

import jax
import jax.numpy as jnp
from jax import lax
from jax.experimental import pallas as pl
from jax.experimental.pallas import tpu as pltpu
from jax.sharding import PartitionSpec as P

HV = 32
HK = 16
DK = 128
DV = 128
REP = HV // HK
SMALL_BITS = 4
SMALL_ROWS = 1 << SMALL_BITS
CHUNKS = 8
BASE_BITS = 3
BASE = 1 << BASE_BITS
PIECE_ROWS = 8
EPSILON = 1e-06
BF16 = jnp.bfloat16
F32 = jnp.float32


def nn(a, b):
    return lax.dot_general(a, b, (((1,), (0,)), ((), ())), preferred_element_type=F32)


def nt(a, b):
    return lax.dot_general(a, b, (((1,), (1,)), ((), ())), preferred_element_type=F32)


def two_pieces(x):
    high = x.astype(BF16)
    return high, (x - high.astype(F32)).astype(BF16)


def iotas(shape):
    return lax.broadcasted_iota(jnp.int32, shape, 0), lax.broadcasted_iota(jnp.int32, shape, 1)


def triangles(size):
    row, col = iotas((size, size))
    return row, col, (col <= row).astype(BF16), (row <= col).astype(BF16), (row == col).astype(BF16)


def solved(lowers, rights, size):
    count = len(lowers)
    row, col = iotas((size, size))
    place, lane = iotas((BASE, size))
    packed = []
    for low in lowers:
        held = low[0:BASE]
        for b in range(1, size // BASE):
            held = jnp.where(lane >> BASE_BITS == b, low[b * BASE : (b + 1) * BASE], held)
        packed.append(held)
    packed = jnp.concatenate(packed, axis=0).astype(BF16)
    found = [jnp.where(place == (lane & (BASE - 1)), 1.0, 0.0)] * count
    first_col = col & ~(BASE - 1)
    for k in range(BASE - 1):
        spread = jnp.where(row == first_col + k, 1.0, 0.0).astype(BF16)
        column = nn(packed, spread)
        found = [
            x - column[h * BASE : (h + 1) * BASE] * x[k : k + 1] for h, x in enumerate(found)
        ]
    rounded = [low.astype(BF16) for low in lowers]
    step, apart = BASE, row ^ col
    while True:
        pair = 2 * step
        below = jnp.where((apart >= step) & (apart < pair) & (col < row), 1.0, 0.0).astype(BF16)
        diagonal = jnp.where(apart < step, 1.0, 0.0)
        lane = lax.broadcasted_iota(jnp.int32, (step, size), 1)
        even = (lane & step) == 0
        first = [nn(x.astype(BF16), low * below).astype(BF16) for x, low in zip(found, rounded)]
        whole = [
            (jnp.concatenate([x] * (size // step), axis=0) * diagonal).astype(BF16) for x in found
        ]
        if pair == size:
            ends = [nn(w, right) for w, right in zip(whole, rights)]
            fixes = [nn(f, end.astype(BF16)) for f, end in zip(first, ends)]
            return [
                jnp.concatenate([end[:step], end[step:] - fix], axis=0)
                for end, fix in zip(ends, fixes)
            ]
        second = [nn(f, w) for f, w in zip(first, whole)]
        found = [
            jnp.concatenate([jnp.where(even, x, 0.0), jnp.where(even, -y, x)], axis=0)
            for x, y in zip(found, second)
        ]
        step = pair


def decay_gaps(cum_col, cum_row, row, col):
    return jnp.exp(jnp.where(col <= row, cum_col - cum_row, -1e30))


def inverse_norms(gram, row, col):
    diagonal = jnp.where(row == col, gram, 0.0)
    return (
        lax.rsqrt(jnp.sum(diagonal, axis=1, keepdims=True) + EPSILON),
        lax.rsqrt(jnp.sum(diagonal, axis=0, keepdims=True) + EPSILON),
    )


def place_in_group(group):
    return lax.rem(lax.axis_index("ctx"), group)


def pack_kernel(key_hbm, value_hbm, strength_hbm, decay_hbm, *refs):
    group = len(refs) - 6
    out_refs, (rows_ref, held, scalars, small, in_sems, out_sems) = refs[:group], refs[group:]
    tokens = key_hbm.shape[0]
    heads = strength_hbm.shape[0]
    place = place_in_group(group)
    base = (1 + REP) * tokens
    scalar_copies = [
        pltpu.make_async_copy(ref, scalars.at[kind], in_sems.at[group, kind])
        for kind, ref in enumerate((strength_hbm, decay_hbm))
    ]
    arrivals = []
    for s in range(group):
        j = place ^ s
        sources = [key_hbm.at[:, pl.ds(pl.multiple_of(j * DK, DK), DK)]] + [
            value_hbm.at[:, pl.ds(pl.multiple_of((j * REP + r) * DV, DV), DV)] for r in range(REP)
        ]
        arrivals.append(
            [
                pltpu.make_async_copy(
                    source, held.at[s, pl.ds(n * tokens, tokens), :], in_sems.at[s, n]
                )
                for n, source in enumerate(sources)
            ]
        )
    for copy in scalar_copies + sum(arrivals, []):
        copy.start()
    row, col = iotas((SMALL_ROWS * group, 4 * heads))
    slot, target = row & (SMALL_ROWS - 1), row >> SMALL_BITS

    def picked(target):
        pick = jnp.zeros(row.shape, F32)
        for kind in range(2):
            for piece in range(2):
                at = slot - piece * PIECE_ROWS - kind * REP
                wanted = (2 * kind + piece) * heads + target * REP + at
                pick = pick + jnp.where((at >= 0) & (at < REP) & (col == wanted), 1.0, 0.0)
        return pick.astype(BF16)

    picks = picked(target ^ place), picked(target)
    for copy in scalar_copies:
        copy.wait()
    pieces = jnp.concatenate(two_pieces(scalars[0]) + two_pieces(scalars[1]), axis=0)
    sent, natural = [nn(pick, pieces).astype(BF16) for pick in picks]
    if tokens < DK:
        fill = jnp.zeros((sent.shape[0], DK - tokens), BF16)
        sent, natural = [jnp.concatenate([x, fill], axis=1) for x in (sent, natural)]
    small[...] = natural
    departures = [pltpu.make_async_copy(small, rows_ref, out_sems.at[group])]
    departures[0].start()
    for s, out_ref in enumerate(out_refs):
        held[s, base : base + SMALL_ROWS, :] = sent[s * SMALL_ROWS : (s + 1) * SMALL_ROWS, :]
        for copy in arrivals[s]:
            copy.wait()
        departures.append(pltpu.make_async_copy(held.at[s], out_ref, out_sems.at[s]))
        departures[-1].start()
    for copy in departures:
        copy.wait()


def solved_blocks(blocks, small, tokens):
    row, col, lower_ones, upper_ones, eye = triangles(tokens)
    small = small.astype(F32)
    pieces = [
        jnp.concatenate(
            [
                small[b * SMALL_ROWS + start : b * SMALL_ROWS + start + PIECE_ROWS]
                for b in range(len(blocks))
            ],
            axis=0,
        ).astype(BF16)
        for start in (0, PIECE_ROWS)
    ]
    cum_rows = sum(nn(p, upper_ones) for p in pieces)
    plain_cols = sum(nt(eye, p) for p in pieces)
    cum_cols = sum(nt(lower_ones, p) for p in pieces)

    def spread(array, at):
        return jnp.broadcast_to(array[:, at : at + 1], (tokens, DK))

    lowers, rights, works = [], [], []
    for b, (keys, values) in enumerate(blocks):
        gram = nt(keys, keys)
        key_col, key_row = inverse_norms(gram, row, col)
        key_col = jnp.broadcast_to(key_col, (tokens, DK))
        gram = gram * key_row * key_col[:, :tokens]
        unit_keys = keys.astype(F32) * key_col
        for r in range(REP):
            at = b * PIECE_ROWS + r
            strength = spread(plain_cols, at)
            cum_row, cum_col = cum_rows[at + REP : at + REP + 1, :], spread(cum_cols, at + REP)
            factors = decay_gaps(cum_col[:, :tokens], cum_row, row, col)
            lowers.append(jnp.where(col < row, strength[:, :tokens] * factors * gram, 0.0))
            rights.append(
                jnp.concatenate(
                    [
                        (strength * values[r].astype(F32)).astype(BF16),
                        (strength * jnp.exp(cum_col) * unit_keys).astype(BF16),
                    ],
                    axis=1,
                )
            )
            works.append((keys, cum_col, key_col, key_row, factors))
    return solved(lowers, rights, tokens), works


def inside_kernel(query_ref, key_ref, value_ref, rows_ref, *refs, first, shifts=0):
    copies = []
    if shifts:
        weight_hbm, inside_ref, window_ref, early_ref, sems = refs
        target = lax.rem(lax.axis_index("head") + 1, shifts)
        copies = weight_copies(weight_hbm, target, 0, early_ref, sems)
    else:
        inside_ref, window_ref = refs
    tokens = query_ref.shape[0]
    blocks = inside_ref.shape[0] // REP

    def columns(ref, start, size):
        return ref[:, start * size : (start + 1) * size]

    sides, works = solved_blocks(
        [
            (
                columns(key_ref, j, DK),
                [columns(value_ref, j * REP + r, DV) for r in range(REP)],
            )
            for j in range(first, first + blocks)
        ],
        rows_ref[first * SMALL_ROWS : (first + blocks) * SMALL_ROWS, :][:, :tokens],
        tokens,
    )
    for b in range(blocks):
        queries = columns(query_ref, first + b, DK)
        products = nt(queries, works[b * REP][0])
        queries = queries.astype(F32)
        query_col = lax.rsqrt(
            jnp.sum(queries * queries, axis=1, keepdims=True) + EPSILON
        ) * DK**-0.5
        query_col = jnp.broadcast_to(query_col, (tokens, DK))
        queries = queries * query_col
        products = products * works[b * REP][3] * query_col[:, :tokens]
        for r in range(REP):
            at = b * REP + r
            _, cum_col, _, _, factors = works[at]
            scores = (products * factors).astype(BF16)
            both = nn(scores, sides[at].astype(BF16))
            inside_ref[at] = both[:, :DV].astype(BF16)
            window_ref[at] = (jnp.exp(cum_col) * queries - both[:, DV:]).astype(BF16)
    for copy in copies:
        copy.wait()


def in_order(own_half, own, other):
    return jnp.where(own_half == 0, own, other), jnp.where(own_half == 0, other, own)


def half_kernel(*refs, blocks, group, tokens, own, with_map):
    taken, refs = refs[:blocks], refs[blocks:]
    if not own:
        (own_end, own_map), refs = refs[:2], refs[2:]
    before_ref, map_ref, end_ref, end_map_ref, *refs = refs
    if not own:
        group_ref, *refs = refs
        if with_map:
            group_map_ref, *refs = refs
    offsets, removals, decays = refs
    place = place_in_group(group)
    low = lax.rem(place, blocks)
    base = (1 + REP) * tokens
    sides, works = solved_blocks(
        [
            (t[0:tokens, :], [t[(1 + r) * tokens : (2 + r) * tokens, :] for r in range(REP)])
            for t in taken
        ],
        jnp.concatenate([t[base : base + SMALL_ROWS, :][:, :tokens] for t in taken], axis=0),
        tokens,
    )
    for b in range(blocks):
        keys_turned = works[b * REP][0].T
        for r in range(REP):
            at = b * REP + r
            _, cum_col, key_col, _, _ = works[at]
            last = cum_col[tokens - 1 : tokens, :]
            decays[at] = jnp.broadcast_to(jnp.exp(last), (PIECE_ROWS, DK))
            tail = key_col * jnp.exp(last - cum_col)
            tail = jnp.concatenate([tail, tail], axis=1)
            both = nn(keys_turned, (sides[at] * tail).astype(BF16))
            offsets[at] = both[:, :DV]
            removals[at] = both[:, DV:].astype(BF16)

    key_row, key_col = iotas((DK, DK))
    eye = (key_row == key_col).astype(F32)
    states = [None] * REP
    for i in range(blocks):
        following = []
        for r in range(REP):
            at = (low ^ i) * REP + r
            decay = decays[at][0:1, :]
            if i == 0:
                map_ref[at] = eye.astype(BF16)
                before_ref[at] = jnp.zeros((DK, DV), F32)
                following.append(
                    jnp.concatenate(
                        [eye * decay - removals[at].astype(F32), offsets[at]], axis=1
                    )
                )
                continue
            held = states[r].astype(BF16)
            map_ref[at] = held[:, :DK]
            before_ref[at] = states[r][:, DK:]
            moved = nn(removals[at], held)
            following.append(
                jnp.concatenate(
                    [
                        states[r][:, :DK] * decay - moved[:, :DK],
                        states[r][:, DK:] * decay - moved[:, DK:] + offsets[at],
                    ],
                    axis=1,
                )
            )
        states = following
    own_half = place // blocks
    for r in range(REP):
        end_map, end = states[r][:, :DK], states[r][:, DK:]
        end_map_ref[r] = end_map
        end_ref[r] = end
        if not own:
            first_end, second_end = in_order(own_half, own_end[r], end)
            first_map, second_map = in_order(own_half, own_map[r], end_map)
            second_map = second_map.astype(BF16)
            group_ref[r] = (nn(second_map, first_end.astype(BF16)) + second_end).astype(BF16)
            if with_map:
                group_map_ref[r] = nn(second_map, first_map.astype(BF16))


def carry_kernel(
    own_before, own_maps, own_end, own_map, other_before, other_maps, other_end, other_map,
    carried_ref, out_ref, held, sems,
):
    group = held.shape[0]
    half = group // 2
    place = place_in_group(group)
    own_half = place // half
    later_group = lax.axis_index("ctx") >= group
    starts = []
    for r in range(REP):
        carried = jnp.where(later_group, carried_ref[r].astype(F32), 0.0)
        first_end, _ = in_order(own_half, own_end[r], other_end[r])
        first_map, _ = in_order(own_half, own_map[r], other_map[r])
        middle = first_end + nn(first_map.astype(BF16), carried.astype(BF16))
        starts.append([x.astype(BF16) for x in in_order(own_half, carried, middle)])
    copies = []
    for s in range(group):
        before, maps = (own_before, own_maps) if s < half else (other_before, other_maps)
        for r in range(REP):
            at = (s % half) * REP + r
            start = starts[r][0] if s < half else starts[r][1]
            held[s, r * DK : (r + 1) * DK, :] = (before[at] + nn(maps[at], start)).astype(BF16)
        copies.append(pltpu.make_async_copy(held.at[s], out_ref.at[place ^ s], sems.at[s]))
        copies[-1].start()
    for copy in copies:
        copy.wait()


def weight_copies(weight_hbm, target, first, held, sems):
    count, depth, width = held.shape
    columns = pl.ds(pl.multiple_of(target * width, width), width)
    copies = [
        pltpu.make_async_copy(
            weight_hbm.at[pl.ds((first + c) * depth, depth), columns], held.at[c], sems.at[c]
        )
        for c in range(count)
    ]
    for copy in copies:
        copy.start()
    return copies


def project(chunk_of, targets):
    totals = [None] * len(targets)
    for c in range(len(targets[0])):
        rows = chunk_of(c)
        for n, chunks in enumerate(targets):
            chunk, copy = chunks[c]
            if copy is not None:
                copy.wait()
            part = nn(rows, chunk[...])
            totals[n] = part if totals[n] is None else totals[n] + part
    return [total.astype(BF16) for total in totals]


def mixed_kernel(
    state_ref, first_inside, first_window, second_inside, second_window, gate_ref, gain_ref,
    early_ref, weight_hbm, mixed_ref, own_early_ref, *refs, shifts,
):
    out_refs, (held, sems, own_sems) = refs[:-3], refs[-3:]
    me = lax.axis_index("head")
    early, depth, _ = early_ref.shape
    chunks = held.shape[0] // (shifts - 1)
    targets = []
    for n in range(shifts - 1):
        known = early if n == 0 else 0
        slots = pl.ds(n * chunks, chunks - known)
        copies = weight_copies(
            weight_hbm, lax.rem(me + 1 + n, shifts), known, held.at[slots], sems.at[slots]
        )
        targets.append(
            [(early_ref.at[c], None) for c in range(known)]
            + [(held.at[n * chunks + c], copy) for c, copy in enumerate(copies)]
        )
    own_copies = weight_copies(weight_hbm, me, 0, own_early_ref, own_sems)
    gain = gain_ref[...]
    split = first_inside.shape[0]

    def head(h):
        inside, window, at = (
            (first_inside, first_window, h) if h < split
            else (second_inside, second_window, h - split)
        )
        j, r = h // REP, h % REP
        columns = pl.ds(h * DV, DV)
        rows = inside[at].astype(F32) + nn(window[at], state_ref[j, r * DK : (r + 1) * DK, :])
        scale = lax.rsqrt(jnp.mean(rows * rows, axis=1, keepdims=True) + EPSILON)
        gate = gate_ref[:, columns].astype(F32)
        mixed_ref[:, columns] = (
            rows * scale * gain * (gate / (1.0 + jnp.exp(-gate)))
        ).astype(BF16)

    for h in range(split + second_inside.shape[0]):
        head(h)
    rows = mixed_ref[...]

    def chunk_of(c):
        return rows[:, c * depth : (c + 1) * depth]

    for out_ref, total in zip(out_refs, project(chunk_of, targets)):
        out_ref[...] = total
    for copy in own_copies:
        copy.wait()


def own_columns_kernel(mixed_ref, early_ref, weight_hbm, out_ref, held, sems):
    early, depth, _ = early_ref.shape
    copies = weight_copies(weight_hbm, lax.axis_index("head"), early, held, sems)
    chunks = [(early_ref.at[c], None) for c in range(early)]
    chunks += [(held.at[c], copy) for c, copy in enumerate(copies)]
    (out_ref[...],) = project(lambda c: mixed_ref[:, c * depth : (c + 1) * depth], [chunks])


def local(
    query_proj, key_proj, value_proj, gate_proj, write_strength, log_decay, norm_gain, out_weight,
    *, n_ctx, n_head,
):
    tokens = query_proj.shape[0]
    heads = value_proj.shape[1] // DV
    group = query_proj.shape[1] // DK
    half = group // 2
    width = out_weight.shape[1] // n_head
    n_groups = n_ctx // group
    groups = [list(range(g, g + group)) for g in range(0, n_ctx, group)]
    packed_rows = (1 + REP) * tokens + SMALL_ROWS
    mib = 1024 * 1024

    def kernel(body, out, name, limit, micros, scratch=(), specs=None, out_specs=None):
        return pl.pallas_call(
            body,
            out_shape=out,
            scratch_shapes=scratch,
            compiler_params=pltpu.CompilerParams(
                vmem_limit_bytes=None if limit is None else limit * mib
            ),
            cost_estimate=pl.CostEstimate(
                flops=int(micros * 1e9), bytes_accessed=mib, transcendentals=0
            ),
            name=name,
            **({} if specs is None else {"in_specs": specs}),
            **({} if out_specs is None else {"out_specs": out_specs}),
        )

    def shape(dims, kind):
        return jax.ShapeDtypeStruct(dims, kind)

    def shifted(array, distance):
        return lax.ppermute(array, "ctx", [(i, i + distance) for i in range(n_ctx - distance)])

    def swapped(array, distance):
        return lax.ppermute(array, "ctx", [(i, i ^ distance) for i in range(n_ctx)])

    any_space = pl.BlockSpec(memory_space=pl.ANY)
    vmem = pl.BlockSpec(memory_space=pltpu.VMEM)
    *packed, rows = kernel(
        pack_kernel,
        (shape((packed_rows, DK), BF16),) * group + (shape((group * SMALL_ROWS, DK), BF16),),
        "pack",
        None,
        2,
        scratch=[
            pltpu.VMEM((group, packed_rows, DK), BF16),
            pltpu.VMEM((2, heads, tokens), F32),
            pltpu.VMEM((group * SMALL_ROWS, DK), BF16),
            pltpu.SemaphoreType.DMA((group + 1, 1 + REP)),
            pltpu.SemaphoreType.DMA((group + 1,)),
        ],
        specs=[any_space] * 4,
        out_specs=(any_space,) * (group + 1),
    )(key_proj, value_proj, write_strength.T, log_decay.T)
    taken = [packed[0]] + [swapped(packed[s], s) for s in range(1, group)]

    def half_states(blocks, more, name):
        own, with_map = not more, n_groups > 2
        return kernel(
            functools.partial(half_kernel, blocks=half, group=group, tokens=tokens, own=own, with_map=with_map),
            (
                shape((half * REP, DK, DV), F32),
                shape((half * REP, DK, DK), BF16),
                shape((REP, DK, DV), F32),
                shape((REP, DK, DK), F32),
            )
            + (() if own else (shape((REP, DK, DV), BF16),))
            + ((shape((REP, DK, DK), F32),) if with_map and not own else ()),
            name,
            16,
            3.5,
            scratch=[
                pltpu.VMEM((half * REP, DK, DV), F32),
                pltpu.VMEM((half * REP, DK, DK), BF16),
                pltpu.VMEM((half * REP, PIECE_ROWS, DK), F32),
            ],
        )(*blocks, *more)

    own = half_states(taken[:half], (), "own_half")
    later, own = lax.optimization_barrier((taken[half:], own))
    *other, end = half_states(later, own[2:], "other_half")

    if n_groups == 2:
        carried = swapped(end, group)
    elif n_groups > 2:
        carried, mapping = shifted(other[-1], group).astype(F32), shifted(end, group)
        other = other[:-1]
        distance = 1
        while distance < n_groups - 1:
            earlier, earlier_map = shifted(carried, distance * group), shifted(mapping, distance * group)
            carried = carried + jnp.einsum("rkl,rlv->rkv", mapping, earlier, precision="highest")
            mapping = jnp.einsum("rkl,rlv->rkv", mapping, earlier_map, precision="highest")
            distance *= 2
        carried = carried.astype(BF16)
    else:
        carried = jnp.zeros((REP, DK, DV), BF16)

    chunks = min(CHUNKS, out_weight.shape[0] // DV)
    depth = out_weight.shape[0] // chunks

    def inside_part(start, count, rows, micros, limit, fetch):
        return kernel(
            functools.partial(inside_kernel, first=start, shifts=n_head if fetch else 0),
            (
                shape((count * REP, tokens, DV), BF16),
                shape((count * REP, tokens, DK), BF16),
            )
            + ((shape((fetch, depth, width), BF16),) if fetch else ()),
            "inside",
            limit,
            micros,
            scratch=[pltpu.SemaphoreType.DMA((fetch,))] if fetch else (),
            specs=[vmem] * 4 + ([any_space] if fetch else []),
        )(query_proj, key_proj, value_proj, rows, *((out_weight,) if fetch else ()))

    early = max(1, group // 4)
    rows, end = lax.optimization_barrier((rows, end))
    first = inside_part(0, early, rows, 2.4, 16, 0)
    carried, first = lax.optimization_barrier((carried, first))
    states = kernel(
        carry_kernel,
        shape((group, REP * DK, DV), BF16),
        "carry",
        8,
        0.6,
        scratch=[pltpu.VMEM((group, REP * DK, DV), BF16), pltpu.SemaphoreType.DMA((group,))],
        out_specs=any_space,
    )(*own, *other, carried)
    state_in = lax.all_to_all(states, "ctx", 0, 0, axis_index_groups=groups, tiled=True)
    rows, states = lax.optimization_barrier((rows, states))
    *second, weight_rows = inside_part(early, group - early, rows, 4, 44, chunks // 4)

    early_shape = shape((chunks // 2, depth, width), BF16)
    mixed, own_rows, *others = kernel(
        functools.partial(mixed_kernel, shifts=n_head),
        (shape((tokens, heads * DV), BF16), early_shape)
        + (shape((tokens, width), BF16),) * (n_head - 1),
        "mixed",
        43,
        2.5,
        scratch=[
            pltpu.VMEM(((n_head - 1) * chunks, depth, width), BF16),
            pltpu.SemaphoreType.DMA(((n_head - 1) * chunks,)),
            pltpu.SemaphoreType.DMA((chunks // 2,)),
        ],
        specs=[vmem] * 8 + [any_space],
    )(
        state_in, *first, *second, gate_proj, norm_gain.reshape(1, DV), weight_rows, out_weight
    )
    received = [
        lax.ppermute(other, "head", [(i, (i + 1 + s) % n_head) for i in range(n_head)])
        for s, other in enumerate(others)
    ]
    total = kernel(
        own_columns_kernel,
        shape((tokens, width), BF16),
        "own_columns",
        46,
        2,
        scratch=[
            pltpu.VMEM((chunks - chunks // 2, depth, width), BF16),
            pltpu.SemaphoreType.DMA((chunks - chunks // 2,)),
        ],
        specs=[vmem] * 2 + [any_space],
    )(mixed, own_rows, out_weight).astype(F32)
    for other in received:
        total = total + other.astype(F32)
    return total.astype(BF16)


def solution(mesh):
    return jax.shard_map(
        functools.partial(local, n_ctx=mesh.shape["ctx"], n_head=mesh.shape["head"]),
        mesh=mesh,
        in_specs=(
            P("ctx", "head"),
            P("ctx", "head"),
            P("ctx", "head"),
            P("ctx", "head"),
            P("ctx", "head"),
            P("ctx", "head"),
            P(),
            P("head", None),
        ),
        out_specs=P("ctx", "head"),
        check_vma=False,
    )
```

```python
import functools

import jax
import jax.numpy as jnp
from jax import lax
from jax.experimental import pallas as pl
from jax.experimental.pallas import tpu as pltpu
from jax.sharding import PartitionSpec as P

HV = 32
HK = 16
DK = 128
DV = 128
REP = HV // HK
SMALL_BITS = 4
SMALL_ROWS = 1 << SMALL_BITS
BASE_BITS = 3
BASE = 1 << BASE_BITS
PIECE_ROWS = 8
EPSILON = 1e-06
BF16 = jnp.bfloat16
F32 = jnp.float32


def nn(a, b):
    return lax.dot_general(a, b, (((1,), (0,)), ((), ())), preferred_element_type=F32)


def nt(a, b):
    return lax.dot_general(a, b, (((1,), (1,)), ((), ())), preferred_element_type=F32)


def two_pieces(x):
    high = x.astype(BF16)
    return high, (x - high.astype(F32)).astype(BF16)


def iotas(shape):
    return lax.broadcasted_iota(jnp.int32, shape, 0), lax.broadcasted_iota(jnp.int32, shape, 1)


def triangles(size):
    row, col = iotas((size, size))
    return row, col, (col <= row).astype(BF16), (row <= col).astype(BF16), (row == col).astype(BF16)


def solved(lowers, rights, size):
    count = len(lowers)
    row, col = iotas((size, size))
    place, lane = iotas((BASE, size))
    packed = []
    for low in lowers:
        held = low[0:BASE]
        for b in range(1, size // BASE):
            held = jnp.where(lane >> BASE_BITS == b, low[b * BASE : (b + 1) * BASE], held)
        packed.append(held)
    packed = jnp.concatenate(packed, axis=0).astype(BF16)
    found = [jnp.where(place == (lane & (BASE - 1)), 1.0, 0.0)] * count
    first_col = col & ~(BASE - 1)
    for k in range(BASE - 1):
        spread = jnp.where(row == first_col + k, 1.0, 0.0).astype(BF16)
        column = nn(packed, spread)
        found = [
            x - column[h * BASE : (h + 1) * BASE] * x[k : k + 1] for h, x in enumerate(found)
        ]
    rounded = [low.astype(BF16) for low in lowers]
    step, apart = BASE, row ^ col
    while True:
        pair = 2 * step
        below = jnp.where((apart >= step) & (apart < pair) & (col < row), 1.0, 0.0).astype(BF16)
        diagonal = jnp.where(apart < step, 1.0, 0.0)
        lane = lax.broadcasted_iota(jnp.int32, (step, size), 1)
        even = (lane & step) == 0
        first = [nn(x.astype(BF16), low * below).astype(BF16) for x, low in zip(found, rounded)]
        whole = [
            (jnp.concatenate([x] * (size // step), axis=0) * diagonal).astype(BF16) for x in found
        ]
        if pair == size:
            ends = [nn(w, right) for w, right in zip(whole, rights)]
            fixes = [nn(f, end.astype(BF16)) for f, end in zip(first, ends)]
            return [
                jnp.concatenate([end[:step], end[step:] - fix], axis=0)
                for end, fix in zip(ends, fixes)
            ]
        second = [nn(f, w) for f, w in zip(first, whole)]
        found = [
            jnp.concatenate([jnp.where(even, x, 0.0), jnp.where(even, -y, x)], axis=0)
            for x, y in zip(found, second)
        ]
        step = pair


def decay_gaps(cum_col, cum_row, row, col):
    return jnp.exp(jnp.where(col <= row, cum_col - cum_row, -1e30))


def inverse_norms(gram, row, col):
    diagonal = jnp.where(row == col, gram, 0.0)
    return (
        lax.rsqrt(jnp.sum(diagonal, axis=1, keepdims=True) + EPSILON),
        lax.rsqrt(jnp.sum(diagonal, axis=0, keepdims=True) + EPSILON),
    )


def place_in_group(group):
    return lax.rem(lax.axis_index("ctx"), group)


def pack_kernel(key_hbm, value_hbm, strength_hbm, decay_hbm, *refs):
    group = len(refs) - 6
    out_refs, (rows_ref, held, scalars, small, in_sems, out_sems) = refs[:group], refs[group:]
    tokens = key_hbm.shape[0]
    heads = strength_hbm.shape[0]
    place = place_in_group(group)
    base = (1 + REP) * tokens
    scalar_copies = [
        pltpu.make_async_copy(ref, scalars.at[kind], in_sems.at[group, kind])
        for kind, ref in enumerate((strength_hbm, decay_hbm))
    ]
    arrivals = []
    for s in range(group):
        j = place ^ s
        sources = [key_hbm.at[:, pl.ds(pl.multiple_of(j * DK, DK), DK)]] + [
            value_hbm.at[:, pl.ds(pl.multiple_of((j * REP + r) * DV, DV), DV)] for r in range(REP)
        ]
        arrivals.append(
            [
                pltpu.make_async_copy(
                    source, held.at[s, pl.ds(n * tokens, tokens), :], in_sems.at[s, n]
                )
                for n, source in enumerate(sources)
            ]
        )
    for copy in scalar_copies + sum(arrivals, []):
        copy.start()
    row, col = iotas((SMALL_ROWS * group, 4 * heads))
    slot, target = row & (SMALL_ROWS - 1), row >> SMALL_BITS

    def picked(target):
        pick = jnp.zeros(row.shape, F32)
        for kind in range(2):
            for piece in range(2):
                at = slot - piece * PIECE_ROWS - kind * REP
                wanted = (2 * kind + piece) * heads + target * REP + at
                pick = pick + jnp.where((at >= 0) & (at < REP) & (col == wanted), 1.0, 0.0)
        return pick.astype(BF16)

    picks = picked(target ^ place), picked(target)
    for copy in scalar_copies:
        copy.wait()
    pieces = jnp.concatenate(two_pieces(scalars[0]) + two_pieces(scalars[1]), axis=0)
    sent, natural = [nn(pick, pieces).astype(BF16) for pick in picks]
    if tokens < DK:
        fill = jnp.zeros((sent.shape[0], DK - tokens), BF16)
        sent, natural = [jnp.concatenate([x, fill], axis=1) for x in (sent, natural)]
    small[...] = natural
    departures = [pltpu.make_async_copy(small, rows_ref, out_sems.at[group])]
    departures[0].start()
    for s, out_ref in enumerate(out_refs):
        held[s, base : base + SMALL_ROWS, :] = sent[s * SMALL_ROWS : (s + 1) * SMALL_ROWS, :]
        for copy in arrivals[s]:
            copy.wait()
        departures.append(pltpu.make_async_copy(held.at[s], out_ref, out_sems.at[s]))
        departures[-1].start()
    for copy in departures:
        copy.wait()


def solved_blocks(blocks, small, tokens):
    row, col, lower_ones, upper_ones, eye = triangles(tokens)
    small = small.astype(F32)
    pieces = [
        jnp.concatenate(
            [
                small[b * SMALL_ROWS + start : b * SMALL_ROWS + start + PIECE_ROWS]
                for b in range(len(blocks))
            ],
            axis=0,
        ).astype(BF16)
        for start in (0, PIECE_ROWS)
    ]
    cum_rows = sum(nn(p, upper_ones) for p in pieces)
    plain_cols = sum(nt(eye, p) for p in pieces)
    cum_cols = sum(nt(lower_ones, p) for p in pieces)

    def spread(array, at):
        return jnp.broadcast_to(array[:, at : at + 1], (tokens, DK))

    lowers, rights, works = [], [], []
    for b, (keys, values) in enumerate(blocks):
        gram = nt(keys, keys)
        key_col, key_row = inverse_norms(gram, row, col)
        key_col = jnp.broadcast_to(key_col, (tokens, DK))
        gram = gram * key_row * key_col[:, :tokens]
        unit_keys = keys.astype(F32) * key_col
        for r in range(REP):
            at = b * PIECE_ROWS + r
            strength = spread(plain_cols, at)
            cum_row, cum_col = cum_rows[at + REP : at + REP + 1, :], spread(cum_cols, at + REP)
            factors = decay_gaps(cum_col[:, :tokens], cum_row, row, col)
            lowers.append(jnp.where(col < row, strength[:, :tokens] * factors * gram, 0.0))
            rights.append(
                jnp.concatenate(
                    [
                        (strength * values[r].astype(F32)).astype(BF16),
                        (strength * jnp.exp(cum_col) * unit_keys).astype(BF16),
                    ],
                    axis=1,
                )
            )
            works.append((keys, cum_col, key_col, key_row, factors))
    return solved(lowers, rights, tokens), works


def inside_heads(query_ref, key_ref, value_ref, rows_ref, inside_ref, window_ref, first, blocks):
    tokens = query_ref.shape[0]

    def columns(ref, start, size):
        return ref[:, start * size : (start + 1) * size]

    sides, works = solved_blocks(
        [
            (
                columns(key_ref, j, DK),
                [columns(value_ref, j * REP + r, DV) for r in range(REP)],
            )
            for j in range(first, first + blocks)
        ],
        rows_ref[first * SMALL_ROWS : (first + blocks) * SMALL_ROWS, :][:, :tokens],
        tokens,
    )
    for b in range(blocks):
        queries = columns(query_ref, first + b, DK)
        products = nt(queries, works[b * REP][0])
        queries = queries.astype(F32)
        query_col = lax.rsqrt(
            jnp.sum(queries * queries, axis=1, keepdims=True) + EPSILON
        ) * DK**-0.5
        query_col = jnp.broadcast_to(query_col, (tokens, DK))
        queries = queries * query_col
        products = products * works[b * REP][3] * query_col[:, :tokens]
        for r in range(REP):
            at = b * REP + r
            _, cum_col, _, _, factors = works[at]
            scores = (products * factors).astype(BF16)
            both = nn(scores, sides[at].astype(BF16))
            to = first * REP + at
            inside_ref[to] = both[:, :DV].astype(BF16)
            window_ref[to] = (jnp.exp(cum_col) * queries - both[:, DV:]).astype(BF16)


def early_inside_kernel(*refs, group):
    @pl.when(lax.axis_index("ctx") < group)
    def _():
        inside_heads(*refs, 0, group // 2)


def inside_kernel(early_inside, early_window, *refs, group):
    known = (group // 2) * REP
    first_group = lax.axis_index("ctx") < group

    @pl.when(first_group)
    def _():
        inside_ref, window_ref = refs[-2:]
        inside_ref[0:known] = early_inside[...]
        window_ref[0:known] = early_window[...]
        inside_heads(*refs, group // 2, group - group // 2)

    @pl.when(jnp.logical_not(first_group))
    def _():
        inside_heads(*refs, 0, group)


def in_order(own_half, own, other):
    return jnp.where(own_half == 0, own, other), jnp.where(own_half == 0, other, own)


def half_kernel(*refs, blocks, extra, group, tokens, own, with_map):
    count = blocks + extra if own else blocks - extra
    taken, refs = refs[:count], refs[count:]
    if not own:
        (own_end, own_map), refs = refs[:2], refs[2:]
    known = ()
    if extra and not own:
        known, refs = refs[:3], refs[3:]
    before_ref, map_ref, end_ref, end_map_ref, *refs = refs
    if not own:
        group_ref, *refs = refs
        if with_map:
            group_map_ref, *refs = refs
    handed = ()
    if extra and own:
        handed, refs = refs[:3], refs[3:]
    offsets, removals, decays = refs
    place = place_in_group(group)
    low = lax.rem(place, blocks)
    base = (1 + REP) * tokens
    sides, works = solved_blocks(
        [
            (t[0:tokens, :], [t[(1 + r) * tokens : (2 + r) * tokens, :] for r in range(REP)])
            for t in taken
        ],
        jnp.concatenate([t[base : base + SMALL_ROWS, :][:, :tokens] for t in taken], axis=0),
        tokens,
    )
    if known:
        for held, ref in zip((offsets, removals, decays), known):
            held[0 : extra * REP] = ref[...]
    for b in range(count):
        keys_turned = works[b * REP][0].T
        for r in range(REP):
            at = b * REP + r
            _, cum_col, key_col, _, _ = works[at]
            last = cum_col[tokens - 1 : tokens, :]
            tail = key_col * jnp.exp(last - cum_col)
            tail = jnp.concatenate([tail, tail], axis=1)
            both = nn(keys_turned, (sides[at] * tail).astype(BF16))
            to, held = at if own else at + extra * REP, (offsets, removals, decays)
            if own and b >= blocks:
                to, held = at - blocks * REP, handed
            held[0][to] = both[:, :DV]
            held[1][to] = both[:, DV:].astype(BF16)
            held[2][to] = jnp.broadcast_to(jnp.exp(last), (PIECE_ROWS, DK))

    key_row, key_col = iotas((DK, DK))
    eye = (key_row == key_col).astype(F32)
    states = [None] * REP
    for i in range(blocks):
        following = []
        for r in range(REP):
            at = (low ^ i) * REP + r
            decay = decays[at][0:1, :]
            if i == 0:
                map_ref[at] = eye.astype(BF16)
                before_ref[at] = jnp.zeros((DK, DV), F32)
                following.append(
                    jnp.concatenate(
                        [eye * decay - removals[at].astype(F32), offsets[at]], axis=1
                    )
                )
                continue
            held = states[r].astype(BF16)
            map_ref[at] = held[:, :DK]
            before_ref[at] = states[r][:, DK:]
            moved = nn(removals[at], held)
            following.append(
                jnp.concatenate(
                    [
                        states[r][:, :DK] * decay - moved[:, :DK],
                        states[r][:, DK:] * decay - moved[:, DK:] + offsets[at],
                    ],
                    axis=1,
                )
            )
        states = following
    own_half = place // blocks
    for r in range(REP):
        end_map, end = states[r][:, :DK], states[r][:, DK:]
        end_map_ref[r] = end_map
        end_ref[r] = end
        if not own:
            first_end, second_end = in_order(own_half, own_end[r], end)
            first_map, second_map = in_order(own_half, own_map[r], end_map)
            second_map = second_map.astype(BF16)
            group_ref[r] = (nn(second_map, first_end.astype(BF16)) + second_end).astype(BF16)
            if with_map:
                group_map_ref[r] = nn(second_map, first_map.astype(BF16))


def carry_kernel(
    own_before, own_maps, own_end, own_map, other_before, other_maps, other_end, other_map,
    carried_ref, out_ref,
):
    group = out_ref.shape[0]
    half = group // 2
    place = place_in_group(group)
    own_half = place // half
    later_group = lax.axis_index("ctx") >= group
    starts = []
    for r in range(REP):
        carried = jnp.where(later_group, carried_ref[r].astype(F32), 0.0)
        first_end, _ = in_order(own_half, own_end[r], other_end[r])
        first_map, _ = in_order(own_half, own_map[r], other_map[r])
        middle = first_end + nn(first_map.astype(BF16), carried.astype(BF16))
        starts.append([x.astype(BF16) for x in in_order(own_half, carried, middle)])
    for s in range(group):
        before, maps = (own_before, own_maps) if s < half else (other_before, other_maps)
        for r in range(REP):
            at = (s % half) * REP + r
            start = starts[r][0] if s < half else starts[r][1]
            out_ref[place ^ s, r * DK : (r + 1) * DK, :] = (
                before[at] + nn(maps[at], start)
            ).astype(BF16)


def columns_of(width, target):
    return pl.ds(pl.multiple_of(target * width, width), width)


def mixed_kernel(
    state_ref, inside_ref, window_ref, gate_ref, gain_ref, weight_ref, mixed_ref, *out_refs, shifts
):
    me = lax.axis_index("head")
    gain = gain_ref[...]
    for j in range(state_ref.shape[0]):
        for r in range(REP):
            h = j * REP + r
            columns = pl.ds(h * DV, DV)
            state = state_ref[j, r * DK : (r + 1) * DK, :]
            rows = inside_ref[h].astype(F32) + nn(window_ref[h], state)
            scale = lax.rsqrt(jnp.mean(rows * rows, axis=1, keepdims=True) + EPSILON)
            gate = gate_ref[:, columns].astype(F32)
            mixed_ref[:, columns] = (
                rows * scale * gain * (gate / (1.0 + jnp.exp(-gate)))
            ).astype(BF16)
    for n, out_ref in enumerate(out_refs):
        columns = columns_of(out_ref.shape[1], lax.rem(me + 1 + n, shifts))
        out_ref[...] = nn(mixed_ref[...], weight_ref[:, columns]).astype(BF16)


def own_columns_kernel(mixed_ref, weight_ref, out_ref):
    columns = columns_of(out_ref.shape[1], lax.axis_index("head"))
    out_ref[...] = nn(mixed_ref[...], weight_ref[:, columns]).astype(BF16)


def local(
    query_proj, key_proj, value_proj, gate_proj, write_strength, log_decay, norm_gain, out_weight,
    *, n_ctx, n_head,
):
    tokens = query_proj.shape[0]
    heads = value_proj.shape[1] // DV
    group = query_proj.shape[1] // DK
    half = group // 2
    width = out_weight.shape[1] // n_head
    n_groups = n_ctx // group
    packed_rows = (1 + REP) * tokens + SMALL_ROWS
    mib = 1024 * 1024

    def kernel(body, out, name, limit, micros, scratch=(), specs=None, out_specs=None):
        return pl.pallas_call(
            body,
            out_shape=out,
            scratch_shapes=scratch,
            compiler_params=pltpu.CompilerParams(
                vmem_limit_bytes=None if limit is None else int(limit * mib)
            ),
            cost_estimate=pl.CostEstimate(
                flops=int(micros * 1e9), bytes_accessed=mib, transcendentals=0
            ),
            name=name,
            **({} if specs is None else {"in_specs": specs}),
            **({} if out_specs is None else {"out_specs": out_specs}),
        )

    def shape(dims, kind):
        return jax.ShapeDtypeStruct(dims, kind)

    def shifted(array, distance):
        return lax.ppermute(array, "ctx", [(i, i + distance) for i in range(n_ctx - distance)])

    def swapped(array, distance):
        return lax.ppermute(array, "ctx", [(i, i ^ distance) for i in range(n_ctx)])

    any_space = pl.BlockSpec(memory_space=pl.ANY)
    vmem = pl.BlockSpec(memory_space=pltpu.VMEM)
    *packed, rows = kernel(
        pack_kernel,
        (shape((packed_rows, DK), BF16),) * group + (shape((group * SMALL_ROWS, DK), BF16),),
        "pack",
        None,
        2,
        scratch=[
            pltpu.VMEM((group, packed_rows, DK), BF16),
            pltpu.VMEM((2, heads, tokens), F32),
            pltpu.VMEM((group * SMALL_ROWS, DK), BF16),
            pltpu.SemaphoreType.DMA((group + 1, 1 + REP)),
            pltpu.SemaphoreType.DMA((group + 1,)),
        ],
        specs=[any_space] * 4,
        out_specs=(any_space,) * (group + 1),
    )(key_proj, value_proj, write_strength.T, log_decay.T)
    taken = [packed[0]] + [swapped(packed[s], s) for s in range(1, group)]

    extra = 1 if half >= 4 else 0

    def half_states(blocks, more, name):
        own, with_map = not more, n_groups > 2
        passed = (
            shape((extra * REP, DK, DV), F32),
            shape((extra * REP, DK, DK), BF16),
            shape((extra * REP, PIECE_ROWS, DK), F32),
        )
        return kernel(
            functools.partial(
                half_kernel, blocks=half, extra=extra, group=group, tokens=tokens, own=own,
                with_map=with_map,
            ),
            (
                shape((half * REP, DK, DV), F32),
                shape((half * REP, DK, DK), BF16),
                shape((REP, DK, DV), F32),
                shape((REP, DK, DK), F32),
            )
            + (() if own else (shape((REP, DK, DV), BF16),))
            + ((shape((REP, DK, DK), F32),) if with_map and not own else ())
            + (passed if own and extra else ()),
            name,
            16,
            3.5,
            scratch=[
                pltpu.VMEM((half * REP, DK, DV), F32),
                pltpu.VMEM((half * REP, DK, DK), BF16),
                pltpu.VMEM((half * REP, PIECE_ROWS, DK), F32),
            ],
        )(*blocks, *more)

    own = half_states(taken[: half + extra], (), "own_half")
    later, own = lax.optimization_barrier((taken[half + extra :], own))
    *other, end = half_states(later, own[2:], "other_half")
    own = own[:4]

    def inside_part(body, name, count, micros, operands):
        return kernel(
            functools.partial(body, group=group),
            (shape((count, tokens, DV), BF16), shape((count, tokens, DK), BF16)),
            name,
            16,
            micros,
        )(*operands)

    rows, end = lax.optimization_barrier((rows, end))
    activations = (query_proj, key_proj, value_proj, rows)
    early = inside_part(early_inside_kernel, "early_inside", half * REP, 3, activations)
    end, *early = lax.optimization_barrier((end, *early))

    if n_groups == 2:
        carried = swapped(end, group)
    elif n_groups > 2:
        carried, mapping = shifted(other[-1], group).astype(F32), shifted(end, group)
        other = other[:-1]
        distance = 1
        while distance < n_groups - 1:
            earlier, earlier_map = shifted(carried, distance * group), shifted(mapping, distance * group)
            carried = carried + jnp.einsum("rkl,rlv->rkv", mapping, earlier, precision="highest")
            mapping = jnp.einsum("rkl,rlv->rkv", mapping, earlier_map, precision="highest")
            distance *= 2
        carried = carried.astype(BF16)
    else:
        carried = jnp.zeros((REP, DK, DV), BF16)

    inside, window = inside_part(inside_kernel, "inside", heads, 5, (*early, *activations))
    carried, inside, window = lax.optimization_barrier((carried, inside, window))
    states = kernel(
        carry_kernel, shape((group, REP * DK, DV), BF16), "carry", 8, 0.6
    )(*own, *other, carried)
    groups = [list(range(g, g + group)) for g in range(0, n_ctx, group)]
    state_in = lax.all_to_all(states, "ctx", 0, 0, axis_index_groups=groups, tiled=True)

    mixed, *others = kernel(
        functools.partial(mixed_kernel, shifts=n_head),
        (shape((tokens, heads * DV), BF16),) + (shape((tokens, width), BF16),) * (n_head - 1),
        "mixed",
        16,
        2,
    )(state_in, inside, window, gate_proj, norm_gain.reshape(1, DV), out_weight)
    received = [
        lax.ppermute(other, "head", [(i, (i + 1 + s) % n_head) for i in range(n_head)])
        for s, other in enumerate(others)
    ]
    total = kernel(own_columns_kernel, shape((tokens, width), BF16), "own_columns", 16, 1)(
        mixed, out_weight
    ).astype(F32)
    for other in received:
        total = total + other.astype(F32)
    return total.astype(BF16)


def solution(mesh):
    return jax.shard_map(
        functools.partial(local, n_ctx=mesh.shape["ctx"], n_head=mesh.shape["head"]),
        mesh=mesh,
        in_specs=(
            P("ctx", "head"),
            P("ctx", "head"),
            P("ctx", "head"),
            P("ctx", "head"),
            P("ctx", "head"),
            P("ctx", "head"),
            P(),
            P("head", None),
        ),
        out_specs=P("ctx", "head"),
        check_vma=False,
    )
```

```python
import functools

import jax
import jax.numpy as jnp
from jax import lax
from jax.experimental import pallas as pl
from jax.experimental.pallas import tpu as pltpu
from jax.sharding import PartitionSpec as P

HV = 32
HK = 16
DK = 128
DV = 128
REP = HV // HK
SMALL_BITS = 4
SMALL_ROWS = 1 << SMALL_BITS
BASE_BITS = 4
BASE = 1 << BASE_BITS
PIECE_ROWS = 8
EPSILON = 1e-06
BF16 = jnp.bfloat16
F32 = jnp.float32


def nn(a, b):
    return lax.dot_general(a, b, (((1,), (0,)), ((), ())), preferred_element_type=F32)


def nt(a, b):
    return lax.dot_general(a, b, (((1,), (1,)), ((), ())), preferred_element_type=F32)


def two_pieces(x):
    high = x.astype(BF16)
    return high, (x - high.astype(F32)).astype(BF16)


def iotas(shape):
    return lax.broadcasted_iota(jnp.int32, shape, 0), lax.broadcasted_iota(jnp.int32, shape, 1)


def triangles(size):
    row, col = iotas((size, size))
    return row, col, (col <= row).astype(BF16), (row <= col).astype(BF16), (row == col).astype(BF16)


def solved(lowers, rights, size):
    count = len(lowers)
    row, col = iotas((size, size))
    place, lane = iotas((BASE, size))
    packed = []
    for low in lowers:
        held = low[0:BASE]
        for b in range(1, size // BASE):
            held = jnp.where(lane >> BASE_BITS == b, low[b * BASE : (b + 1) * BASE], held)
        packed.append(held)
    packed = jnp.concatenate(packed, axis=0).astype(BF16)
    found = [jnp.where(place == (lane & (BASE - 1)), 1.0, 0.0)] * count
    first_col = col & ~(BASE - 1)
    for k in range(BASE - 1):
        spread = jnp.where(row == first_col + k, 1.0, 0.0).astype(BF16)
        column = nn(packed, spread)
        found = [
            x - column[h * BASE : (h + 1) * BASE] * x[k : k + 1] for h, x in enumerate(found)
        ]
    rounded = [low.astype(BF16) for low in lowers]
    step, apart = BASE, row ^ col
    while True:
        pair = 2 * step
        below = jnp.where((apart >= step) & (apart < pair) & (col < row), 1.0, 0.0).astype(BF16)
        diagonal = jnp.where(apart < step, 1.0, 0.0)
        lane = lax.broadcasted_iota(jnp.int32, (step, size), 1)
        even = (lane & step) == 0
        first = [nn(x.astype(BF16), low * below).astype(BF16) for x, low in zip(found, rounded)]
        whole = [
            (jnp.concatenate([x] * (size // step), axis=0) * diagonal).astype(BF16) for x in found
        ]
        if pair == size:
            ends = [nn(w, right) for w, right in zip(whole, rights)]
            fixes = [nn(f, end.astype(BF16)) for f, end in zip(first, ends)]
            return [
                jnp.concatenate([end[:step], end[step:] - fix], axis=0)
                for end, fix in zip(ends, fixes)
            ]
        second = [nn(f, w) for f, w in zip(first, whole)]
        found = [
            jnp.concatenate([jnp.where(even, x, 0.0), jnp.where(even, -y, x)], axis=0)
            for x, y in zip(found, second)
        ]
        step = pair


def decay_gaps(cum_col, cum_row, row, col):
    return jnp.exp(jnp.where(col <= row, cum_col - cum_row, -1e30))


def inverse_norms(gram, row, col):
    diagonal = jnp.where(row == col, gram, 0.0)
    return (
        lax.rsqrt(jnp.sum(diagonal, axis=1, keepdims=True) + EPSILON),
        lax.rsqrt(jnp.sum(diagonal, axis=0, keepdims=True) + EPSILON),
    )


def place_in_group(group):
    return lax.rem(lax.axis_index("ctx"), group)


def pack_kernel(key_hbm, value_hbm, strength_hbm, decay_hbm, *refs):
    group = len(refs) - 6
    out_refs, (rows_ref, held, scalars, small, in_sems, out_sems) = refs[:group], refs[group:]
    tokens = key_hbm.shape[0]
    heads = strength_hbm.shape[0]
    place = place_in_group(group)
    base = (1 + REP) * tokens
    scalar_copies = [
        pltpu.make_async_copy(ref, scalars.at[kind], in_sems.at[group, kind])
        for kind, ref in enumerate((strength_hbm, decay_hbm))
    ]
    arrivals = []
    for s in range(group):
        j = place ^ s
        sources = [key_hbm.at[:, pl.ds(pl.multiple_of(j * DK, DK), DK)]] + [
            value_hbm.at[:, pl.ds(pl.multiple_of((j * REP + r) * DV, DV), DV)] for r in range(REP)
        ]
        arrivals.append(
            [
                pltpu.make_async_copy(
                    source, held.at[s, pl.ds(n * tokens, tokens), :], in_sems.at[s, n]
                )
                for n, source in enumerate(sources)
            ]
        )
    for copy in scalar_copies + sum(arrivals, []):
        copy.start()
    row, col = iotas((SMALL_ROWS * group, 4 * heads))
    slot, target = row & (SMALL_ROWS - 1), row >> SMALL_BITS

    def picked(target):
        pick = jnp.zeros(row.shape, F32)
        for kind in range(2):
            for piece in range(2):
                at = slot - piece * PIECE_ROWS - kind * REP
                wanted = (2 * kind + piece) * heads + target * REP + at
                pick = pick + jnp.where((at >= 0) & (at < REP) & (col == wanted), 1.0, 0.0)
        return pick.astype(BF16)

    picks = picked(target ^ place), picked(target)
    for copy in scalar_copies:
        copy.wait()
    pieces = jnp.concatenate(two_pieces(scalars[0]) + two_pieces(scalars[1]), axis=0)
    sent, natural = [nn(pick, pieces).astype(BF16) for pick in picks]
    if tokens < DK:
        fill = jnp.zeros((sent.shape[0], DK - tokens), BF16)
        sent, natural = [jnp.concatenate([x, fill], axis=1) for x in (sent, natural)]
    small[...] = natural
    departures = [pltpu.make_async_copy(small, rows_ref, out_sems.at[group])]
    departures[0].start()
    for s, out_ref in enumerate(out_refs):
        held[s, base : base + SMALL_ROWS, :] = sent[s * SMALL_ROWS : (s + 1) * SMALL_ROWS, :]
        for copy in arrivals[s]:
            copy.wait()
        departures.append(pltpu.make_async_copy(held.at[s], out_ref, out_sems.at[s]))
        departures[-1].start()
    for copy in departures:
        copy.wait()


def solved_blocks(blocks, small, tokens):
    row, col, lower_ones, upper_ones, eye = triangles(tokens)
    small = small.astype(F32)
    pieces = [
        jnp.concatenate(
            [
                small[b * SMALL_ROWS + start : b * SMALL_ROWS + start + PIECE_ROWS]
                for b in range(len(blocks))
            ],
            axis=0,
        ).astype(BF16)
        for start in (0, PIECE_ROWS)
    ]
    cum_rows = sum(nn(p, upper_ones) for p in pieces)
    plain_cols = sum(nt(eye, p) for p in pieces)
    cum_cols = sum(nt(lower_ones, p) for p in pieces)

    def spread(array, at):
        return jnp.broadcast_to(array[:, at : at + 1], (tokens, DK))

    lowers, rights, works = [], [], []
    for b, (keys, values) in enumerate(blocks):
        gram = nt(keys, keys)
        key_col, key_row = inverse_norms(gram, row, col)
        key_col = jnp.broadcast_to(key_col, (tokens, DK))
        gram = gram * key_row * key_col[:, :tokens]
        unit_keys = keys.astype(F32) * key_col
        for r in range(REP):
            at = b * PIECE_ROWS + r
            strength = spread(plain_cols, at)
            cum_row, cum_col = cum_rows[at + REP : at + REP + 1, :], spread(cum_cols, at + REP)
            factors = decay_gaps(cum_col[:, :tokens], cum_row, row, col)
            lowers.append(jnp.where(col < row, strength[:, :tokens] * factors * gram, 0.0))
            rights.append(
                jnp.concatenate(
                    [
                        (strength * values[r].astype(F32)).astype(BF16),
                        (strength * jnp.exp(cum_col) * unit_keys).astype(BF16),
                    ],
                    axis=1,
                )
            )
            works.append((keys, cum_col, key_col, key_row, factors))
    return solved(lowers, rights, tokens), works


def inside_kernel(query_ref, key_ref, value_ref, rows_ref, inside_ref, window_ref):
    tokens = query_ref.shape[0]
    blocks = inside_ref.shape[0] // REP

    def columns(ref, start, size):
        return ref[:, start * size : (start + 1) * size]

    sides, works = solved_blocks(
        [
            (
                columns(key_ref, j, DK),
                [columns(value_ref, j * REP + r, DV) for r in range(REP)],
            )
            for j in range(blocks)
        ],
        rows_ref[:, :tokens],
        tokens,
    )
    for b in range(blocks):
        queries = columns(query_ref, b, DK)
        products = nt(queries, works[b * REP][0])
        queries = queries.astype(F32)
        query_col = lax.rsqrt(
            jnp.sum(queries * queries, axis=1, keepdims=True) + EPSILON
        ) * DK**-0.5
        query_col = jnp.broadcast_to(query_col, (tokens, DK))
        queries = queries * query_col
        products = products * works[b * REP][3] * query_col[:, :tokens]
        for r in range(REP):
            at = b * REP + r
            _, cum_col, _, _, factors = works[at]
            scores = (products * factors).astype(BF16)
            both = nn(scores, sides[at].astype(BF16))
            inside_ref[at] = both[:, :DV].astype(BF16)
            window_ref[at] = (jnp.exp(cum_col) * queries - both[:, DV:]).astype(BF16)


def in_order(own_half, own, other):
    return jnp.where(own_half == 0, own, other), jnp.where(own_half == 0, other, own)


def half_kernel(*refs, blocks, extra, group, tokens, own, with_map):
    count = blocks + extra if own else blocks - extra
    taken, refs = refs[:count], refs[count:]
    if not own:
        (own_end, own_map), refs = refs[:2], refs[2:]
    known = ()
    if extra and not own:
        known, refs = refs[:3], refs[3:]
    before_ref, map_ref, end_ref, end_map_ref, *refs = refs
    if not own:
        group_ref, *refs = refs
        if with_map:
            group_map_ref, *refs = refs
    handed = ()
    if extra and own:
        handed, refs = refs[:3], refs[3:]
    offsets, removals, decays = refs
    place = place_in_group(group)
    low = lax.rem(place, blocks)
    base = (1 + REP) * tokens
    sides, works = solved_blocks(
        [
            (t[0:tokens, :], [t[(1 + r) * tokens : (2 + r) * tokens, :] for r in range(REP)])
            for t in taken
        ],
        jnp.concatenate([t[base : base + SMALL_ROWS, :][:, :tokens] for t in taken], axis=0),
        tokens,
    )
    if known:
        for held, ref in zip((offsets, removals, decays), known):
            held[0 : extra * REP] = ref[...]
    for b in range(count):
        keys_turned = works[b * REP][0].T
        for r in range(REP):
            at = b * REP + r
            _, cum_col, key_col, _, _ = works[at]
            last = cum_col[tokens - 1 : tokens, :]
            tail = key_col * jnp.exp(last - cum_col)
            tail = jnp.concatenate([tail, tail], axis=1)
            both = nn(keys_turned, (sides[at] * tail).astype(BF16))
            to, held = at if own else at + extra * REP, (offsets, removals, decays)
            if own and b >= blocks:
                to, held = at - blocks * REP, handed
            held[0][to] = both[:, :DV]
            held[1][to] = both[:, DV:].astype(BF16)
            held[2][to] = jnp.broadcast_to(jnp.exp(last), (PIECE_ROWS, DK))

    key_row, key_col = iotas((DK, DK))
    eye = (key_row == key_col).astype(F32)
    states = [None] * REP
    for i in range(blocks):
        following = []
        for r in range(REP):
            at = (low ^ i) * REP + r
            decay = decays[at][0:1, :]
            if i == 0:
                map_ref[at] = eye.astype(BF16)
                before_ref[at] = jnp.zeros((DK, DV), F32)
                following.append(
                    jnp.concatenate(
                        [eye * decay - removals[at].astype(F32), offsets[at]], axis=1
                    )
                )
                continue
            held = states[r].astype(BF16)
            map_ref[at] = held[:, :DK]
            before_ref[at] = states[r][:, DK:]
            moved = nn(removals[at], held)
            following.append(
                jnp.concatenate(
                    [
                        states[r][:, :DK] * decay - moved[:, :DK],
                        states[r][:, DK:] * decay - moved[:, DK:] + offsets[at],
                    ],
                    axis=1,
                )
            )
        states = following
    own_half = place // blocks
    for r in range(REP):
        end_map, end = states[r][:, :DK], states[r][:, DK:]
        end_map_ref[r] = end_map
        end_ref[r] = end
        if not own:
            first_end, second_end = in_order(own_half, own_end[r], end)
            first_map, second_map = in_order(own_half, own_map[r], end_map)
            second_map = second_map.astype(BF16)
            group_ref[r] = (nn(second_map, first_end.astype(BF16)) + second_end).astype(BF16)
            if with_map:
                group_map_ref[r] = nn(second_map, first_map.astype(BF16))


def carry_kernel(
    own_before, own_maps, own_end, own_map, other_before, other_maps, other_end, other_map,
    carried_ref, out_ref,
):
    group = out_ref.shape[0]
    half = group // 2
    place = place_in_group(group)
    own_half = place // half
    later_group = lax.axis_index("ctx") >= group
    starts = []
    for r in range(REP):
        carried = jnp.where(later_group, carried_ref[r].astype(F32), 0.0)
        first_end, _ = in_order(own_half, own_end[r], other_end[r])
        first_map, _ = in_order(own_half, own_map[r], other_map[r])
        middle = first_end + nn(first_map.astype(BF16), carried.astype(BF16))
        starts.append([x.astype(BF16) for x in in_order(own_half, carried, middle)])
    for s in range(group):
        before, maps = (own_before, own_maps) if s < half else (other_before, other_maps)
        for r in range(REP):
            at = (s % half) * REP + r
            start = starts[r][0] if s < half else starts[r][1]
            out_ref[place ^ s, r * DK : (r + 1) * DK, :] = (
                before[at] + nn(maps[at], start)
            ).astype(BF16)


def columns_of(width, target):
    return pl.ds(pl.multiple_of(target * width, width), width)


def mixed_kernel(
    state_ref, inside_ref, window_ref, gate_ref, gain_ref, weight_ref, mixed_ref, *out_refs, shifts
):
    me = lax.axis_index("head")
    gain = gain_ref[...]
    for j in range(state_ref.shape[0]):
        for r in range(REP):
            h = j * REP + r
            columns = pl.ds(h * DV, DV)
            state = state_ref[j, r * DK : (r + 1) * DK, :]
            rows = inside_ref[h].astype(F32) + nn(window_ref[h], state)
            scale = lax.rsqrt(jnp.mean(rows * rows, axis=1, keepdims=True) + EPSILON)
            gate = gate_ref[:, columns].astype(F32)
            mixed_ref[:, columns] = (
                rows * scale * gain * (gate / (1.0 + jnp.exp(-gate)))
            ).astype(BF16)
    for n, out_ref in enumerate(out_refs):
        columns = columns_of(out_ref.shape[1], lax.rem(me + 1 + n, shifts))
        out_ref[...] = nn(mixed_ref[...], weight_ref[:, columns]).astype(BF16)


def own_columns_kernel(mixed_ref, weight_ref, out_ref):
    columns = columns_of(out_ref.shape[1], lax.axis_index("head"))
    out_ref[...] = nn(mixed_ref[...], weight_ref[:, columns]).astype(BF16)


def local(
    query_proj, key_proj, value_proj, gate_proj, write_strength, log_decay, norm_gain, out_weight,
    *, n_ctx, n_head,
):
    tokens = query_proj.shape[0]
    heads = value_proj.shape[1] // DV
    group = query_proj.shape[1] // DK
    half = group // 2
    width = out_weight.shape[1] // n_head
    n_groups = n_ctx // group
    packed_rows = (1 + REP) * tokens + SMALL_ROWS
    mib = 1024 * 1024

    def kernel(body, out, name, limit, micros, scratch=(), specs=None, out_specs=None):
        return pl.pallas_call(
            body,
            out_shape=out,
            scratch_shapes=scratch,
            compiler_params=pltpu.CompilerParams(
                vmem_limit_bytes=None if limit is None else int(limit * mib)
            ),
            cost_estimate=pl.CostEstimate(
                flops=int(micros * 1e9), bytes_accessed=mib, transcendentals=0
            ),
            name=name,
            **({} if specs is None else {"in_specs": specs}),
            **({} if out_specs is None else {"out_specs": out_specs}),
        )

    def shape(dims, kind):
        return jax.ShapeDtypeStruct(dims, kind)

    def shifted(array, distance):
        return lax.ppermute(array, "ctx", [(i, i + distance) for i in range(n_ctx - distance)])

    def swapped(array, distance):
        return lax.ppermute(array, "ctx", [(i, i ^ distance) for i in range(n_ctx)])

    any_space = pl.BlockSpec(memory_space=pl.ANY)
    vmem = pl.BlockSpec(memory_space=pltpu.VMEM)
    *packed, rows = kernel(
        pack_kernel,
        (shape((packed_rows, DK), BF16),) * group + (shape((group * SMALL_ROWS, DK), BF16),),
        "pack",
        None,
        2,
        scratch=[
            pltpu.VMEM((group, packed_rows, DK), BF16),
            pltpu.VMEM((2, heads, tokens), F32),
            pltpu.VMEM((group * SMALL_ROWS, DK), BF16),
            pltpu.SemaphoreType.DMA((group + 1, 1 + REP)),
            pltpu.SemaphoreType.DMA((group + 1,)),
        ],
        specs=[any_space] * 4,
        out_specs=(any_space,) * (group + 1),
    )(key_proj, value_proj, write_strength.T, log_decay.T)
    taken = [packed[0]] + [swapped(packed[s], s) for s in range(1, group)]

    extra = 1 if half >= 4 else 0

    def half_states(blocks, more, name):
        own, with_map = not more, n_groups > 2
        passed = (
            shape((extra * REP, DK, DV), F32),
            shape((extra * REP, DK, DK), BF16),
            shape((extra * REP, PIECE_ROWS, DK), F32),
        )
        return kernel(
            functools.partial(
                half_kernel, blocks=half, extra=extra, group=group, tokens=tokens, own=own,
                with_map=with_map,
            ),
            (
                shape((half * REP, DK, DV), F32),
                shape((half * REP, DK, DK), BF16),
                shape((REP, DK, DV), F32),
                shape((REP, DK, DK), F32),
            )
            + (() if own else (shape((REP, DK, DV), BF16),))
            + ((shape((REP, DK, DK), F32),) if with_map and not own else ())
            + (passed if own and extra else ()),
            name,
            16,
            3.5,
            scratch=[
                pltpu.VMEM((half * REP, DK, DV), F32),
                pltpu.VMEM((half * REP, DK, DK), BF16),
                pltpu.VMEM((half * REP, PIECE_ROWS, DK), F32),
            ],
        )(*blocks, *more)

    own = half_states(taken[: half + extra], (), "own_half")
    later, own = lax.optimization_barrier((taken[half + extra :], own))
    *other, end = half_states(later, own[2:], "other_half")
    own = own[:4]

    if n_groups == 2:
        carried = swapped(end, group)
    elif n_groups > 2:
        carried, mapping = shifted(other[-1], group).astype(F32), shifted(end, group)
        other = other[:-1]
        distance = 1
        while distance < n_groups - 1:
            earlier, earlier_map = shifted(carried, distance * group), shifted(mapping, distance * group)
            carried = carried + jnp.einsum("rkl,rlv->rkv", mapping, earlier, precision="highest")
            mapping = jnp.einsum("rkl,rlv->rkv", mapping, earlier_map, precision="highest")
            distance *= 2
        carried = carried.astype(BF16)
    else:
        carried = jnp.zeros((REP, DK, DV), BF16)

    rows, end = lax.optimization_barrier((rows, end))
    inside, window = kernel(
        inside_kernel,
        (
            shape((heads, tokens, DV), BF16),
            shape((heads, tokens, DK), BF16),
        ),
        "inside",
        16,
        5,
    )(query_proj, key_proj, value_proj, rows)
    carried, inside, window = lax.optimization_barrier((carried, inside, window))
    states = kernel(
        carry_kernel, shape((group, REP * DK, DV), BF16), "carry", 8, 0.6
    )(*own, *other, carried)
    groups = [list(range(g, g + group)) for g in range(0, n_ctx, group)]
    state_in = lax.all_to_all(states, "ctx", 0, 0, axis_index_groups=groups, tiled=True)

    mixed, *others = kernel(
        functools.partial(mixed_kernel, shifts=n_head),
        (shape((tokens, heads * DV), BF16),) + (shape((tokens, width), BF16),) * (n_head - 1),
        "mixed",
        16,
        2,
    )(state_in, inside, window, gate_proj, norm_gain.reshape(1, DV), out_weight)
    received = [
        lax.ppermute(other, "head", [(i, (i + 1 + s) % n_head) for i in range(n_head)])
        for s, other in enumerate(others)
    ]
    total = kernel(own_columns_kernel, shape((tokens, width), BF16), "own_columns", 16, 1)(
        mixed, out_weight
    ).astype(F32)
    for other in received:
        total = total + other.astype(F32)
    return total.astype(BF16)


def solution(mesh):
    return jax.shard_map(
        functools.partial(local, n_ctx=mesh.shape["ctx"], n_head=mesh.shape["head"]),
        mesh=mesh,
        in_specs=(
            P("ctx", "head"),
            P("ctx", "head"),
            P("ctx", "head"),
            P("ctx", "head"),
            P("ctx", "head"),
            P("ctx", "head"),
            P(),
            P("head", None),
        ),
        out_specs=P("ctx", "head"),
        check_vma=False,
    )
```

```python
import functools

import jax
import jax.numpy as jnp
from jax import lax
from jax.experimental import pallas as pl
from jax.experimental.pallas import tpu as pltpu
from jax.sharding import PartitionSpec as P

HV = 32
HK = 16
DK = 128
DV = 128
REP = HV // HK
SMALL_BITS = 4
SMALL_ROWS = 1 << SMALL_BITS
PIECE_ROWS = 8
EPSILON = 1e-06
BF16 = jnp.bfloat16
F32 = jnp.float32


def nn(a, b):
    return lax.dot_general(a, b, (((1,), (0,)), ((), ())), preferred_element_type=F32)


def nt(a, b):
    return lax.dot_general(a, b, (((1,), (1,)), ((), ())), preferred_element_type=F32)


def two_pieces(x):
    high = x.astype(BF16)
    return high, (x - high.astype(F32)).astype(BF16)


def iotas(shape):
    return lax.broadcasted_iota(jnp.int32, shape, 0), lax.broadcasted_iota(jnp.int32, shape, 1)


def triangles(size):
    row, col = iotas((size, size))
    return row, col, (col <= row).astype(BF16), (row <= col).astype(BF16), (row == col).astype(BF16)


def solved(lowers, rights, size, base_bits):
    count, base = len(lowers), 1 << base_bits
    row, col = iotas((size, size))
    place, lane = iotas((base, size))
    packed = []
    for low in lowers:
        held = low[0:base]
        for b in range(1, size // base):
            held = jnp.where(lane >> base_bits == b, low[b * base : (b + 1) * base], held)
        packed.append(held)
    packed = jnp.concatenate(packed, axis=0).astype(BF16)
    found = [jnp.where(place == (lane & (base - 1)), 1.0, 0.0)] * count
    first_col = col & ~(base - 1)
    for k in range(base - 1):
        spread = jnp.where(row == first_col + k, 1.0, 0.0).astype(BF16)
        column = nn(packed, spread)
        found = [
            x - column[h * base : (h + 1) * base] * x[k : k + 1] for h, x in enumerate(found)
        ]
    rounded = [low.astype(BF16) for low in lowers]
    step, apart = base, row ^ col
    while True:
        pair = 2 * step
        below = jnp.where((apart >= step) & (apart < pair) & (col < row), 1.0, 0.0).astype(BF16)
        diagonal = jnp.where(apart < step, 1.0, 0.0)
        lane = lax.broadcasted_iota(jnp.int32, (step, size), 1)
        even = (lane & step) == 0
        first = [nn(x.astype(BF16), low * below).astype(BF16) for x, low in zip(found, rounded)]
        whole = [
            (jnp.concatenate([x] * (size // step), axis=0) * diagonal).astype(BF16) for x in found
        ]
        if pair == size:
            ends = [nn(w, right) for w, right in zip(whole, rights)]
            fixes = [nn(f, end.astype(BF16)) for f, end in zip(first, ends)]
            return [
                jnp.concatenate([end[:step], end[step:] - fix], axis=0)
                for end, fix in zip(ends, fixes)
            ]
        second = [nn(f, w) for f, w in zip(first, whole)]
        found = [
            jnp.concatenate([jnp.where(even, x, 0.0), jnp.where(even, -y, x)], axis=0)
            for x, y in zip(found, second)
        ]
        step = pair


def decay_gaps(cum_col, cum_row, row, col):
    return jnp.exp(jnp.where(col <= row, cum_col - cum_row, -1e30))


def inverse_norms(gram, row, col):
    diagonal = jnp.where(row == col, gram, 0.0)
    return (
        lax.rsqrt(jnp.sum(diagonal, axis=1, keepdims=True) + EPSILON),
        lax.rsqrt(jnp.sum(diagonal, axis=0, keepdims=True) + EPSILON),
    )


def place_in_group(group):
    return lax.rem(lax.axis_index("ctx"), group)


def pack_kernel(key_hbm, value_hbm, scalars_ref, *refs):
    group = len(refs) - 2
    out_refs, (rows_ref, in_sems) = refs[:group], refs[group:]
    tokens = key_hbm.shape[0]
    heads = scalars_ref.shape[1]
    place = place_in_group(group)
    base = (1 + REP) * tokens
    arrivals = []
    for s in range(group):
        j = place ^ s
        sources = [key_hbm.at[:, pl.ds(pl.multiple_of(j * DK, DK), DK)]] + [
            value_hbm.at[:, pl.ds(pl.multiple_of((j * REP + r) * DV, DV), DV)] for r in range(REP)
        ]
        arrivals.append(
            [
                pltpu.make_async_copy(
                    source, out_refs[s].at[pl.ds(n * tokens, tokens), :], in_sems.at[s, n]
                )
                for n, source in enumerate(sources)
            ]
        )
    for copy in sum(arrivals, []):
        copy.start()
    row, col = iotas((SMALL_ROWS * group, 4 * heads))
    slot, target = row & (SMALL_ROWS - 1), row >> SMALL_BITS

    def picked(target):
        pick = jnp.zeros(row.shape, F32)
        for kind in range(2):
            for piece in range(2):
                at = slot - piece * PIECE_ROWS - kind * REP
                wanted = (2 * kind + piece) * heads + target * REP + at
                pick = pick + jnp.where((at >= 0) & (at < REP) & (col == wanted), 1.0, 0.0)
        return pick.astype(BF16)

    picks = picked(target ^ place), picked(target)
    pieces = jnp.concatenate(
        two_pieces(scalars_ref[0]) + two_pieces(scalars_ref[1]), axis=0
    )
    sent, natural = [nn(pick, pieces).astype(BF16) for pick in picks]
    if tokens < DK:
        fill = jnp.zeros((sent.shape[0], DK - tokens), BF16)
        sent, natural = [jnp.concatenate([x, fill], axis=1) for x in (sent, natural)]
    rows_ref[...] = natural
    for s, out_ref in enumerate(out_refs):
        out_ref[base : base + SMALL_ROWS, :] = sent[s * SMALL_ROWS : (s + 1) * SMALL_ROWS, :]
        for copy in arrivals[s]:
            copy.wait()


def solved_blocks(blocks, small, tokens, base_bits):
    row, col, lower_ones, upper_ones, eye = triangles(tokens)
    small = small.astype(F32)
    pieces = [
        jnp.concatenate(
            [
                small[b * SMALL_ROWS + start : b * SMALL_ROWS + start + PIECE_ROWS]
                for b in range(len(blocks))
            ],
            axis=0,
        ).astype(BF16)
        for start in (0, PIECE_ROWS)
    ]
    cum_rows = sum(nn(p, upper_ones) for p in pieces)
    plain_cols = sum(nt(eye, p) for p in pieces)
    cum_cols = sum(nt(lower_ones, p) for p in pieces)

    def spread(array, at):
        return jnp.broadcast_to(array[:, at : at + 1], (tokens, DK))

    lowers, rights, works = [], [], []
    for b, (keys, values) in enumerate(blocks):
        gram = nt(keys, keys)
        key_col, key_row = inverse_norms(gram, row, col)
        key_col = jnp.broadcast_to(key_col, (tokens, DK))
        gram = gram * key_row * key_col[:, :tokens]
        unit_keys = keys.astype(F32) * key_col
        for r in range(REP):
            at = b * PIECE_ROWS + r
            strength = spread(plain_cols, at)
            cum_row, cum_col = cum_rows[at + REP : at + REP + 1, :], spread(cum_cols, at + REP)
            factors = decay_gaps(cum_col[:, :tokens], cum_row, row, col)
            lowers.append(jnp.where(col < row, strength[:, :tokens] * factors * gram, 0.0))
            rights.append(
                jnp.concatenate(
                    [
                        (strength * values[r].astype(F32)).astype(BF16),
                        (strength * jnp.exp(cum_col) * unit_keys).astype(BF16),
                    ],
                    axis=1,
                )
            )
            works.append((keys, cum_col, key_col, key_row, factors))
    return solved(lowers, rights, tokens, base_bits), works


def inside_kernel(query_ref, key_ref, value_ref, rows_ref, inside_ref, window_ref):
    tokens = query_ref.shape[0]
    blocks = inside_ref.shape[0] // REP

    def columns(ref, start, size):
        return ref[:, start * size : (start + 1) * size]

    sides, works = solved_blocks(
        [
            (
                columns(key_ref, j, DK),
                [columns(value_ref, j * REP + r, DV) for r in range(REP)],
            )
            for j in range(blocks)
        ],
        rows_ref[:, :tokens],
        tokens,
        3,
    )
    for b in range(blocks):
        queries = columns(query_ref, b, DK)
        products = nt(queries, works[b * REP][0])
        queries = queries.astype(F32)
        query_col = lax.rsqrt(
            jnp.sum(queries * queries, axis=1, keepdims=True) + EPSILON
        ) * DK**-0.5
        query_col = jnp.broadcast_to(query_col, (tokens, DK))
        queries = queries * query_col
        products = products * works[b * REP][3] * query_col[:, :tokens]
        for r in range(REP):
            at = b * REP + r
            _, cum_col, _, _, factors = works[at]
            scores = (products * factors).astype(BF16)
            both = nn(scores, sides[at].astype(BF16))
            inside_ref[at] = both[:, :DV].astype(BF16)
            window_ref[at] = (jnp.exp(cum_col) * queries - both[:, DV:]).astype(BF16)


def in_order(own_half, own, other):
    return jnp.where(own_half == 0, own, other), jnp.where(own_half == 0, other, own)


def half_kernel(*refs, blocks, extra, group, tokens, own, with_map):
    count = blocks + extra if own else blocks - extra
    taken, refs = refs[:count], refs[count:]
    if not own:
        (own_end, own_map), refs = refs[:2], refs[2:]
    known = ()
    if extra and not own:
        known, refs = refs[:3], refs[3:]
    before_ref, map_ref, end_ref, end_map_ref, *refs = refs
    if not own:
        group_ref, *refs = refs
        if with_map:
            group_map_ref, *refs = refs
    handed = ()
    if extra and own:
        handed, refs = refs[:3], refs[3:]
    offsets, removals, decays = refs
    place = place_in_group(group)
    low = lax.rem(place, blocks)
    base = (1 + REP) * tokens
    sides, works = solved_blocks(
        [
            (t[0:tokens, :], [t[(1 + r) * tokens : (2 + r) * tokens, :] for r in range(REP)])
            for t in taken
        ],
        jnp.concatenate([t[base : base + SMALL_ROWS, :][:, :tokens] for t in taken], axis=0),
        tokens,
        4,
    )
    if known:
        for held, ref in zip((offsets, removals, decays), known):
            held[0 : extra * REP] = ref[...]
    for b in range(count):
        keys_turned = works[b * REP][0].T
        for r in range(REP):
            at = b * REP + r
            _, cum_col, key_col, _, _ = works[at]
            last = cum_col[tokens - 1 : tokens, :]
            tail = key_col * jnp.exp(last - cum_col)
            tail = jnp.concatenate([tail, tail], axis=1)
            both = nn(keys_turned, (sides[at] * tail).astype(BF16))
            to, held = at if own else at + extra * REP, (offsets, removals, decays)
            if own and b >= blocks:
                to, held = at - blocks * REP, handed
            held[0][to] = both[:, :DV]
            held[1][to] = both[:, DV:].astype(BF16)
            held[2][to] = jnp.broadcast_to(jnp.exp(last), (PIECE_ROWS, DK))

    key_row, key_col = iotas((DK, DK))
    eye = (key_row == key_col).astype(F32)
    states = [None] * REP
    for i in range(blocks):
        following = []
        for r in range(REP):
            at = (low ^ i) * REP + r
            decay = decays[at][0:1, :]
            if i == 0:
                map_ref[at] = eye.astype(BF16)
                before_ref[at] = jnp.zeros((DK, DV), F32)
                following.append(
                    jnp.concatenate(
                        [eye * decay - removals[at].astype(F32), offsets[at]], axis=1
                    )
                )
                continue
            held = states[r].astype(BF16)
            map_ref[at] = held[:, :DK]
            before_ref[at] = states[r][:, DK:]
            moved = nn(removals[at], held)
            following.append(
                jnp.concatenate(
                    [
                        states[r][:, :DK] * decay - moved[:, :DK],
                        states[r][:, DK:] * decay - moved[:, DK:] + offsets[at],
                    ],
                    axis=1,
                )
            )
        states = following
    own_half = place // blocks
    for r in range(REP):
        end_map, end = states[r][:, :DK], states[r][:, DK:]
        end_map_ref[r] = end_map
        end_ref[r] = end
        if not own:
            first_end, second_end = in_order(own_half, own_end[r], end)
            first_map, second_map = in_order(own_half, own_map[r], end_map)
            second_map = second_map.astype(BF16)
            group_ref[r] = (nn(second_map, first_end.astype(BF16)) + second_end).astype(BF16)
            if with_map:
                group_map_ref[r] = nn(second_map, first_map.astype(BF16))


def carry_kernel(
    own_before, own_maps, own_end, own_map, other_before, other_maps, other_end, other_map,
    carried_ref, out_ref,
):
    group = out_ref.shape[0]
    half = group // 2
    place = place_in_group(group)
    own_half = place // half
    later_group = lax.axis_index("ctx") >= group
    starts = []
    for r in range(REP):
        carried = jnp.where(later_group, carried_ref[r].astype(F32), 0.0)
        first_end, _ = in_order(own_half, own_end[r], other_end[r])
        first_map, _ = in_order(own_half, own_map[r], other_map[r])
        middle = first_end + nn(first_map.astype(BF16), carried.astype(BF16))
        starts.append([x.astype(BF16) for x in in_order(own_half, carried, middle)])
    for s in range(group):
        before, maps = (own_before, own_maps) if s < half else (other_before, other_maps)
        for r in range(REP):
            at = (s % half) * REP + r
            start = starts[r][0] if s < half else starts[r][1]
            out_ref[place ^ s, r * DK : (r + 1) * DK, :] = (
                before[at] + nn(maps[at], start)
            ).astype(BF16)


def columns_of(width, target):
    return pl.ds(pl.multiple_of(target * width, width), width)


def mixed_kernel(
    state_ref, inside_ref, window_ref, gate_ref, gain_ref, weight_ref, mixed_ref, *out_refs, shifts
):
    me = lax.axis_index("head")
    gain = gain_ref[...]
    for j in range(state_ref.shape[0]):
        for r in range(REP):
            h = j * REP + r
            columns = pl.ds(h * DV, DV)
            state = state_ref[j, r * DK : (r + 1) * DK, :]
            rows = inside_ref[h].astype(F32) + nn(window_ref[h], state)
            scale = lax.rsqrt(jnp.mean(rows * rows, axis=1, keepdims=True) + EPSILON)
            gate = gate_ref[:, columns].astype(F32)
            mixed_ref[:, columns] = (
                rows * scale * gain * (gate / (1.0 + jnp.exp(-gate)))
            ).astype(BF16)
    for n, out_ref in enumerate(out_refs):
        columns = columns_of(out_ref.shape[1], lax.rem(me + 1 + n, shifts))
        out_ref[...] = nn(mixed_ref[...], weight_ref[:, columns]).astype(BF16)


def own_columns_kernel(mixed_ref, weight_ref, out_ref):
    columns = columns_of(out_ref.shape[1], lax.axis_index("head"))
    out_ref[...] = nn(mixed_ref[...], weight_ref[:, columns]).astype(BF16)


def local(
    query_proj, key_proj, value_proj, gate_proj, write_strength, log_decay, norm_gain, out_weight,
    *, n_ctx, n_head,
):
    tokens = query_proj.shape[0]
    heads = value_proj.shape[1] // DV
    group = query_proj.shape[1] // DK
    half = group // 2
    width = out_weight.shape[1] // n_head
    n_groups = n_ctx // group
    packed_rows = (1 + REP) * tokens + SMALL_ROWS
    mib = 1024 * 1024

    def kernel(body, out, name, limit, micros, scratch=(), specs=None, out_specs=None):
        return pl.pallas_call(
            body,
            out_shape=out,
            scratch_shapes=scratch,
            compiler_params=pltpu.CompilerParams(
                vmem_limit_bytes=None if limit is None else int(limit * mib)
            ),
            cost_estimate=pl.CostEstimate(
                flops=int(micros * 1e9), bytes_accessed=mib, transcendentals=0
            ),
            name=name,
            **({} if specs is None else {"in_specs": specs}),
            **({} if out_specs is None else {"out_specs": out_specs}),
        )

    def shape(dims, kind):
        return jax.ShapeDtypeStruct(dims, kind)

    def shifted(array, distance):
        return lax.ppermute(array, "ctx", [(i, i + distance) for i in range(n_ctx - distance)])

    def swapped(array, distance):
        return lax.ppermute(array, "ctx", [(i, i ^ distance) for i in range(n_ctx)])

    any_space = pl.BlockSpec(memory_space=pl.ANY)
    vmem = pl.BlockSpec(memory_space=pltpu.VMEM)
    *packed, rows = kernel(
        pack_kernel,
        (shape((packed_rows, DK), BF16),) * group + (shape((group * SMALL_ROWS, DK), BF16),),
        "pack",
        53,
        2,
        scratch=[pltpu.SemaphoreType.DMA((group, 1 + REP))],
        specs=[any_space, any_space, vmem],
    )(key_proj, value_proj, jnp.stack([write_strength.T, log_decay.T]))
    taken = [packed[0]] + [swapped(packed[s], s) for s in range(1, group)]

    extra = 1 if half >= 4 else 0

    def half_states(blocks, more, name):
        own, with_map = not more, n_groups > 2
        passed = (
            shape((extra * REP, DK, DV), F32),
            shape((extra * REP, DK, DK), BF16),
            shape((extra * REP, PIECE_ROWS, DK), F32),
        )
        return kernel(
            functools.partial(
                half_kernel, blocks=half, extra=extra, group=group, tokens=tokens, own=own,
                with_map=with_map,
            ),
            (
                shape((half * REP, DK, DV), F32),
                shape((half * REP, DK, DK), BF16),
                shape((REP, DK, DV), F32),
                shape((REP, DK, DK), F32),
            )
            + (() if own else (shape((REP, DK, DV), BF16),))
            + ((shape((REP, DK, DK), F32),) if with_map and not own else ())
            + (passed if own and extra else ()),
            name,
            16,
            3.5,
            scratch=[
                pltpu.VMEM((half * REP, DK, DV), F32),
                pltpu.VMEM((half * REP, DK, DK), BF16),
                pltpu.VMEM((half * REP, PIECE_ROWS, DK), F32),
            ],
        )(*blocks, *more)

    own = half_states(taken[: half + extra], (), "own_half")
    later, own = lax.optimization_barrier((taken[half + extra :], own))
    *other, end = half_states(later, own[2:], "other_half")
    own = own[:4]

    if n_groups == 2:
        carried = swapped(end, group)
    elif n_groups > 2:
        carried, mapping = shifted(other[-1], group).astype(F32), shifted(end, group)
        other = other[:-1]
        distance = 1
        while distance < n_groups - 1:
            earlier, earlier_map = shifted(carried, distance * group), shifted(mapping, distance * group)
            carried = carried + jnp.einsum("rkl,rlv->rkv", mapping, earlier, precision="highest")
            mapping = jnp.einsum("rkl,rlv->rkv", mapping, earlier_map, precision="highest")
            distance *= 2
        carried = carried.astype(BF16)
    else:
        carried = jnp.zeros((REP, DK, DV), BF16)

    rows, end = lax.optimization_barrier((rows, end))
    inside, window = kernel(
        inside_kernel,
        (
            shape((heads, tokens, DV), BF16),
            shape((heads, tokens, DK), BF16),
        ),
        "inside",
        16,
        5,
    )(query_proj, key_proj, value_proj, rows)
    carried, inside, window = lax.optimization_barrier((carried, inside, window))
    states = kernel(
        carry_kernel, shape((group, REP * DK, DV), BF16), "carry", 8, 0.6
    )(*own, *other, carried)
    groups = [list(range(g, g + group)) for g in range(0, n_ctx, group)]
    state_in = lax.all_to_all(states, "ctx", 0, 0, axis_index_groups=groups, tiled=True)

    mixed, *others = kernel(
        functools.partial(mixed_kernel, shifts=n_head),
        (shape((tokens, heads * DV), BF16),) + (shape((tokens, width), BF16),) * (n_head - 1),
        "mixed",
        16,
        2,
    )(state_in, inside, window, gate_proj, norm_gain.reshape(1, DV), out_weight)
    received = [
        lax.ppermute(other, "head", [(i, (i + 1 + s) % n_head) for i in range(n_head)])
        for s, other in enumerate(others)
    ]
    total = kernel(own_columns_kernel, shape((tokens, width), BF16), "own_columns", 16, 1)(
        mixed, out_weight
    ).astype(F32)
    for other in received:
        total = total + other.astype(F32)
    return total.astype(BF16)


def solution(mesh):
    return jax.shard_map(
        functools.partial(local, n_ctx=mesh.shape["ctx"], n_head=mesh.shape["head"]),
        mesh=mesh,
        in_specs=(
            P("ctx", "head"),
            P("ctx", "head"),
            P("ctx", "head"),
            P("ctx", "head"),
            P("ctx", "head"),
            P("ctx", "head"),
            P(),
            P("head", None),
        ),
        out_specs=P("ctx", "head"),
        check_vma=False,
    )
```

```python
import functools

import jax
import jax.numpy as jnp
from jax import lax
from jax.experimental import pallas as pl
from jax.experimental.pallas import tpu as pltpu
from jax.sharding import PartitionSpec as P

HV = 32
HK = 16
DK = 128
DV = 128
REP = HV // HK
SMALL_BITS = 4
SMALL_ROWS = 1 << SMALL_BITS
PIECE_ROWS = 8
EPSILON = 1e-06
BF16 = jnp.bfloat16
F32 = jnp.float32


def nn(a, b):
    return lax.dot_general(a, b, (((1,), (0,)), ((), ())), preferred_element_type=F32)


def nt(a, b):
    return lax.dot_general(a, b, (((1,), (1,)), ((), ())), preferred_element_type=F32)


def two_pieces(x):
    high = x.astype(BF16)
    return high, (x - high.astype(F32)).astype(BF16)


def iotas(shape):
    return lax.broadcasted_iota(jnp.int32, shape, 0), lax.broadcasted_iota(jnp.int32, shape, 1)


def triangles(size):
    row, col = iotas((size, size))
    return row, col, (col <= row).astype(BF16), (row <= col).astype(BF16), (row == col).astype(BF16)


def solved(lowers, rights, size, base_bits):
    count, base = len(lowers), 1 << base_bits
    row, col = iotas((size, size))
    place, lane = iotas((base, size))
    packed = []
    for low in lowers:
        held = low[0:base]
        for b in range(1, size // base):
            held = jnp.where(lane >> base_bits == b, low[b * base : (b + 1) * base], held)
        packed.append(held)
    packed = jnp.concatenate(packed, axis=0).astype(BF16)
    found = [jnp.where(place == (lane & (base - 1)), 1.0, 0.0)] * count
    first_col = col & ~(base - 1)
    for k in range(base - 1):
        spread = jnp.where(row == first_col + k, 1.0, 0.0).astype(BF16)
        column = nn(packed, spread)
        found = [
            x - column[h * base : (h + 1) * base] * x[k : k + 1] for h, x in enumerate(found)
        ]
    rounded = [low.astype(BF16) for low in lowers]
    step, apart = base, row ^ col
    while True:
        pair = 2 * step
        below = jnp.where((apart >= step) & (apart < pair) & (col < row), 1.0, 0.0).astype(BF16)
        diagonal = jnp.where(apart < step, 1.0, 0.0)
        lane = lax.broadcasted_iota(jnp.int32, (step, size), 1)
        even = (lane & step) == 0
        first = [nn(x.astype(BF16), low * below).astype(BF16) for x, low in zip(found, rounded)]
        whole = [
            (jnp.concatenate([x] * (size // step), axis=0) * diagonal).astype(BF16) for x in found
        ]
        if pair == size:
            ends = [nn(w, right) for w, right in zip(whole, rights)]
            fixes = [nn(f, end.astype(BF16)) for f, end in zip(first, ends)]
            return [
                jnp.concatenate([end[:step], end[step:] - fix], axis=0)
                for end, fix in zip(ends, fixes)
            ]
        second = [nn(f, w) for f, w in zip(first, whole)]
        found = [
            jnp.concatenate([jnp.where(even, x, 0.0), jnp.where(even, -y, x)], axis=0)
            for x, y in zip(found, second)
        ]
        step = pair


def decay_gaps(cum_col, cum_row, row, col):
    return jnp.exp(jnp.where(col <= row, cum_col - cum_row, -1e30))


def inverse_norms(gram, row, col):
    diagonal = jnp.where(row == col, gram, 0.0)
    return (
        lax.rsqrt(jnp.sum(diagonal, axis=1, keepdims=True) + EPSILON),
        lax.rsqrt(jnp.sum(diagonal, axis=0, keepdims=True) + EPSILON),
    )


def place_in_group(group):
    return lax.rem(lax.axis_index("ctx"), group)


def pack_kernel(key_hbm, value_hbm, scalars_ref, *refs):
    group = len(refs) - 2
    out_refs, (rows_ref, in_sems) = refs[:group], refs[group:]
    tokens = key_hbm.shape[0]
    heads = scalars_ref.shape[1]
    place = place_in_group(group)
    base = (1 + REP) * tokens
    arrivals = []
    for s in range(group):
        j = place ^ s
        sources = [key_hbm.at[:, pl.ds(pl.multiple_of(j * DK, DK), DK)]] + [
            value_hbm.at[:, pl.ds(pl.multiple_of((j * REP + r) * DV, DV), DV)] for r in range(REP)
        ]
        arrivals.append(
            [
                pltpu.make_async_copy(
                    source, out_refs[s].at[pl.ds(n * tokens, tokens), :], in_sems.at[s, n]
                )
                for n, source in enumerate(sources)
            ]
        )
    for copy in sum(arrivals, []):
        copy.start()
    row, col = iotas((SMALL_ROWS * group, 4 * heads))
    slot, target = row & (SMALL_ROWS - 1), row >> SMALL_BITS

    def picked(target):
        pick = jnp.zeros(row.shape, F32)
        for kind in range(2):
            for piece in range(2):
                at = slot - piece * PIECE_ROWS - kind * REP
                wanted = (2 * kind + piece) * heads + target * REP + at
                pick = pick + jnp.where((at >= 0) & (at < REP) & (col == wanted), 1.0, 0.0)
        return pick.astype(BF16)

    picks = picked(target ^ place), picked(target)
    pieces = jnp.concatenate(
        two_pieces(scalars_ref[0]) + two_pieces(scalars_ref[1]), axis=0
    )
    sent, natural = [nn(pick, pieces).astype(BF16) for pick in picks]
    if tokens < DK:
        fill = jnp.zeros((sent.shape[0], DK - tokens), BF16)
        sent, natural = [jnp.concatenate([x, fill], axis=1) for x in (sent, natural)]
    rows_ref[...] = natural
    for s, out_ref in enumerate(out_refs):
        out_ref[base : base + SMALL_ROWS, :] = sent[s * SMALL_ROWS : (s + 1) * SMALL_ROWS, :]
        for copy in arrivals[s]:
            copy.wait()


def solved_blocks(blocks, small, tokens, base_bits):
    row, col, lower_ones, upper_ones, eye = triangles(tokens)
    small = small.astype(F32)
    pieces = [
        jnp.concatenate(
            [
                small[b * SMALL_ROWS + start : b * SMALL_ROWS + start + PIECE_ROWS]
                for b in range(len(blocks))
            ],
            axis=0,
        ).astype(BF16)
        for start in (0, PIECE_ROWS)
    ]
    cum_rows = sum(nn(p, upper_ones) for p in pieces)
    plain_cols = sum(nt(eye, p) for p in pieces)
    cum_cols = sum(nt(lower_ones, p) for p in pieces)

    def spread(array, at):
        return jnp.broadcast_to(array[:, at : at + 1], (tokens, DK))

    lowers, rights, works = [], [], []
    for b, (keys, values) in enumerate(blocks):
        gram = nt(keys, keys)
        key_col, key_row = inverse_norms(gram, row, col)
        key_col = jnp.broadcast_to(key_col, (tokens, DK))
        gram = gram * key_row * key_col[:, :tokens]
        unit_keys = keys.astype(F32) * key_col
        for r in range(REP):
            at = b * PIECE_ROWS + r
            strength = spread(plain_cols, at)
            cum_row, cum_col = cum_rows[at + REP : at + REP + 1, :], spread(cum_cols, at + REP)
            factors = decay_gaps(cum_col[:, :tokens], cum_row, row, col)
            lowers.append(jnp.where(col < row, strength[:, :tokens] * factors * gram, 0.0))
            rights.append(
                jnp.concatenate(
                    [
                        (strength * values[r].astype(F32)).astype(BF16),
                        (strength * jnp.exp(cum_col) * unit_keys).astype(BF16),
                    ],
                    axis=1,
                )
            )
            works.append((keys, cum_col, key_col, key_row, factors))
    return solved(lowers, rights, tokens, base_bits), works


def inside_kernel(
    query_ref, key_ref, value_ref, rows_ref, inside_ref, window_ref, *, first, base_bits
):
    tokens = query_ref.shape[0]
    blocks = inside_ref.shape[0] // REP

    def columns(ref, start, size):
        return ref[:, start * size : (start + 1) * size]

    sides, works = solved_blocks(
        [
            (
                columns(key_ref, j, DK),
                [columns(value_ref, j * REP + r, DV) for r in range(REP)],
            )
            for j in range(first, first + blocks)
        ],
        rows_ref[first * SMALL_ROWS : (first + blocks) * SMALL_ROWS, :][:, :tokens],
        tokens,
        base_bits,
    )
    for b in range(blocks):
        queries = columns(query_ref, first + b, DK)
        products = nt(queries, works[b * REP][0])
        queries = queries.astype(F32)
        query_col = lax.rsqrt(
            jnp.sum(queries * queries, axis=1, keepdims=True) + EPSILON
        ) * DK**-0.5
        query_col = jnp.broadcast_to(query_col, (tokens, DK))
        queries = queries * query_col
        products = products * works[b * REP][3] * query_col[:, :tokens]
        for r in range(REP):
            at = b * REP + r
            _, cum_col, _, _, factors = works[at]
            scores = (products * factors).astype(BF16)
            both = nn(scores, sides[at].astype(BF16))
            inside_ref[at] = both[:, :DV].astype(BF16)
            window_ref[at] = (jnp.exp(cum_col) * queries - both[:, DV:]).astype(BF16)


def in_order(own_half, own, other):
    return jnp.where(own_half == 0, own, other), jnp.where(own_half == 0, other, own)


def half_kernel(*refs, blocks, extra, group, tokens, own, with_map):
    count = blocks + extra if own else blocks - extra
    taken, refs = refs[:count], refs[count:]
    if not own:
        (own_end, own_map), refs = refs[:2], refs[2:]
    known = ()
    if extra and not own:
        known, refs = refs[:3], refs[3:]
    before_ref, map_ref, end_ref, end_map_ref, *refs = refs
    if not own:
        group_ref, *refs = refs
        if with_map:
            group_map_ref, *refs = refs
    handed = ()
    if extra and own:
        handed, refs = refs[:3], refs[3:]
    offsets, removals, decays = refs
    place = place_in_group(group)
    low = lax.rem(place, blocks)
    base = (1 + REP) * tokens
    sides, works = solved_blocks(
        [
            (t[0:tokens, :], [t[(1 + r) * tokens : (2 + r) * tokens, :] for r in range(REP)])
            for t in taken
        ],
        jnp.concatenate([t[base : base + SMALL_ROWS, :][:, :tokens] for t in taken], axis=0),
        tokens,
        4,
    )
    if known:
        for held, ref in zip((offsets, removals, decays), known):
            held[0 : extra * REP] = ref[...]
    for b in range(count):
        keys_turned = works[b * REP][0].T
        for r in range(REP):
            at = b * REP + r
            _, cum_col, key_col, _, _ = works[at]
            last = cum_col[tokens - 1 : tokens, :]
            tail = key_col * jnp.exp(last - cum_col)
            tail = jnp.concatenate([tail, tail], axis=1)
            both = nn(keys_turned, (sides[at] * tail).astype(BF16))
            to, held = at if own else at + extra * REP, (offsets, removals, decays)
            if own and b >= blocks:
                to, held = at - blocks * REP, handed
            held[0][to] = both[:, :DV]
            held[1][to] = both[:, DV:].astype(BF16)
            held[2][to] = jnp.broadcast_to(jnp.exp(last), (PIECE_ROWS, DK))

    key_row, key_col = iotas((DK, DK))
    eye = (key_row == key_col).astype(F32)
    states = [None] * REP
    for i in range(blocks):
        following = []
        for r in range(REP):
            at = (low ^ i) * REP + r
            decay = decays[at][0:1, :]
            if i == 0:
                map_ref[at] = eye.astype(BF16)
                before_ref[at] = jnp.zeros((DK, DV), F32)
                following.append(
                    jnp.concatenate(
                        [eye * decay - removals[at].astype(F32), offsets[at]], axis=1
                    )
                )
                continue
            held = states[r].astype(BF16)
            map_ref[at] = held[:, :DK]
            before_ref[at] = states[r][:, DK:]
            moved = nn(removals[at], held)
            following.append(
                jnp.concatenate(
                    [
                        states[r][:, :DK] * decay - moved[:, :DK],
                        states[r][:, DK:] * decay - moved[:, DK:] + offsets[at],
                    ],
                    axis=1,
                )
            )
        states = following
    own_half = place // blocks
    for r in range(REP):
        end_map, end = states[r][:, :DK], states[r][:, DK:]
        end_map_ref[r] = end_map
        end_ref[r] = end
        if not own:
            first_end, second_end = in_order(own_half, own_end[r], end)
            first_map, second_map = in_order(own_half, own_map[r], end_map)
            second_map = second_map.astype(BF16)
            group_ref[r] = (nn(second_map, first_end.astype(BF16)) + second_end).astype(BF16)
            if with_map:
                group_map_ref[r] = nn(second_map, first_map.astype(BF16))


def carry_kernel(
    own_before, own_maps, own_end, own_map, other_before, other_maps, other_end, other_map,
    carried_ref, out_ref,
):
    group = out_ref.shape[0]
    half = group // 2
    place = place_in_group(group)
    own_half = place // half
    later_group = lax.axis_index("ctx") >= group
    starts = []
    for r in range(REP):
        carried = jnp.where(later_group, carried_ref[r].astype(F32), 0.0)
        first_end, _ = in_order(own_half, own_end[r], other_end[r])
        first_map, _ = in_order(own_half, own_map[r], other_map[r])
        middle = first_end + nn(first_map.astype(BF16), carried.astype(BF16))
        starts.append([x.astype(BF16) for x in in_order(own_half, carried, middle)])
    for s in range(group):
        before, maps = (own_before, own_maps) if s < half else (other_before, other_maps)
        for r in range(REP):
            at = (s % half) * REP + r
            start = starts[r][0] if s < half else starts[r][1]
            out_ref[place ^ s, r * DK : (r + 1) * DK, :] = (
                before[at] + nn(maps[at], start)
            ).astype(BF16)


def columns_of(width, target):
    return pl.ds(pl.multiple_of(target * width, width), width)


def mixed_kernel(
    state_ref, first_inside, first_window, second_inside, second_window, gate_ref, gain_ref,
    weight_ref, mixed_ref, *out_refs, shifts,
):
    me = lax.axis_index("head")
    gain, split = gain_ref[...], first_inside.shape[0]
    for j in range(state_ref.shape[0]):
        for r in range(REP):
            h = j * REP + r
            columns = pl.ds(h * DV, DV)
            state = state_ref[j, r * DK : (r + 1) * DK, :]
            inside, window, at = (
                (first_inside, first_window, h) if h < split
                else (second_inside, second_window, h - split)
            )
            rows = inside[at].astype(F32) + nn(window[at], state)
            scale = lax.rsqrt(jnp.mean(rows * rows, axis=1, keepdims=True) + EPSILON)
            gate = gate_ref[:, columns].astype(F32)
            mixed_ref[:, columns] = (
                rows * scale * gain * (gate / (1.0 + jnp.exp(-gate)))
            ).astype(BF16)
    for n, out_ref in enumerate(out_refs):
        columns = columns_of(out_ref.shape[1], lax.rem(me + 1 + n, shifts))
        out_ref[...] = nn(mixed_ref[...], weight_ref[:, columns]).astype(BF16)


def own_columns_kernel(mixed_ref, weight_ref, out_ref):
    columns = columns_of(out_ref.shape[1], lax.axis_index("head"))
    out_ref[...] = nn(mixed_ref[...], weight_ref[:, columns]).astype(BF16)


def local(
    query_proj, key_proj, value_proj, gate_proj, write_strength, log_decay, norm_gain, out_weight,
    *, n_ctx, n_head,
):
    tokens = query_proj.shape[0]
    heads = value_proj.shape[1] // DV
    group = query_proj.shape[1] // DK
    half = group // 2
    width = out_weight.shape[1] // n_head
    n_groups = n_ctx // group
    packed_rows = (1 + REP) * tokens + SMALL_ROWS
    mib = 1024 * 1024

    def kernel(body, out, name, limit, micros, scratch=(), specs=None, out_specs=None):
        return pl.pallas_call(
            body,
            out_shape=out,
            scratch_shapes=scratch,
            compiler_params=pltpu.CompilerParams(
                vmem_limit_bytes=None if limit is None else int(limit * mib)
            ),
            cost_estimate=pl.CostEstimate(
                flops=int(micros * 1e9), bytes_accessed=mib, transcendentals=0
            ),
            name=name,
            **({} if specs is None else {"in_specs": specs}),
            **({} if out_specs is None else {"out_specs": out_specs}),
        )

    def shape(dims, kind):
        return jax.ShapeDtypeStruct(dims, kind)

    def shifted(array, distance):
        return lax.ppermute(array, "ctx", [(i, i + distance) for i in range(n_ctx - distance)])

    def swapped(array, distance):
        return lax.ppermute(array, "ctx", [(i, i ^ distance) for i in range(n_ctx)])

    any_space = pl.BlockSpec(memory_space=pl.ANY)
    vmem = pl.BlockSpec(memory_space=pltpu.VMEM)
    *packed, rows = kernel(
        pack_kernel,
        (shape((packed_rows, DK), BF16),) * group + (shape((group * SMALL_ROWS, DK), BF16),),
        "pack",
        53,
        2,
        scratch=[pltpu.SemaphoreType.DMA((group, 1 + REP))],
        specs=[any_space, any_space, vmem],
    )(key_proj, value_proj, jnp.stack([write_strength.T, log_decay.T]))
    taken = [packed[0]] + [swapped(packed[s], s) for s in range(1, group)]

    extra = 1 if half >= 4 else 0

    def half_states(blocks, more, name):
        own, with_map = not more, n_groups > 2
        passed = (
            shape((extra * REP, DK, DV), F32),
            shape((extra * REP, DK, DK), BF16),
            shape((extra * REP, PIECE_ROWS, DK), F32),
        )
        return kernel(
            functools.partial(
                half_kernel, blocks=half, extra=extra, group=group, tokens=tokens, own=own,
                with_map=with_map,
            ),
            (
                shape((half * REP, DK, DV), F32),
                shape((half * REP, DK, DK), BF16),
                shape((REP, DK, DV), F32),
                shape((REP, DK, DK), F32),
            )
            + (() if own else (shape((REP, DK, DV), BF16),))
            + ((shape((REP, DK, DK), F32),) if with_map and not own else ())
            + (passed if own and extra else ()),
            name,
            16,
            3.5,
            scratch=[
                pltpu.VMEM((half * REP, DK, DV), F32),
                pltpu.VMEM((half * REP, DK, DK), BF16),
                pltpu.VMEM((half * REP, PIECE_ROWS, DK), F32),
            ],
        )(*blocks, *more)

    own = half_states(taken[: half + extra], (), "own_half")
    def inside_part(start, count, rows, micros, base_bits):
        return kernel(
            functools.partial(inside_kernel, first=start, base_bits=base_bits),
            (
                shape((count * REP, tokens, DV), BF16),
                shape((count * REP, tokens, DK), BF16),
            ),
            "inside",
            16,
            micros,
        )(query_proj, key_proj, value_proj, rows)

    early = max(1, group // 4)
    rows, own = lax.optimization_barrier((rows, own))
    first = inside_part(0, early, rows, 2.3, 4)
    later, own, first = lax.optimization_barrier((taken[half + extra :], own, first))
    *other, end = half_states(later, own[2:], "other_half")
    own = own[:4]

    if n_groups == 2:
        carried = swapped(end, group)
    elif n_groups > 2:
        carried, mapping = shifted(other[-1], group).astype(F32), shifted(end, group)
        other = other[:-1]
        distance = 1
        while distance < n_groups - 1:
            earlier, earlier_map = shifted(carried, distance * group), shifted(mapping, distance * group)
            carried = carried + jnp.einsum("rkl,rlv->rkv", mapping, earlier, precision="highest")
            mapping = jnp.einsum("rkl,rlv->rkv", mapping, earlier_map, precision="highest")
            distance *= 2
        carried = carried.astype(BF16)
    else:
        carried = jnp.zeros((REP, DK, DV), BF16)

    rows, end = lax.optimization_barrier((rows, end))
    second = inside_part(early, group - early, rows, 5, 3)
    carried, second = lax.optimization_barrier((carried, second))
    states = kernel(
        carry_kernel, shape((group, REP * DK, DV), BF16), "carry", 8, 0.6
    )(*own, *other, carried)
    groups = [list(range(g, g + group)) for g in range(0, n_ctx, group)]
    state_in = lax.all_to_all(states, "ctx", 0, 0, axis_index_groups=groups, tiled=True)

    mixed, *others = kernel(
        functools.partial(mixed_kernel, shifts=n_head),
        (shape((tokens, heads * DV), BF16),) + (shape((tokens, width), BF16),) * (n_head - 1),
        "mixed",
        16,
        2,
    )(state_in, *first, *second, gate_proj, norm_gain.reshape(1, DV), out_weight)
    received = [
        lax.ppermute(other, "head", [(i, (i + 1 + s) % n_head) for i in range(n_head)])
        for s, other in enumerate(others)
    ]
    total = kernel(own_columns_kernel, shape((tokens, width), BF16), "own_columns", 16, 1)(
        mixed, out_weight
    ).astype(F32)
    for other in received:
        total = total + other.astype(F32)
    return total.astype(BF16)


def solution(mesh):
    return jax.shard_map(
        functools.partial(local, n_ctx=mesh.shape["ctx"], n_head=mesh.shape["head"]),
        mesh=mesh,
        in_specs=(
            P("ctx", "head"),
            P("ctx", "head"),
            P("ctx", "head"),
            P("ctx", "head"),
            P("ctx", "head"),
            P("ctx", "head"),
            P(),
            P("head", None),
        ),
        out_specs=P("ctx", "head"),
        check_vma=False,
    )
```

```python
import functools

import jax
import jax.numpy as jnp
from jax import lax
from jax.experimental import pallas as pl
from jax.experimental.pallas import tpu as pltpu
from jax.sharding import PartitionSpec as P

HV = 32
HK = 16
DK = 128
DV = 128
REP = HV // HK
SMALL_BITS = 4
SMALL_ROWS = 1 << SMALL_BITS
PIECE_ROWS = 8
EPSILON = 1e-06
BF16 = jnp.bfloat16
F32 = jnp.float32


def nn(a, b):
    return lax.dot_general(a, b, (((1,), (0,)), ((), ())), preferred_element_type=F32)


def nt(a, b):
    return lax.dot_general(a, b, (((1,), (1,)), ((), ())), preferred_element_type=F32)


def two_pieces(x):
    high = x.astype(BF16)
    return high, (x - high.astype(F32)).astype(BF16)


def iotas(shape):
    return lax.broadcasted_iota(jnp.int32, shape, 0), lax.broadcasted_iota(jnp.int32, shape, 1)


def triangles(size):
    row, col = iotas((size, size))
    return row, col, (col <= row).astype(BF16), (row <= col).astype(BF16), (row == col).astype(BF16)


def solved(lowers, rights, size, base_bits):
    count, base = len(lowers), 1 << base_bits
    row, col = iotas((size, size))
    place, lane = iotas((base, size))
    packed = []
    for low in lowers:
        held = low[0:base]
        for b in range(1, size // base):
            held = jnp.where(lane >> base_bits == b, low[b * base : (b + 1) * base], held)
        packed.append(held)
    packed = jnp.concatenate(packed, axis=0).astype(BF16)
    found = [jnp.where(place == (lane & (base - 1)), 1.0, 0.0)] * count
    first_col = col & ~(base - 1)
    for k in range(base - 1):
        spread = jnp.where(row == first_col + k, 1.0, 0.0).astype(BF16)
        column = nn(packed, spread)
        found = [
            x - column[h * base : (h + 1) * base] * x[k : k + 1] for h, x in enumerate(found)
        ]
    rounded = [low.astype(BF16) for low in lowers]
    step, apart = base, row ^ col
    while True:
        pair = 2 * step
        below = jnp.where((apart >= step) & (apart < pair) & (col < row), 1.0, 0.0).astype(BF16)
        diagonal = jnp.where(apart < step, 1.0, 0.0)
        lane = lax.broadcasted_iota(jnp.int32, (step, size), 1)
        even = (lane & step) == 0
        first = [nn(x.astype(BF16), low * below).astype(BF16) for x, low in zip(found, rounded)]
        whole = [
            (jnp.concatenate([x] * (size // step), axis=0) * diagonal).astype(BF16) for x in found
        ]
        if pair == size:
            ends = [nn(w, right) for w, right in zip(whole, rights)]
            fixes = [nn(f, end.astype(BF16)) for f, end in zip(first, ends)]
            return [
                jnp.concatenate([end[:step], end[step:] - fix], axis=0)
                for end, fix in zip(ends, fixes)
            ]
        second = [nn(f, w) for f, w in zip(first, whole)]
        found = [
            jnp.concatenate([jnp.where(even, x, 0.0), jnp.where(even, -y, x)], axis=0)
            for x, y in zip(found, second)
        ]
        step = pair


def decay_gaps(cum_col, cum_row, row, col):
    return jnp.exp(jnp.where(col <= row, cum_col - cum_row, -1e30))


def inverse_norms(gram, row, col):
    diagonal = jnp.where(row == col, gram, 0.0)
    return (
        lax.rsqrt(jnp.sum(diagonal, axis=1, keepdims=True) + EPSILON),
        lax.rsqrt(jnp.sum(diagonal, axis=0, keepdims=True) + EPSILON),
    )


def place_in_group(group):
    return lax.rem(lax.axis_index("ctx"), group)


def pack_kernel(key_hbm, value_hbm, scalars_ref, *refs):
    group = len(refs) - 2
    out_refs, (rows_ref, in_sems) = refs[:group], refs[group:]
    tokens = key_hbm.shape[0]
    heads = scalars_ref.shape[1]
    place = place_in_group(group)
    base = (1 + REP) * tokens
    arrivals = []
    for s in range(group):
        j = place ^ s
        sources = [key_hbm.at[:, pl.ds(pl.multiple_of(j * DK, DK), DK)]] + [
            value_hbm.at[:, pl.ds(pl.multiple_of((j * REP + r) * DV, DV), DV)] for r in range(REP)
        ]
        arrivals.append(
            [
                pltpu.make_async_copy(
                    source, out_refs[s].at[pl.ds(n * tokens, tokens), :], in_sems.at[s, n]
                )
                for n, source in enumerate(sources)
            ]
        )
    for copy in sum(arrivals, []):
        copy.start()
    row, col = iotas((SMALL_ROWS * group, 4 * heads))
    slot, target = row & (SMALL_ROWS - 1), row >> SMALL_BITS

    def picked(target):
        pick = jnp.zeros(row.shape, F32)
        for kind in range(2):
            for piece in range(2):
                at = slot - piece * PIECE_ROWS - kind * REP
                wanted = (2 * kind + piece) * heads + target * REP + at
                pick = pick + jnp.where((at >= 0) & (at < REP) & (col == wanted), 1.0, 0.0)
        return pick.astype(BF16)

    picks = picked(target ^ place), picked(target)
    pieces = jnp.concatenate(
        two_pieces(scalars_ref[0]) + two_pieces(scalars_ref[1]), axis=0
    )
    sent, natural = [nn(pick, pieces).astype(BF16) for pick in picks]
    if tokens < DK:
        fill = jnp.zeros((sent.shape[0], DK - tokens), BF16)
        sent, natural = [jnp.concatenate([x, fill], axis=1) for x in (sent, natural)]
    rows_ref[...] = natural
    for s, out_ref in enumerate(out_refs):
        out_ref[base : base + SMALL_ROWS, :] = sent[s * SMALL_ROWS : (s + 1) * SMALL_ROWS, :]
        for copy in arrivals[s]:
            copy.wait()


def solved_blocks(blocks, small, tokens, base_bits):
    row, col, lower_ones, upper_ones, eye = triangles(tokens)
    small = small.astype(F32)
    pieces = [
        jnp.concatenate(
            [
                small[b * SMALL_ROWS + start : b * SMALL_ROWS + start + PIECE_ROWS]
                for b in range(len(blocks))
            ],
            axis=0,
        ).astype(BF16)
        for start in (0, PIECE_ROWS)
    ]
    cum_rows = sum(nn(p, upper_ones) for p in pieces)
    plain_cols = sum(nt(eye, p) for p in pieces)
    cum_cols = sum(nt(lower_ones, p) for p in pieces)

    def spread(array, at):
        return jnp.broadcast_to(array[:, at : at + 1], (tokens, DK))

    lowers, rights, works = [], [], []
    for b, (keys, values) in enumerate(blocks):
        gram = nt(keys, keys)
        key_col, key_row = inverse_norms(gram, row, col)
        key_col = jnp.broadcast_to(key_col, (tokens, DK))
        gram = gram * key_row * key_col[:, :tokens]
        unit_keys = keys.astype(F32) * key_col
        for r in range(REP):
            at = b * PIECE_ROWS + r
            strength = spread(plain_cols, at)
            cum_row, cum_col = cum_rows[at + REP : at + REP + 1, :], spread(cum_cols, at + REP)
            factors = decay_gaps(cum_col[:, :tokens], cum_row, row, col)
            lowers.append(jnp.where(col < row, strength[:, :tokens] * factors * gram, 0.0))
            rights.append(
                jnp.concatenate(
                    [
                        (strength * values[r].astype(F32)).astype(BF16),
                        (strength * jnp.exp(cum_col) * unit_keys).astype(BF16),
                    ],
                    axis=1,
                )
            )
            works.append((keys, cum_col, key_col, key_row, factors))
    return solved(lowers, rights, tokens, base_bits), works


def inside_kernel(
    query_ref, key_ref, value_ref, rows_ref, inside_ref, window_ref, *, first, base_bits
):
    tokens = query_ref.shape[0]
    blocks = inside_ref.shape[0] // REP

    def columns(ref, start, size):
        return ref[:, start * size : (start + 1) * size]

    sides, works = solved_blocks(
        [
            (
                columns(key_ref, j, DK),
                [columns(value_ref, j * REP + r, DV) for r in range(REP)],
            )
            for j in range(first, first + blocks)
        ],
        rows_ref[first * SMALL_ROWS : (first + blocks) * SMALL_ROWS, :][:, :tokens],
        tokens,
        base_bits,
    )
    for b in range(blocks):
        queries = columns(query_ref, first + b, DK)
        products = nt(queries, works[b * REP][0])
        queries = queries.astype(F32)
        query_col = lax.rsqrt(
            jnp.sum(queries * queries, axis=1, keepdims=True) + EPSILON
        ) * DK**-0.5
        query_col = jnp.broadcast_to(query_col, (tokens, DK))
        queries = queries * query_col
        products = products * works[b * REP][3] * query_col[:, :tokens]
        for r in range(REP):
            at = b * REP + r
            _, cum_col, _, _, factors = works[at]
            scores = (products * factors).astype(BF16)
            both = nn(scores, sides[at].astype(BF16))
            inside_ref[at] = both[:, :DV].astype(BF16)
            window_ref[at] = (jnp.exp(cum_col) * queries - both[:, DV:]).astype(BF16)


def in_order(own_half, own, other):
    return jnp.where(own_half == 0, own, other), jnp.where(own_half == 0, other, own)


def half_kernel(*refs, blocks, extra, group, tokens, own, with_map):
    count = blocks + extra if own else blocks - extra
    taken, refs = refs[:count], refs[count:]
    if not own:
        (own_end, own_map), refs = refs[:2], refs[2:]
    known = ()
    if extra and not own:
        known, refs = refs[:3], refs[3:]
    before_ref, map_ref, end_ref, end_map_ref, *refs = refs
    if not own:
        group_ref, *refs = refs
        if with_map:
            group_map_ref, *refs = refs
    handed = ()
    if extra and own:
        handed, refs = refs[:3], refs[3:]
    offsets, removals, decays = refs
    place = place_in_group(group)
    low = lax.rem(place, blocks)
    base = (1 + REP) * tokens
    sides, works = solved_blocks(
        [
            (t[0:tokens, :], [t[(1 + r) * tokens : (2 + r) * tokens, :] for r in range(REP)])
            for t in taken
        ],
        jnp.concatenate([t[base : base + SMALL_ROWS, :][:, :tokens] for t in taken], axis=0),
        tokens,
        4,
    )
    if known:
        for held, ref in zip((offsets, removals, decays), known):
            held[0 : extra * REP] = ref[...]
    for b in range(count):
        keys_turned = works[b * REP][0].T
        for r in range(REP):
            at = b * REP + r
            _, cum_col, key_col, _, _ = works[at]
            last = cum_col[tokens - 1 : tokens, :]
            tail = key_col * jnp.exp(last - cum_col)
            tail = jnp.concatenate([tail, tail], axis=1)
            both = nn(keys_turned, (sides[at] * tail).astype(BF16))
            to, held = at if own else at + extra * REP, (offsets, removals, decays)
            if own and b >= blocks:
                to, held = at - blocks * REP, handed
            held[0][to] = both[:, :DV]
            held[1][to] = both[:, DV:].astype(BF16)
            held[2][to] = jnp.broadcast_to(jnp.exp(last), (PIECE_ROWS, DK))

    key_row, key_col = iotas((DK, DK))
    eye = (key_row == key_col).astype(F32)
    states = [None] * REP
    for i in range(blocks):
        following = []
        for r in range(REP):
            at = (low ^ i) * REP + r
            decay = decays[at][0:1, :]
            if i == 0:
                map_ref[at] = eye.astype(BF16)
                before_ref[at] = jnp.zeros((DK, DV), F32)
                following.append(
                    jnp.concatenate(
                        [eye * decay - removals[at].astype(F32), offsets[at]], axis=1
                    )
                )
                continue
            held = states[r].astype(BF16)
            map_ref[at] = held[:, :DK]
            before_ref[at] = states[r][:, DK:]
            moved = nn(removals[at], held)
            following.append(
                jnp.concatenate(
                    [
                        states[r][:, :DK] * decay - moved[:, :DK],
                        states[r][:, DK:] * decay - moved[:, DK:] + offsets[at],
                    ],
                    axis=1,
                )
            )
        states = following
    own_half = place // blocks
    for r in range(REP):
        end_map, end = states[r][:, :DK], states[r][:, DK:]
        end_map_ref[r] = end_map
        end_ref[r] = end
        if not own:
            first_end, second_end = in_order(own_half, own_end[r], end)
            first_map, second_map = in_order(own_half, own_map[r], end_map)
            second_map = second_map.astype(BF16)
            group_ref[r] = (nn(second_map, first_end.astype(BF16)) + second_end).astype(BF16)
            if with_map:
                group_map_ref[r] = nn(second_map, first_map.astype(BF16))


def carry_kernel(
    own_before, own_maps, own_end, own_map, other_before, other_maps, other_end, other_map,
    carried_ref, out_ref,
):
    group = out_ref.shape[0]
    half = group // 2
    place = place_in_group(group)
    own_half = place // half
    later_group = lax.axis_index("ctx") >= group
    starts = []
    for r in range(REP):
        carried = jnp.where(later_group, carried_ref[r].astype(F32), 0.0)
        first_end, _ = in_order(own_half, own_end[r], other_end[r])
        first_map, _ = in_order(own_half, own_map[r], other_map[r])
        middle = first_end + nn(first_map.astype(BF16), carried.astype(BF16))
        starts.append([x.astype(BF16) for x in in_order(own_half, carried, middle)])
    for s in range(group):
        before, maps = (own_before, own_maps) if s < half else (other_before, other_maps)
        for r in range(REP):
            at = (s % half) * REP + r
            start = starts[r][0] if s < half else starts[r][1]
            out_ref[place ^ s, r * DK : (r + 1) * DK, :] = (
                before[at] + nn(maps[at], start)
            ).astype(BF16)


def columns_of(width, target):
    return pl.ds(pl.multiple_of(target * width, width), width)


def mixed_kernel(
    state_ref, first_inside, first_window, second_inside, second_window, gate_ref, gain_ref,
    weight_ref, mixed_ref, *out_refs, shifts,
):
    me = lax.axis_index("head")
    gain, split = gain_ref[...], first_inside.shape[0]
    for j in range(state_ref.shape[0]):
        for r in range(REP):
            h = j * REP + r
            columns = pl.ds(h * DV, DV)
            state = state_ref[j, r * DK : (r + 1) * DK, :]
            inside, window, at = (
                (first_inside, first_window, h) if h < split
                else (second_inside, second_window, h - split)
            )
            rows = inside[at].astype(F32) + nn(window[at], state)
            scale = lax.rsqrt(jnp.mean(rows * rows, axis=1, keepdims=True) + EPSILON)
            gate = gate_ref[:, columns].astype(F32)
            mixed_ref[:, columns] = (
                rows * scale * gain * (0.5 * gate * (1.0 + jnp.tanh(0.5 * gate)))
            ).astype(BF16)
    for n, out_ref in enumerate(out_refs):
        columns = columns_of(out_ref.shape[1], lax.rem(me + 1 + n, shifts))
        out_ref[...] = nn(mixed_ref[...], weight_ref[:, columns]).astype(BF16)


def own_columns_kernel(mixed_ref, weight_ref, out_ref):
    columns = columns_of(out_ref.shape[1], lax.axis_index("head"))
    out_ref[...] = nn(mixed_ref[...], weight_ref[:, columns]).astype(BF16)


def local(
    query_proj, key_proj, value_proj, gate_proj, write_strength, log_decay, norm_gain, out_weight,
    *, n_ctx, n_head,
):
    tokens = query_proj.shape[0]
    heads = value_proj.shape[1] // DV
    group = query_proj.shape[1] // DK
    half = group // 2
    width = out_weight.shape[1] // n_head
    n_groups = n_ctx // group
    packed_rows = (1 + REP) * tokens + SMALL_ROWS
    mib = 1024 * 1024

    def kernel(body, out, name, limit, micros, scratch=(), specs=None, out_specs=None):
        return pl.pallas_call(
            body,
            out_shape=out,
            scratch_shapes=scratch,
            compiler_params=pltpu.CompilerParams(
                vmem_limit_bytes=None if limit is None else int(limit * mib)
            ),
            cost_estimate=pl.CostEstimate(
                flops=int(micros * 1e9), bytes_accessed=mib, transcendentals=0
            ),
            name=name,
            **({} if specs is None else {"in_specs": specs}),
            **({} if out_specs is None else {"out_specs": out_specs}),
        )

    def shape(dims, kind):
        return jax.ShapeDtypeStruct(dims, kind)

    def shifted(array, distance):
        return lax.ppermute(array, "ctx", [(i, i + distance) for i in range(n_ctx - distance)])

    def swapped(array, distance):
        return lax.ppermute(array, "ctx", [(i, i ^ distance) for i in range(n_ctx)])

    any_space = pl.BlockSpec(memory_space=pl.ANY)
    vmem = pl.BlockSpec(memory_space=pltpu.VMEM)
    *packed, rows = kernel(
        pack_kernel,
        (shape((packed_rows, DK), BF16),) * group + (shape((group * SMALL_ROWS, DK), BF16),),
        "pack",
        53,
        2,
        scratch=[pltpu.SemaphoreType.DMA((group, 1 + REP))],
        specs=[any_space, any_space, vmem],
    )(key_proj, value_proj, jnp.stack([write_strength.T, log_decay.T]))
    taken = [packed[0]] + [swapped(packed[s], s) for s in range(1, group)]

    extra = 1 if half >= 4 else 0

    def half_states(blocks, more, name):
        own, with_map = not more, n_groups > 2
        passed = (
            shape((extra * REP, DK, DV), F32),
            shape((extra * REP, DK, DK), BF16),
            shape((extra * REP, PIECE_ROWS, DK), F32),
        )
        return kernel(
            functools.partial(
                half_kernel, blocks=half, extra=extra, group=group, tokens=tokens, own=own,
                with_map=with_map,
            ),
            (
                shape((half * REP, DK, DV), F32),
                shape((half * REP, DK, DK), BF16),
                shape((REP, DK, DV), F32),
                shape((REP, DK, DK), F32),
            )
            + (() if own else (shape((REP, DK, DV), BF16),))
            + ((shape((REP, DK, DK), F32),) if with_map and not own else ())
            + (passed if own and extra else ()),
            name,
            16,
            3.5,
            scratch=[
                pltpu.VMEM((half * REP, DK, DV), F32),
                pltpu.VMEM((half * REP, DK, DK), BF16),
                pltpu.VMEM((half * REP, PIECE_ROWS, DK), F32),
            ],
        )(*blocks, *more)

    own = half_states(taken[: half + extra], (), "own_half")
    def inside_part(start, count, rows, micros, base_bits):
        return kernel(
            functools.partial(inside_kernel, first=start, base_bits=base_bits),
            (
                shape((count * REP, tokens, DV), BF16),
                shape((count * REP, tokens, DK), BF16),
            ),
            "inside",
            16,
            micros,
        )(query_proj, key_proj, value_proj, rows)

    early = max(1, group // 4)
    rows, own = lax.optimization_barrier((rows, own))
    first = inside_part(0, early, rows, 2.3, 4)
    later, own, first = lax.optimization_barrier((taken[half + extra :], own, first))
    *other, end = half_states(later, own[2:], "other_half")
    own = own[:4]

    if n_groups == 2:
        carried = swapped(end, group)
    elif n_groups > 2:
        carried, mapping = shifted(other[-1], group).astype(F32), shifted(end, group)
        other = other[:-1]
        distance = 1
        while distance < n_groups - 1:
            earlier, earlier_map = shifted(carried, distance * group), shifted(mapping, distance * group)
            carried = carried + jnp.einsum("rkl,rlv->rkv", mapping, earlier, precision="highest")
            mapping = jnp.einsum("rkl,rlv->rkv", mapping, earlier_map, precision="highest")
            distance *= 2
        carried = carried.astype(BF16)
    else:
        carried = jnp.zeros((REP, DK, DV), BF16)

    rows, end = lax.optimization_barrier((rows, end))
    second = inside_part(early, group - early, rows, 5, 3)
    carried, second = lax.optimization_barrier((carried, second))
    states = kernel(
        carry_kernel, shape((group, REP * DK, DV), BF16), "carry", 8, 0.6
    )(*own, *other, carried)
    groups = [list(range(g, g + group)) for g in range(0, n_ctx, group)]
    state_in = lax.all_to_all(states, "ctx", 0, 0, axis_index_groups=groups, tiled=True)

    mixed, *others = kernel(
        functools.partial(mixed_kernel, shifts=n_head),
        (shape((tokens, heads * DV), BF16),) + (shape((tokens, width), BF16),) * (n_head - 1),
        "mixed",
        16,
        2,
    )(state_in, *first, *second, gate_proj, norm_gain.reshape(1, DV), out_weight)
    received = [
        lax.ppermute(other, "head", [(i, (i + 1 + s) % n_head) for i in range(n_head)])
        for s, other in enumerate(others)
    ]
    total = kernel(own_columns_kernel, shape((tokens, width), BF16), "own_columns", 16, 1)(
        mixed, out_weight
    ).astype(F32)
    for other in received:
        total = total + other.astype(F32)
    return total.astype(BF16)


def solution(mesh):
    return jax.shard_map(
        functools.partial(local, n_ctx=mesh.shape["ctx"], n_head=mesh.shape["head"]),
        mesh=mesh,
        in_specs=(
            P("ctx", "head"),
            P("ctx", "head"),
            P("ctx", "head"),
            P("ctx", "head"),
            P("ctx", "head"),
            P("ctx", "head"),
            P(),
            P("head", None),
        ),
        out_specs=P("ctx", "head"),
        check_vma=False,
    )
```

```python
import functools

import jax
import jax.numpy as jnp
from jax import lax
from jax.experimental import pallas as pl
from jax.experimental.pallas import tpu as pltpu
from jax.sharding import PartitionSpec as P

HV = 32
HK = 16
DK = 128
DV = 128
REP = HV // HK
SMALL_BITS = 4
SMALL_ROWS = 1 << SMALL_BITS
PIECE_ROWS = 8
EPSILON = 1e-06
BF16 = jnp.bfloat16
F32 = jnp.float32


def nn(a, b):
    return lax.dot_general(a, b, (((1,), (0,)), ((), ())), preferred_element_type=F32)


def nt(a, b):
    return lax.dot_general(a, b, (((1,), (1,)), ((), ())), preferred_element_type=F32)


def two_pieces(x):
    high = x.astype(BF16)
    return high, (x - high.astype(F32)).astype(BF16)


def iotas(shape):
    return lax.broadcasted_iota(jnp.int32, shape, 0), lax.broadcasted_iota(jnp.int32, shape, 1)


def triangles(size):
    row, col = iotas((size, size))
    return row, col, (col <= row).astype(BF16), (row <= col).astype(BF16), (row == col).astype(BF16)


def solved(lowers, rights, size, base_bits):
    count, base = len(lowers), 1 << base_bits
    row, col = iotas((size, size))
    place, lane = iotas((base, size))
    packed = []
    for low in lowers:
        held = low[0:base]
        for b in range(1, size // base):
            held = jnp.where(lane >> base_bits == b, low[b * base : (b + 1) * base], held)
        packed.append(held)
    packed = jnp.concatenate(packed, axis=0).astype(BF16)
    found = [jnp.where(place == (lane & (base - 1)), 1.0, 0.0)] * count
    first_col = col & ~(base - 1)
    for k in range(base - 1):
        spread = jnp.where(row == first_col + k, 1.0, 0.0).astype(BF16)
        column = nn(packed, spread)
        found = [
            x - column[h * base : (h + 1) * base] * x[k : k + 1] for h, x in enumerate(found)
        ]
    rounded = [low.astype(BF16) for low in lowers]
    step, apart = base, row ^ col
    while True:
        pair = 2 * step
        below = jnp.where((apart >= step) & (apart < pair) & (col < row), 1.0, 0.0).astype(BF16)
        diagonal = jnp.where(apart < step, 1.0, 0.0)
        lane = lax.broadcasted_iota(jnp.int32, (step, size), 1)
        even = (lane & step) == 0
        first = [nn(x.astype(BF16), low * below).astype(BF16) for x, low in zip(found, rounded)]
        whole = [
            (jnp.concatenate([x] * (size // step), axis=0) * diagonal).astype(BF16) for x in found
        ]
        if pair == size:
            ends = [nn(w, right) for w, right in zip(whole, rights)]
            fixes = [nn(f, end.astype(BF16)) for f, end in zip(first, ends)]
            return [
                jnp.concatenate([end[:step], end[step:] - fix], axis=0)
                for end, fix in zip(ends, fixes)
            ]
        second = [nn(f, w) for f, w in zip(first, whole)]
        found = [
            jnp.concatenate([jnp.where(even, x, 0.0), jnp.where(even, -y, x)], axis=0)
            for x, y in zip(found, second)
        ]
        step = pair


def decay_gaps(cum_col, cum_row, row, col):
    return jnp.exp(jnp.where(col <= row, cum_col - cum_row, -1e30))


def inverse_norms(gram, row, col):
    diagonal = jnp.where(row == col, gram, 0.0)
    return (
        lax.rsqrt(jnp.sum(diagonal, axis=1, keepdims=True) + EPSILON),
        lax.rsqrt(jnp.sum(diagonal, axis=0, keepdims=True) + EPSILON),
    )


def place_in_group(group):
    return lax.rem(lax.axis_index("ctx"), group)


def partner(group, n):
    half = group // 2
    return n ^ (half - 1) if n >= half else n


def pack_kernel(key_hbm, value_hbm, scalars_ref, *refs):
    group = len(refs) - 2
    out_refs, (rows_ref, in_sems) = refs[:group], refs[group:]
    tokens = key_hbm.shape[0]
    heads = scalars_ref.shape[1]
    place = place_in_group(group)
    base = (1 + REP) * tokens
    arrivals = []
    for s in range(group):
        j = place ^ partner(group, s)
        sources = [key_hbm.at[:, pl.ds(pl.multiple_of(j * DK, DK), DK)]] + [
            value_hbm.at[:, pl.ds(pl.multiple_of((j * REP + r) * DV, DV), DV)] for r in range(REP)
        ]
        arrivals.append(
            [
                pltpu.make_async_copy(
                    source, out_refs[s].at[pl.ds(n * tokens, tokens), :], in_sems.at[s, n]
                )
                for n, source in enumerate(sources)
            ]
        )
    for copy in sum(arrivals, []):
        copy.start()
    row, col = iotas((SMALL_ROWS * group, 4 * heads))
    slot, target = row & (SMALL_ROWS - 1), row >> SMALL_BITS

    def picked(target):
        pick = jnp.zeros(row.shape, F32)
        for kind in range(2):
            for piece in range(2):
                at = slot - piece * PIECE_ROWS - kind * REP
                wanted = (2 * kind + piece) * heads + target * REP + at
                pick = pick + jnp.where((at >= 0) & (at < REP) & (col == wanted), 1.0, 0.0)
        return pick.astype(BF16)

    half = group // 2
    sent_to = jnp.where(target >= half, target ^ (half - 1), target)
    picks = picked(sent_to ^ place), picked(target)
    pieces = jnp.concatenate(
        two_pieces(scalars_ref[0]) + two_pieces(scalars_ref[1]), axis=0
    )
    sent, natural = [nn(pick, pieces).astype(BF16) for pick in picks]
    if tokens < DK:
        fill = jnp.zeros((sent.shape[0], DK - tokens), BF16)
        sent, natural = [jnp.concatenate([x, fill], axis=1) for x in (sent, natural)]
    rows_ref[...] = natural
    for s, out_ref in enumerate(out_refs):
        out_ref[base : base + SMALL_ROWS, :] = sent[s * SMALL_ROWS : (s + 1) * SMALL_ROWS, :]
        for copy in arrivals[s]:
            copy.wait()


def solved_blocks(blocks, small, tokens, base_bits):
    row, col, lower_ones, upper_ones, eye = triangles(tokens)
    small = small.astype(F32)
    pieces = [
        jnp.concatenate(
            [
                small[b * SMALL_ROWS + start : b * SMALL_ROWS + start + PIECE_ROWS]
                for b in range(len(blocks))
            ],
            axis=0,
        ).astype(BF16)
        for start in (0, PIECE_ROWS)
    ]
    cum_rows = sum(nn(p, upper_ones) for p in pieces)
    plain_cols = sum(nt(eye, p) for p in pieces)
    cum_cols = sum(nt(lower_ones, p) for p in pieces)

    def spread(array, at):
        return jnp.broadcast_to(array[:, at : at + 1], (tokens, DK))

    lowers, rights, works = [], [], []
    for b, (keys, values) in enumerate(blocks):
        gram = nt(keys, keys)
        key_col, key_row = inverse_norms(gram, row, col)
        key_col = jnp.broadcast_to(key_col, (tokens, DK))
        gram = gram * key_row * key_col[:, :tokens]
        unit_keys = keys.astype(F32) * key_col
        for r in range(REP):
            at = b * PIECE_ROWS + r
            strength = spread(plain_cols, at)
            cum_row, cum_col = cum_rows[at + REP : at + REP + 1, :], spread(cum_cols, at + REP)
            factors = decay_gaps(cum_col[:, :tokens], cum_row, row, col)
            lowers.append(jnp.where(col < row, strength[:, :tokens] * factors * gram, 0.0))
            rights.append(
                jnp.concatenate(
                    [
                        (strength * values[r].astype(F32)).astype(BF16),
                        (strength * jnp.exp(cum_col) * unit_keys).astype(BF16),
                    ],
                    axis=1,
                )
            )
            works.append((keys, cum_col, key_col, key_row, factors))
    return solved(lowers, rights, tokens, base_bits), works


def inside_kernel(
    query_ref, key_ref, value_ref, rows_ref, inside_ref, window_ref, *, first, base_bits
):
    tokens = query_ref.shape[0]
    blocks = inside_ref.shape[0] // REP

    def columns(ref, start, size):
        return ref[:, start * size : (start + 1) * size]

    sides, works = solved_blocks(
        [
            (
                columns(key_ref, j, DK),
                [columns(value_ref, j * REP + r, DV) for r in range(REP)],
            )
            for j in range(first, first + blocks)
        ],
        rows_ref[first * SMALL_ROWS : (first + blocks) * SMALL_ROWS, :][:, :tokens],
        tokens,
        base_bits,
    )
    for b in range(blocks):
        queries = columns(query_ref, first + b, DK)
        products = nt(queries, works[b * REP][0])
        queries = queries.astype(F32)
        query_col = lax.rsqrt(
            jnp.sum(queries * queries, axis=1, keepdims=True) + EPSILON
        ) * DK**-0.5
        query_col = jnp.broadcast_to(query_col, (tokens, DK))
        queries = queries * query_col
        products = products * works[b * REP][3] * query_col[:, :tokens]
        for r in range(REP):
            at = b * REP + r
            _, cum_col, _, _, factors = works[at]
            scores = (products * factors).astype(BF16)
            both = nn(scores, sides[at].astype(BF16))
            inside_ref[at] = both[:, :DV].astype(BF16)
            window_ref[at] = (jnp.exp(cum_col) * queries - both[:, DV:]).astype(BF16)


def in_order(own_half, own, other):
    return jnp.where(own_half == 0, own, other), jnp.where(own_half == 0, other, own)


def half_kernel(*refs, blocks, extra, group, tokens, own, with_map):
    count = blocks + extra if own else blocks - extra
    taken, refs = refs[:count], refs[count:]
    if not own:
        (own_end, own_map), refs = refs[:2], refs[2:]
    known = ()
    if extra and not own:
        known, refs = refs[:3], refs[3:]
    before_ref, map_ref, end_ref, end_map_ref, *refs = refs
    if not own:
        group_ref, *refs = refs
        if with_map:
            group_map_ref, *refs = refs
    handed = ()
    if extra and own:
        handed, refs = refs[:3], refs[3:]
    offsets, removals, decays = refs
    place = place_in_group(group)
    low = lax.rem(place, blocks)
    base = (1 + REP) * tokens
    sides, works = solved_blocks(
        [
            (t[0:tokens, :], [t[(1 + r) * tokens : (2 + r) * tokens, :] for r in range(REP)])
            for t in taken
        ],
        jnp.concatenate([t[base : base + SMALL_ROWS, :][:, :tokens] for t in taken], axis=0),
        tokens,
        4,
    )
    if known:
        for held, ref in zip((offsets, removals, decays), known):
            held[0 : extra * REP] = ref[...]
    for b in range(count):
        keys_turned = works[b * REP][0].T
        for r in range(REP):
            at = b * REP + r
            _, cum_col, key_col, _, _ = works[at]
            last = cum_col[tokens - 1 : tokens, :]
            tail = key_col * jnp.exp(last - cum_col)
            tail = jnp.concatenate([tail, tail], axis=1)
            both = nn(keys_turned, (sides[at] * tail).astype(BF16))
            to, held = at if own else at + extra * REP, (offsets, removals, decays)
            if own and b >= blocks:
                to, held = at - blocks * REP, handed
            held[0][to] = both[:, :DV]
            held[1][to] = both[:, DV:].astype(BF16)
            held[2][to] = jnp.broadcast_to(jnp.exp(last), (PIECE_ROWS, DK))

    key_row, key_col = iotas((DK, DK))
    eye = (key_row == key_col).astype(F32)
    states = [None] * REP
    for i in range(blocks):
        following = []
        for r in range(REP):
            at = (low ^ i if own else low ^ i ^ (blocks - 1)) * REP + r
            decay = decays[at][0:1, :]
            if i == 0:
                map_ref[at] = eye.astype(BF16)
                before_ref[at] = jnp.zeros((DK, DV), F32)
                following.append(
                    jnp.concatenate(
                        [eye * decay - removals[at].astype(F32), offsets[at]], axis=1
                    )
                )
                continue
            held = states[r].astype(BF16)
            map_ref[at] = held[:, :DK]
            before_ref[at] = states[r][:, DK:]
            moved = nn(removals[at], held)
            following.append(
                jnp.concatenate(
                    [
                        states[r][:, :DK] * decay - moved[:, :DK],
                        states[r][:, DK:] * decay - moved[:, DK:] + offsets[at],
                    ],
                    axis=1,
                )
            )
        states = following
    own_half = place // blocks
    for r in range(REP):
        end_map, end = states[r][:, :DK], states[r][:, DK:]
        end_map_ref[r] = end_map
        end_ref[r] = end
        if not own:
            first_end, second_end = in_order(own_half, own_end[r], end)
            first_map, second_map = in_order(own_half, own_map[r], end_map)
            second_map = second_map.astype(BF16)
            group_ref[r] = (nn(second_map, first_end.astype(BF16)) + second_end).astype(BF16)
            if with_map:
                group_map_ref[r] = nn(second_map, first_map.astype(BF16))


def carry_kernel(
    own_before, own_maps, own_end, own_map, other_before, other_maps, other_end, other_map,
    carried_ref, out_ref,
):
    group = out_ref.shape[0]
    half = group // 2
    place = place_in_group(group)
    own_half = place // half
    later_group = lax.axis_index("ctx") >= group
    starts = []
    for r in range(REP):
        carried = jnp.where(later_group, carried_ref[r].astype(F32), 0.0)
        first_end, _ = in_order(own_half, own_end[r], other_end[r])
        first_map, _ = in_order(own_half, own_map[r], other_map[r])
        middle = first_end + nn(first_map.astype(BF16), carried.astype(BF16))
        starts.append([x.astype(BF16) for x in in_order(own_half, carried, middle)])
    for s in range(group):
        before, maps = (own_before, own_maps) if s < half else (other_before, other_maps)
        for r in range(REP):
            at = (s % half) * REP + r
            start = starts[r][0] if s < half else starts[r][1]
            out_ref[place ^ partner(group, s), r * DK : (r + 1) * DK, :] = (
                before[at] + nn(maps[at], start)
            ).astype(BF16)


def columns_of(width, target):
    return pl.ds(pl.multiple_of(target * width, width), width)


def mixed_kernel(
    state_ref, first_inside, first_window, second_inside, second_window, gate_ref, gain_ref,
    weight_ref, mixed_ref, *out_refs, shifts,
):
    me = lax.axis_index("head")
    gain, split = gain_ref[...], first_inside.shape[0]
    for j in range(state_ref.shape[0]):
        for r in range(REP):
            h = j * REP + r
            columns = pl.ds(h * DV, DV)
            state = state_ref[j, r * DK : (r + 1) * DK, :]
            inside, window, at = (
                (first_inside, first_window, h) if h < split
                else (second_inside, second_window, h - split)
            )
            rows = inside[at].astype(F32) + nn(window[at], state)
            scale = lax.rsqrt(jnp.mean(rows * rows, axis=1, keepdims=True) + EPSILON)
            gate = gate_ref[:, columns].astype(F32)
            mixed_ref[:, columns] = (
                rows * scale * gain * (0.5 * gate * (1.0 + jnp.tanh(0.5 * gate)))
            ).astype(BF16)
    for n, out_ref in enumerate(out_refs):
        columns = columns_of(out_ref.shape[1], lax.rem(me + 1 + n, shifts))
        out_ref[...] = nn(mixed_ref[...], weight_ref[:, columns]).astype(BF16)


def own_columns_kernel(mixed_ref, weight_ref, out_ref):
    columns = columns_of(out_ref.shape[1], lax.axis_index("head"))
    out_ref[...] = nn(mixed_ref[...], weight_ref[:, columns]).astype(BF16)


def local(
    query_proj, key_proj, value_proj, gate_proj, write_strength, log_decay, norm_gain, out_weight,
    *, n_ctx, n_head,
):
    tokens = query_proj.shape[0]
    heads = value_proj.shape[1] // DV
    group = query_proj.shape[1] // DK
    half = group // 2
    width = out_weight.shape[1] // n_head
    n_groups = n_ctx // group
    packed_rows = (1 + REP) * tokens + SMALL_ROWS
    mib = 1024 * 1024

    def kernel(body, out, name, limit, micros, scratch=(), specs=None, out_specs=None):
        return pl.pallas_call(
            body,
            out_shape=out,
            scratch_shapes=scratch,
            compiler_params=pltpu.CompilerParams(
                vmem_limit_bytes=None if limit is None else int(limit * mib)
            ),
            cost_estimate=pl.CostEstimate(
                flops=int(micros * 1e9), bytes_accessed=mib, transcendentals=0
            ),
            name=name,
            **({} if specs is None else {"in_specs": specs}),
            **({} if out_specs is None else {"out_specs": out_specs}),
        )

    def shape(dims, kind):
        return jax.ShapeDtypeStruct(dims, kind)

    def shifted(array, distance):
        return lax.ppermute(array, "ctx", [(i, i + distance) for i in range(n_ctx - distance)])

    def swapped(array, distance):
        return lax.ppermute(array, "ctx", [(i, i ^ distance) for i in range(n_ctx)])

    any_space = pl.BlockSpec(memory_space=pl.ANY)
    vmem = pl.BlockSpec(memory_space=pltpu.VMEM)
    *packed, rows = kernel(
        pack_kernel,
        (shape((packed_rows, DK), BF16),) * group + (shape((group * SMALL_ROWS, DK), BF16),),
        "pack",
        53,
        2,
        scratch=[pltpu.SemaphoreType.DMA((group, 1 + REP))],
        specs=[any_space, any_space, vmem],
    )(key_proj, value_proj, jnp.stack([write_strength.T, log_decay.T]))
    taken = [packed[0]] + [swapped(packed[s], partner(group, s)) for s in range(1, group)]

    extra = 1 if half >= 4 else 0

    def half_states(blocks, more, name):
        own, with_map = not more, n_groups > 2
        passed = (
            shape((extra * REP, DK, DV), F32),
            shape((extra * REP, DK, DK), BF16),
            shape((extra * REP, PIECE_ROWS, DK), F32),
        )
        return kernel(
            functools.partial(
                half_kernel, blocks=half, extra=extra, group=group, tokens=tokens, own=own,
                with_map=with_map,
            ),
            (
                shape((half * REP, DK, DV), F32),
                shape((half * REP, DK, DK), BF16),
                shape((REP, DK, DV), F32),
                shape((REP, DK, DK), F32),
            )
            + (() if own else (shape((REP, DK, DV), BF16),))
            + ((shape((REP, DK, DK), F32),) if with_map and not own else ())
            + (passed if own and extra else ()),
            name,
            16,
            3.5,
            scratch=[
                pltpu.VMEM((half * REP, DK, DV), F32),
                pltpu.VMEM((half * REP, DK, DK), BF16),
                pltpu.VMEM((half * REP, PIECE_ROWS, DK), F32),
            ],
        )(*blocks, *more)

    own = half_states(taken[: half + extra], (), "own_half")
    def inside_part(start, count, rows, micros, base_bits):
        return kernel(
            functools.partial(inside_kernel, first=start, base_bits=base_bits),
            (
                shape((count * REP, tokens, DV), BF16),
                shape((count * REP, tokens, DK), BF16),
            ),
            "inside",
            16,
            micros,
        )(query_proj, key_proj, value_proj, rows)

    early = max(1, group // 4)
    rows, own = lax.optimization_barrier((rows, own))
    first = inside_part(0, early, rows, 2.3, 4)
    later, own, first = lax.optimization_barrier((taken[half + extra :], own, first))
    *other, end = half_states(later, own[2:], "other_half")
    own = own[:4]

    if n_groups == 2:
        carried = swapped(end, group)
    elif n_groups > 2:
        carried, mapping = shifted(other[-1], group).astype(F32), shifted(end, group)
        other = other[:-1]
        distance = 1
        while distance < n_groups - 1:
            earlier, earlier_map = shifted(carried, distance * group), shifted(mapping, distance * group)
            carried = carried + jnp.einsum("rkl,rlv->rkv", mapping, earlier, precision="highest")
            mapping = jnp.einsum("rkl,rlv->rkv", mapping, earlier_map, precision="highest")
            distance *= 2
        carried = carried.astype(BF16)
    else:
        carried = jnp.zeros((REP, DK, DV), BF16)

    rows, end = lax.optimization_barrier((rows, end))
    second = inside_part(early, group - early, rows, 5, 3)
    carried, second = lax.optimization_barrier((carried, second))
    states = kernel(
        carry_kernel, shape((group, REP * DK, DV), BF16), "carry", 8, 0.6
    )(*own, *other, carried)
    groups = [list(range(g, g + group)) for g in range(0, n_ctx, group)]
    state_in = lax.all_to_all(states, "ctx", 0, 0, axis_index_groups=groups, tiled=True)

    mixed, *others = kernel(
        functools.partial(mixed_kernel, shifts=n_head),
        (shape((tokens, heads * DV), BF16),) + (shape((tokens, width), BF16),) * (n_head - 1),
        "mixed",
        16,
        2,
    )(state_in, *first, *second, gate_proj, norm_gain.reshape(1, DV), out_weight)
    received = [
        lax.ppermute(other, "head", [(i, (i + 1 + s) % n_head) for i in range(n_head)])
        for s, other in enumerate(others)
    ]
    total = kernel(own_columns_kernel, shape((tokens, width), BF16), "own_columns", 16, 1)(
        mixed, out_weight
    ).astype(F32)
    for other in received:
        total = total + other.astype(F32)
    return total.astype(BF16)


def solution(mesh):
    return jax.shard_map(
        functools.partial(local, n_ctx=mesh.shape["ctx"], n_head=mesh.shape["head"]),
        mesh=mesh,
        in_specs=(
            P("ctx", "head"),
            P("ctx", "head"),
            P("ctx", "head"),
            P("ctx", "head"),
            P("ctx", "head"),
            P("ctx", "head"),
            P(),
            P("head", None),
        ),
        out_specs=P("ctx", "head"),
        check_vma=False,
    )
```

```python
import functools

import jax
import jax.numpy as jnp
from jax import lax
from jax.experimental import pallas as pl
from jax.experimental.pallas import tpu as pltpu
from jax.sharding import PartitionSpec as P

HV = 32
HK = 16
DK = 128
DV = 128
REP = HV // HK
SMALL_BITS = 4
SMALL_ROWS = 1 << SMALL_BITS
PIECE_ROWS = 8
EPSILON = 1e-06
BF16 = jnp.bfloat16
F32 = jnp.float32


def nn(a, b):
    return lax.dot_general(a, b, (((1,), (0,)), ((), ())), preferred_element_type=F32)


def nt(a, b):
    return lax.dot_general(a, b, (((1,), (1,)), ((), ())), preferred_element_type=F32)


def two_pieces(x):
    high = x.astype(BF16)
    return high, (x - high.astype(F32)).astype(BF16)


def iotas(shape):
    return lax.broadcasted_iota(jnp.int32, shape, 0), lax.broadcasted_iota(jnp.int32, shape, 1)


def triangles(size):
    row, col = iotas((size, size))
    return row, col, (col <= row).astype(BF16), (row <= col).astype(BF16), (row == col).astype(BF16)


def solved(lowers, rights, size, base_bits):
    count, base = len(lowers), 1 << base_bits
    row, col = iotas((size, size))
    place, lane = iotas((base, size))
    packed = []
    for low in lowers:
        held = low[0:base]
        for b in range(1, size // base):
            held = jnp.where(lane >> base_bits == b, low[b * base : (b + 1) * base], held)
        packed.append(held)
    packed = jnp.concatenate(packed, axis=0).astype(BF16)
    found = [jnp.where(place == (lane & (base - 1)), 1.0, 0.0)] * count
    first_col = col & ~(base - 1)
    for k in range(base - 1):
        spread = jnp.where(row == first_col + k, 1.0, 0.0).astype(BF16)
        column = nn(packed, spread)
        found = [
            x - column[h * base : (h + 1) * base] * x[k : k + 1] for h, x in enumerate(found)
        ]
    rounded = [low.astype(BF16) for low in lowers]
    step, apart = base, row ^ col
    while True:
        pair = 2 * step
        below = jnp.where((apart >= step) & (apart < pair) & (col < row), 1.0, 0.0).astype(BF16)
        diagonal = jnp.where(apart < step, 1.0, 0.0)
        lane = lax.broadcasted_iota(jnp.int32, (step, size), 1)
        even = (lane & step) == 0
        first = [nn(x.astype(BF16), low * below).astype(BF16) for x, low in zip(found, rounded)]
        whole = [
            (jnp.concatenate([x] * (size // step), axis=0) * diagonal).astype(BF16) for x in found
        ]
        if pair == size:
            ends = [nn(w, right) for w, right in zip(whole, rights)]
            fixes = [nn(f, end.astype(BF16)) for f, end in zip(first, ends)]
            return [
                jnp.concatenate([end[:step], end[step:] - fix], axis=0)
                for end, fix in zip(ends, fixes)
            ]
        second = [nn(f, w) for f, w in zip(first, whole)]
        found = [
            jnp.concatenate([jnp.where(even, x, 0.0), jnp.where(even, -y, x)], axis=0)
            for x, y in zip(found, second)
        ]
        step = pair


def decay_gaps(cum_col, cum_row, row, col):
    return jnp.exp(jnp.where(col <= row, cum_col - cum_row, -1e30))


def inverse_norms(gram, row, col):
    diagonal = jnp.where(row == col, gram, 0.0)
    return (
        lax.rsqrt(jnp.sum(diagonal, axis=1, keepdims=True) + EPSILON),
        lax.rsqrt(jnp.sum(diagonal, axis=0, keepdims=True) + EPSILON),
    )


def place_in_group(group):
    return lax.rem(lax.axis_index("ctx"), group)


def pack_kernel(key_hbm, value_hbm, scalars_ref, *refs):
    group = len(refs) - 2
    out_refs, (rows_ref, in_sems) = refs[:group], refs[group:]
    tokens = key_hbm.shape[0]
    heads = scalars_ref.shape[1]
    place = place_in_group(group)
    base = (1 + REP) * tokens
    arrivals = []
    for s in range(group):
        j = place ^ s
        sources = [key_hbm.at[:, pl.ds(pl.multiple_of(j * DK, DK), DK)]] + [
            value_hbm.at[:, pl.ds(pl.multiple_of((j * REP + r) * DV, DV), DV)] for r in range(REP)
        ]
        arrivals.append(
            [
                pltpu.make_async_copy(
                    source, out_refs[s].at[pl.ds(n * tokens, tokens), :], in_sems.at[s, n]
                )
                for n, source in enumerate(sources)
            ]
        )
    for copy in sum(arrivals, []):
        copy.start()
    row, col = iotas((SMALL_ROWS * group, 4 * heads))
    slot, target = row & (SMALL_ROWS - 1), row >> SMALL_BITS

    def picked(target):
        pick = jnp.zeros(row.shape, F32)
        for kind in range(2):
            for piece in range(2):
                at = slot - piece * PIECE_ROWS - kind * REP
                wanted = (2 * kind + piece) * heads + target * REP + at
                pick = pick + jnp.where((at >= 0) & (at < REP) & (col == wanted), 1.0, 0.0)
        return pick.astype(BF16)

    picks = picked(target ^ place), picked(target)
    pieces = jnp.concatenate(
        two_pieces(scalars_ref[0]) + two_pieces(scalars_ref[1]), axis=0
    )
    sent, natural = [nn(pick, pieces).astype(BF16) for pick in picks]
    if tokens < DK:
        fill = jnp.zeros((sent.shape[0], DK - tokens), BF16)
        sent, natural = [jnp.concatenate([x, fill], axis=1) for x in (sent, natural)]
    rows_ref[...] = natural
    for s, out_ref in enumerate(out_refs):
        out_ref[base : base + SMALL_ROWS, :] = sent[s * SMALL_ROWS : (s + 1) * SMALL_ROWS, :]
        for copy in arrivals[s]:
            copy.wait()


def solved_blocks(blocks, small, tokens, base_bits):
    row, col, lower_ones, upper_ones, eye = triangles(tokens)
    small = small.astype(F32)
    pieces = [
        jnp.concatenate(
            [
                small[b * SMALL_ROWS + start : b * SMALL_ROWS + start + PIECE_ROWS]
                for b in range(len(blocks))
            ],
            axis=0,
        ).astype(BF16)
        for start in (0, PIECE_ROWS)
    ]
    cum_rows = sum(nn(p, upper_ones) for p in pieces)
    plain_cols = sum(nt(eye, p) for p in pieces)
    cum_cols = sum(nt(lower_ones, p) for p in pieces)

    def spread(array, at):
        return jnp.broadcast_to(array[:, at : at + 1], (tokens, DK))

    lowers, rights, works = [], [], []
    for b, (keys, values) in enumerate(blocks):
        gram = nt(keys, keys)
        key_col, key_row = inverse_norms(gram, row, col)
        key_col = jnp.broadcast_to(key_col, (tokens, DK))
        gram = gram * key_row * key_col[:, :tokens]
        unit_keys = keys.astype(F32) * key_col
        for r in range(REP):
            at = b * PIECE_ROWS + r
            strength = spread(plain_cols, at)
            cum_row, cum_col = cum_rows[at + REP : at + REP + 1, :], spread(cum_cols, at + REP)
            factors = decay_gaps(cum_col[:, :tokens], cum_row, row, col)
            lowers.append(jnp.where(col < row, strength[:, :tokens] * factors * gram, 0.0))
            rights.append(
                jnp.concatenate(
                    [
                        (strength * values[r].astype(F32)).astype(BF16),
                        (strength * jnp.exp(cum_col) * unit_keys).astype(BF16),
                    ],
                    axis=1,
                )
            )
            works.append((keys, cum_col, key_col, key_row, factors))
    return solved(lowers, rights, tokens, base_bits), works


def inside_kernel(
    query_ref, key_ref, value_ref, rows_ref, inside_ref, window_ref, *, first, base_bits
):
    tokens = query_ref.shape[0]
    blocks = inside_ref.shape[0] // REP

    def columns(ref, start, size):
        return ref[:, start * size : (start + 1) * size]

    sides, works = solved_blocks(
        [
            (
                columns(key_ref, j, DK),
                [columns(value_ref, j * REP + r, DV) for r in range(REP)],
            )
            for j in range(first, first + blocks)
        ],
        rows_ref[first * SMALL_ROWS : (first + blocks) * SMALL_ROWS, :][:, :tokens],
        tokens,
        base_bits,
    )
    for b in range(blocks):
        queries = columns(query_ref, first + b, DK)
        products = nt(queries, works[b * REP][0])
        queries = queries.astype(F32)
        query_col = lax.rsqrt(
            jnp.sum(queries * queries, axis=1, keepdims=True) + EPSILON
        ) * DK**-0.5
        query_col = jnp.broadcast_to(query_col, (tokens, DK))
        queries = queries * query_col
        products = products * works[b * REP][3] * query_col[:, :tokens]
        for r in range(REP):
            at = b * REP + r
            _, cum_col, _, _, factors = works[at]
            scores = (products * factors).astype(BF16)
            both = nn(scores, sides[at].astype(BF16))
            inside_ref[at] = both[:, :DV].astype(BF16)
            window_ref[at] = (jnp.exp(cum_col) * queries - both[:, DV:]).astype(BF16)


def in_order(own_half, own, other):
    return jnp.where(own_half == 0, own, other), jnp.where(own_half == 0, other, own)


def half_kernel(*refs, blocks, extra, group, tokens, own, with_map):
    count = blocks + extra if own else blocks - extra
    taken, refs = refs[:count], refs[count:]
    if not own:
        (own_end, own_map), refs = refs[:2], refs[2:]
    known = ()
    if extra and not own:
        known, refs = refs[:3], refs[3:]
    before_ref, map_ref, end_ref, end_map_ref, *refs = refs
    if not own:
        group_ref, *refs = refs
        if with_map:
            group_map_ref, *refs = refs
    handed = ()
    if extra and own:
        handed, refs = refs[:3], refs[3:]
    offsets, removals, decays = refs
    place = place_in_group(group)
    low = lax.rem(place, blocks)
    base = (1 + REP) * tokens
    sides, works = solved_blocks(
        [
            (t[0:tokens, :], [t[(1 + r) * tokens : (2 + r) * tokens, :] for r in range(REP)])
            for t in taken
        ],
        jnp.concatenate([t[base : base + SMALL_ROWS, :][:, :tokens] for t in taken], axis=0),
        tokens,
        4,
    )
    if known:
        for held, ref in zip((offsets, removals, decays), known):
            held[0 : extra * REP] = ref[...]
    for b in range(count):
        keys_turned = works[b * REP][0].T
        for r in range(REP):
            at = b * REP + r
            _, cum_col, key_col, _, _ = works[at]
            last = cum_col[tokens - 1 : tokens, :]
            tail = key_col * jnp.exp(last - cum_col)
            tail = jnp.concatenate([tail, tail], axis=1)
            both = nn(keys_turned, (sides[at] * tail).astype(BF16))
            to, held = at if own else at + extra * REP, (offsets, removals, decays)
            if own and b >= blocks:
                to, held = at - blocks * REP, handed
            held[0][to] = both[:, :DV]
            held[1][to] = both[:, DV:].astype(BF16)
            held[2][to] = jnp.broadcast_to(jnp.exp(last), (PIECE_ROWS, DK))

    key_row, key_col = iotas((DK, DK))
    eye = (key_row == key_col).astype(F32)
    states = [None] * REP
    for i in range(blocks):
        following = []
        for r in range(REP):
            at = (low ^ i) * REP + r
            decay = decays[at][0:1, :]
            if i == 0:
                map_ref[at] = eye.astype(BF16)
                before_ref[at] = jnp.zeros((DK, DV), F32)
                following.append(
                    jnp.concatenate(
                        [eye * decay - removals[at].astype(F32), offsets[at]], axis=1
                    )
                )
                continue
            held = states[r].astype(BF16)
            map_ref[at] = held[:, :DK]
            before_ref[at] = states[r][:, DK:]
            moved = nn(removals[at], held)
            following.append(
                jnp.concatenate(
                    [
                        states[r][:, :DK] * decay - moved[:, :DK],
                        states[r][:, DK:] * decay - moved[:, DK:] + offsets[at],
                    ],
                    axis=1,
                )
            )
        states = following
    own_half = place // blocks
    for r in range(REP):
        end_map, end = states[r][:, :DK], states[r][:, DK:]
        end_map_ref[r] = end_map
        end_ref[r] = end
        if not own:
            first_end, second_end = in_order(own_half, own_end[r], end)
            first_map, second_map = in_order(own_half, own_map[r], end_map)
            second_map = second_map.astype(BF16)
            group_ref[r] = (nn(second_map, first_end.astype(BF16)) + second_end).astype(BF16)
            if with_map:
                group_map_ref[r] = nn(second_map, first_map.astype(BF16))


def carry_kernel(
    own_before, own_maps, own_end, own_map, other_before, other_maps, other_end, other_map,
    carried_ref, out_ref,
):
    group = out_ref.shape[0]
    half = group // 2
    place = place_in_group(group)
    own_half = place // half
    later_group = lax.axis_index("ctx") >= group
    starts = []
    for r in range(REP):
        carried = jnp.where(later_group, carried_ref[r].astype(F32), 0.0)
        first_end, _ = in_order(own_half, own_end[r], other_end[r])
        first_map, _ = in_order(own_half, own_map[r], other_map[r])
        middle = first_end + nn(first_map.astype(BF16), carried.astype(BF16))
        starts.append([x.astype(BF16) for x in in_order(own_half, carried, middle)])
    for s in range(group):
        before, maps = (own_before, own_maps) if s < half else (other_before, other_maps)
        for r in range(REP):
            at = (s % half) * REP + r
            start = starts[r][0] if s < half else starts[r][1]
            out_ref[place ^ s, r * DK : (r + 1) * DK, :] = (
                before[at] + nn(maps[at], start)
            ).astype(BF16)


def columns_of(width, target):
    return pl.ds(pl.multiple_of(target * width, width), width)


def mixed_kernel(
    state_ref, first_inside, first_window, second_inside, second_window, gate_ref, gain_ref,
    weight_ref, mixed_ref, *out_refs, shifts,
):
    me = lax.axis_index("head")
    gain, split = gain_ref[...], first_inside.shape[0]
    for j in range(state_ref.shape[0]):
        for r in range(REP):
            h = j * REP + r
            columns = pl.ds(h * DV, DV)
            state = state_ref[j, r * DK : (r + 1) * DK, :]
            inside, window, at = (
                (first_inside, first_window, h) if h < split
                else (second_inside, second_window, h - split)
            )
            rows = inside[at].astype(F32) + nn(window[at], state)
            scale = lax.rsqrt(jnp.mean(rows * rows, axis=1, keepdims=True) + EPSILON)
            gate = gate_ref[:, columns].astype(F32)
            mixed_ref[:, columns] = (
                rows * scale * gain * (0.5 * gate * (1.0 + jnp.tanh(0.5 * gate)))
            ).astype(BF16)
    for n, out_ref in enumerate(out_refs):
        columns = columns_of(out_ref.shape[1], lax.rem(me + 1 + n, shifts))
        out_ref[...] = nn(mixed_ref[...], weight_ref[:, columns]).astype(BF16)


def own_columns_kernel(mixed_ref, weight_ref, out_ref):
    columns = columns_of(out_ref.shape[1], lax.axis_index("head"))
    out_ref[...] = nn(mixed_ref[...], weight_ref[:, columns]).astype(BF16)


def local(
    query_proj, key_proj, value_proj, gate_proj, write_strength, log_decay, norm_gain, out_weight,
    *, n_ctx, n_head,
):
    tokens = query_proj.shape[0]
    heads = value_proj.shape[1] // DV
    group = query_proj.shape[1] // DK
    half = group // 2
    width = out_weight.shape[1] // n_head
    n_groups = n_ctx // group
    packed_rows = (1 + REP) * tokens + SMALL_ROWS
    mib = 1024 * 1024

    def kernel(body, out, name, limit, micros, scratch=(), specs=None, out_specs=None):
        return pl.pallas_call(
            body,
            out_shape=out,
            scratch_shapes=scratch,
            compiler_params=pltpu.CompilerParams(
                vmem_limit_bytes=None if limit is None else int(limit * mib)
            ),
            cost_estimate=pl.CostEstimate(
                flops=int(micros * 1e9), bytes_accessed=mib, transcendentals=0
            ),
            name=name,
            **({} if specs is None else {"in_specs": specs}),
            **({} if out_specs is None else {"out_specs": out_specs}),
        )

    def shape(dims, kind):
        return jax.ShapeDtypeStruct(dims, kind)

    def shifted(array, distance):
        return lax.ppermute(array, "ctx", [(i, i + distance) for i in range(n_ctx - distance)])

    def swapped(array, distance):
        return lax.ppermute(array, "ctx", [(i, i ^ distance) for i in range(n_ctx)])

    any_space = pl.BlockSpec(memory_space=pl.ANY)
    vmem = pl.BlockSpec(memory_space=pltpu.VMEM)
    *packed, rows = kernel(
        pack_kernel,
        (shape((packed_rows, DK), BF16),) * group + (shape((group * SMALL_ROWS, DK), BF16),),
        "pack",
        53,
        2,
        scratch=[pltpu.SemaphoreType.DMA((group, 1 + REP))],
        specs=[any_space, any_space, vmem],
    )(key_proj, value_proj, jnp.stack([write_strength.T, log_decay.T]))
    taken = [packed[0]] + [swapped(packed[s], s) for s in range(1, group)]

    extra = 1 if half >= 4 else 0

    def half_states(blocks, more, name):
        own, with_map = not more, n_groups > 2
        passed = (
            shape((extra * REP, DK, DV), F32),
            shape((extra * REP, DK, DK), BF16),
            shape((extra * REP, PIECE_ROWS, DK), F32),
        )
        return kernel(
            functools.partial(
                half_kernel, blocks=half, extra=extra, group=group, tokens=tokens, own=own,
                with_map=with_map,
            ),
            (
                shape((half * REP, DK, DV), F32),
                shape((half * REP, DK, DK), BF16),
                shape((REP, DK, DV), F32),
                shape((REP, DK, DK), F32),
            )
            + (() if own else (shape((REP, DK, DV), BF16),))
            + ((shape((REP, DK, DK), F32),) if with_map and not own else ())
            + (passed if own and extra else ()),
            name,
            16,
            3.5,
            scratch=[
                pltpu.VMEM((half * REP, DK, DV), F32),
                pltpu.VMEM((half * REP, DK, DK), BF16),
                pltpu.VMEM((half * REP, PIECE_ROWS, DK), F32),
            ],
        )(*blocks, *more)

    own = half_states(taken[: half + extra], (), "own_half")
    def inside_part(start, count, rows, micros, base_bits):
        return kernel(
            functools.partial(inside_kernel, first=start, base_bits=base_bits),
            (
                shape((count * REP, tokens, DV), BF16),
                shape((count * REP, tokens, DK), BF16),
            ),
            "inside",
            16,
            micros,
        )(query_proj, key_proj, value_proj, rows)

    early = max(1, group // 4)
    rows, own = lax.optimization_barrier((rows, own))
    first = inside_part(0, early, rows, 2.3, 4)
    later, own, first = lax.optimization_barrier((taken[half + extra :], own, first))
    *other, end = half_states(later, own[2:], "other_half")
    own = own[:4]

    if n_groups == 2:
        carried = swapped(end, group)
    elif n_groups > 2:
        carried, mapping = shifted(other[-1], group).astype(F32), shifted(end, group)
        other = other[:-1]
        distance = 1
        while distance < n_groups - 1:
            earlier, earlier_map = shifted(carried, distance * group), shifted(mapping, distance * group)
            carried = carried + jnp.einsum("rkl,rlv->rkv", mapping, earlier, precision="highest")
            mapping = jnp.einsum("rkl,rlv->rkv", mapping, earlier_map, precision="highest")
            distance *= 2
        carried = carried.astype(BF16)
    else:
        carried = jnp.zeros((REP, DK, DV), BF16)

    rows, end = lax.optimization_barrier((rows, end))
    second = inside_part(early, group - early, rows, 5, 4)
    carried, second = lax.optimization_barrier((carried, second))
    states = kernel(
        carry_kernel, shape((group, REP * DK, DV), BF16), "carry", 8, 0.6
    )(*own, *other, carried)
    groups = [list(range(g, g + group)) for g in range(0, n_ctx, group)]
    state_in = lax.all_to_all(states, "ctx", 0, 0, axis_index_groups=groups, tiled=True)

    mixed, *others = kernel(
        functools.partial(mixed_kernel, shifts=n_head),
        (shape((tokens, heads * DV), BF16),) + (shape((tokens, width), BF16),) * (n_head - 1),
        "mixed",
        16,
        2,
    )(state_in, *first, *second, gate_proj, norm_gain.reshape(1, DV), out_weight)
    received = [
        lax.ppermute(other, "head", [(i, (i + 1 + s) % n_head) for i in range(n_head)])
        for s, other in enumerate(others)
    ]
    total = kernel(own_columns_kernel, shape((tokens, width), BF16), "own_columns", 16, 1)(
        mixed, out_weight
    ).astype(F32)
    for other in received:
        total = total + other.astype(F32)
    return total.astype(BF16)


def solution(mesh):
    return jax.shard_map(
        functools.partial(local, n_ctx=mesh.shape["ctx"], n_head=mesh.shape["head"]),
        mesh=mesh,
        in_specs=(
            P("ctx", "head"),
            P("ctx", "head"),
            P("ctx", "head"),
            P("ctx", "head"),
            P("ctx", "head"),
            P("ctx", "head"),
            P(),
            P("head", None),
        ),
        out_specs=P("ctx", "head"),
        check_vma=False,
    )
```
